32 devices in a mesh: rep: 4 (over x, core), seq: 8 (over z, y).
Axes of the slice: x: 2, y: 2, z: 4, core: 2. Of those that a mesh axis runs over, the one named last changes fastest.
Arguments:
- tokens: bfloat16 [8192, 1024], P(('rep', 'seq')), may hold values from -6 to 6
- norm_first: bfloat16 [1024], P('seq'), may hold values from 0.25 to 1.75
- joint_weight: bfloat16 [1024, 3072], P('seq'), may hold values from -0.1875 to 0.1875
- output_weight: bfloat16 [1024, 1024], P('seq'), may hold values from -2.5 to 2.5
- norm_second: bfloat16 [1024], P('seq'), may hold values from 0.25 to 1.75
- expand_weight: bfloat16 [1024, 5248], P('seq'), may hold values from -0.1875 to 0.1875
- shrink_weight: bfloat16 [2624, 1024], P('seq'), may hold values from -0.125 to 0.125
- document_start: int32 [8192], P(('rep', 'seq')), may hold values from 0 to 7692, as said below
- cotangent: bfloat16 [8192, 1024], P(('rep', 'seq')), may hold values from -6 to 6
Outputs:
- block_output: bfloat16 [8192, 1024], P(('rep', 'seq'))
- tokens_gradient: bfloat16 [8192, 1024], P(('rep', 'seq'))
- first_gradient: float32 [1024], P('seq')
- joint_gradient: float32 [1024, 3072], P('seq')
- output_gradient: float32 [1024, 1024], P('seq')
- second_gradient: float32 [1024], P('seq')
- expand_gradient: float32 [1024, 5248], P('seq')
- shrink_gradient: float32 [2624, 1024], P('seq')
The draws below stay inside these ranges and needn't reach their ends.
Inputs may be any that keep to these rules, and one draw needn't show every extreme that they name: `document_start`: tokens of one document are contiguous and share the value, the index of the document's first token; a document has 100 to 500 tokens (the one just before a stream's last may be cut shorter) and lies inside one aligned stream of 2048 tokens; the last document of every stream has exactly 500 tokens.
All inputs are finite; a program needn't handle non-finite values.
Results may differ from the reference program's by a relative error of at most 0.017.
Values may be sent and summed in bfloat16 or wider, within the bound.
No kernel may reach another device: no remote copies, remote signals or barrier semaphores. Data moves between devices by JAX's collectives and lax.ppermute only.
A program may use at most 192 MiB of HBM per device.

```python
import jax
import jax.numpy as jnp
from jax import lax

D = 1024
HEADS = 16
HEAD_DIM = 64
FF = 2624
HALO = 512
DOC_MIN = 100
DOC_MAX = 500
SEQ_LEN = 2048
TOKENS = 8192


def draw_document_start(key, part):
    key = jax.random.fold_in(key, 11)
    seq_count = TOKENS // SEQ_LEN
    most_docs = SEQ_LEN // DOC_MIN + 1
    last_start = SEQ_LEN - DOC_MAX
    lengths = jax.random.randint(key, (seq_count, most_docs), DOC_MIN, DOC_MAX + 1).astype(jnp.int32)
    ends = jnp.cumsum(lengths, axis=1).astype(jnp.int32)
    place = jnp.arange(SEQ_LEN, dtype=jnp.int32)
    which = jnp.sum((ends[:, None, :] <= place[None, :, None]).astype(jnp.int32), axis=2).astype(jnp.int32)
    starts = jnp.concatenate([jnp.zeros((seq_count, 1), jnp.int32), ends[:, :-1]], axis=1)
    drawn = jnp.take_along_axis(starts, which, axis=1)
    local = jnp.where(place[None, :] >= last_start, last_start, drawn).astype(jnp.int32)
    offsets = (jnp.arange(seq_count, dtype=jnp.int32) * SEQ_LEN)[:, None]
    return (local + offsets).reshape(-1).astype(jnp.int32)


def level_of(rng, extent, pieces, least, high):
    level = 1.0
    for axis_at, parts in pieces:
        steps = jax.random.uniform(jax.random.fold_in(jax.random.fold_in(rng, 6), axis_at), (parts,), jnp.float32, least / len(pieces), high / len(pieces))
        level = level * jnp.repeat(jnp.exp(steps), extent[axis_at] // parts).reshape((-1,) + (1,) * (len(extent) - 1 - axis_at))
    return level


def gaussian(rng, dims, width, bound, cuts=(), held_as=jnp.bfloat16):
    values = width * jax.random.normal(rng, dims, jnp.float32)
    if cuts:
        values = values * level_of(rng, dims, cuts, -0.22, 0.18)
    return jnp.clip(values, -bound, bound).astype(held_as)


def setup_inputs(seed: int = 0) -> dict:
    arg_keys = jax.random.split(jax.random.key(seed), 10)
    return {
        "tokens": gaussian(arg_keys[0], (TOKENS, D), 1.0, 6.0, ((0, 32),)),
        "norm_first": jnp.clip(1.0 + 0.15 * jax.random.normal(arg_keys[1], (D,), jnp.float32), 0.25, 1.75).astype(jnp.bfloat16),
        "joint_weight": gaussian(arg_keys[2], (D, 3 * D), D ** -0.5, 0.1875, ((0, 8),)),
        "output_weight": gaussian(arg_keys[3], (D, D), (max(1, 3 * D // DOC_MAX)) ** -0.5, 2.5, ((0, 8),)),
        "norm_second": jnp.clip(1.0 + 0.15 * jax.random.normal(arg_keys[4], (D,), jnp.float32), 0.25, 1.75).astype(jnp.bfloat16),
        "expand_weight": gaussian(arg_keys[5], (D, 2 * FF), D ** -0.5, 0.1875, ((0, 8),)),
        "shrink_weight": gaussian(arg_keys[6], (FF, D), FF ** -0.5, 0.125, ((0, 8),)),
        "document_start": draw_document_start(jax.random.fold_in(arg_keys[9], 71), 0),
        "cotangent": gaussian(arg_keys[8], (TOKENS, D), 1.0, 6.0, ((0, 32),)),
    }


EPSILON = 1e-05
THETA = 160000.0
SCALE = 0.125
HIGHEST = lax.Precision.HIGHEST

@jax.custom_vjp
def low(v):
    return lax.optimization_barrier(v.astype(jnp.bfloat16)).astype(jnp.float32)

@jax.custom_vjp
def low_back(v):
    return v

def low_keep(v):
    return (low(v), None)

def low_pass(kept, grad):
    return (grad,)

def back_keep(v):
    return (v, None)

def back_low(kept, grad):
    return (low(grad),)
low.defvjp(low_keep, low_pass)
low_back.defvjp(back_keep, back_low)

def normalize(rows, gain):
    middle = lax.optimization_barrier(jnp.mean(rows, axis=-1, keepdims=True))
    centered = rows - middle
    spread = lax.optimization_barrier(jnp.mean(centered * centered, axis=-1, keepdims=True))
    return centered * lax.rsqrt(spread + EPSILON) * gain

def rotate(values, cosine, sine):
    halves = values.shape[-1] // 2
    first = values[..., :halves]
    second = values[..., halves:]
    return jnp.concatenate([first * cosine - second * sine, second * cosine + first * sine], axis=-1)

def reference(tokens, norm_first, joint_weight, output_weight, norm_second, expand_weight, shrink_weight, document_start, cotangent):
    count = tokens.shape[0]
    place = jnp.arange(count, dtype=jnp.int32)
    position = (place - document_start).astype(jnp.float32)
    halves = HEAD_DIM // 2
    frequency = THETA ** (-(jnp.arange(halves, dtype=jnp.float32) * 2.0) / HEAD_DIM)
    angle = position[:, None] * frequency[None, :]
    cosine = jnp.cos(angle)[:, None, :]
    sine = jnp.sin(angle)[:, None, :]
    edge_doc = jnp.full((HALO,), -1, jnp.int32)
    wide_doc = jnp.concatenate([edge_doc, document_start.astype(jnp.int32), edge_doc])
    starts = jnp.arange(count // 512, dtype=jnp.int32) * 512

    def attend(queries, keys, values):
        padding = jnp.zeros((HALO, HEADS, HEAD_DIM), jnp.float32)
        keys_wide = jnp.concatenate([padding, keys, padding], axis=0)
        values_wide = jnp.concatenate([padding, values, padding], axis=0)

        def one_block(start):
            block_query = lax.dynamic_slice_in_dim(queries, start, 512, 0)
            block_doc = lax.dynamic_slice_in_dim(document_start.astype(jnp.int32), start, 512, 0)
            near_keys = lax.dynamic_slice_in_dim(keys_wide, start, 512 + 2 * HALO, 0)
            near_values = lax.dynamic_slice_in_dim(values_wide, start, 512 + 2 * HALO, 0)
            near_doc = lax.dynamic_slice_in_dim(wide_doc, start, 512 + 2 * HALO, 0)
            raw = jnp.einsum('qhd,khd->hqk', block_query, near_keys, precision=HIGHEST) * SCALE
            allowed = block_doc[:, None] == near_doc[None, :]
            logits = low_back(jnp.where(allowed[None], raw, -jnp.inf))
            weights = low(jax.nn.softmax(logits, axis=-1))
            return jnp.einsum('hqk,khd->qhd', weights, near_values, precision=HIGHEST)
        blocks = lax.map(jax.checkpoint(one_block), starts)
        return blocks.reshape(count, HEADS * HEAD_DIM)

    def forward(stream, gain_one, joint, output, gain_two, expand, shrink):
        first = low(normalize(stream, gain_one))
        mixed = low_back(jnp.dot(first, joint, precision=HIGHEST))
        queries = mixed[:, :D].reshape(count, HEADS, HEAD_DIM)
        keys = mixed[:, D:2 * D].reshape(count, HEADS, HEAD_DIM)
        values = mixed[:, 2 * D:].reshape(count, HEADS, HEAD_DIM)
        queries = low(rotate(queries, cosine, sine))
        keys = low(rotate(keys, cosine, sine))
        values = low(values)
        attended = low(low_back(attend(queries, keys, values)))
        middle = stream + low_back(jnp.dot(attended, output, precision=HIGHEST))
        second = low(normalize(middle, gain_two))
        lifted = low_back(jnp.dot(second, expand, precision=HIGHEST))
        active = low(jax.nn.gelu(lifted[:, :FF], approximate=False) * lifted[:, FF:])
        return middle + low_back(jnp.dot(active, shrink, precision=HIGHEST))
    primals = tuple((item.astype(jnp.float32) for item in (tokens, norm_first, joint_weight, output_weight, norm_second, expand_weight, shrink_weight)))
    result, pull = jax.vjp(forward, *primals)
    grads = pull(cotangent.astype(jnp.float32))
    return (result.astype(jnp.bfloat16), grads[0].astype(jnp.bfloat16), grads[1], grads[2], grads[3], grads[4], grads[5], grads[6])
```

```python
import functools

import jax
import jax.numpy as jnp
from jax import lax
from jax.experimental import pallas as pl
from jax.experimental.pallas import tpu as pltpu
from jax.sharding import PartitionSpec as P

HEADS = 16
HEAD_DIM = 64
FF = 2624
HALO = 512
EPSILON = 1e-05
THETA = 160000.0
SCALE = 0.125
LANES = 128
GROUP = 256
FAR = -1e6
BF = jnp.bfloat16
F32 = jnp.float32


def dot(left, right):
    return jnp.dot(left, right, preferred_element_type=F32)


def inner_rows(left, right):
    return lax.dot_general(left, right, (((0,), (0,)), ((), ())), preferred_element_type=F32)


def outer_rows(left, right):
    return lax.dot_general(left, right, (((1,), (1,)), ((), ())), preferred_element_type=F32)


def pick(flag, one, two):
    return [jnp.where(flag, a, b) for a, b in zip(one, two)]


def centre(rows):
    middle = jnp.mean(rows, axis=-1, keepdims=True)
    centered = rows - middle
    spread = jnp.mean(centered * centered, axis=-1, keepdims=True)
    scale = lax.rsqrt(spread + EPSILON)
    return centered * scale, scale


def centre_back(normal, scale, grads):
    return scale * (
        grads
        - jnp.mean(grads, axis=-1, keepdims=True)
        - normal * jnp.mean(grads * normal, axis=-1, keepdims=True)
    )


def two_parts(values):
    high = lax.reduce_precision(values, 8, 7)
    return high.astype(BF), (values - high).astype(BF)


def swap_core(array):
    return lax.ppermute(array, "rep", [(i, i ^ 1) for i in range(lax.axis_size("rep"))])


def swap_far(array):
    return lax.ppermute(array, "rep", [(i, i ^ 2) for i in range(lax.axis_size("rep"))])


class Direct:
    depth = 4

    def __init__(self):
        self.place = lax.axis_index("seq")
        self.z = self.place // 2
        self.y = self.place % 2
        self.x = lax.axis_index("rep") // 2
        self.core = lax.axis_index("rep") % 2
        self.front = self.core == 0

    def halves(self, four):
        rows, once, other, last = four
        return (
            (rows, jnp.where(self.front, other, once)),
            (jnp.where(self.front, once, other), last),
        )

    def along(self, array, steps):
        n = self.depth
        route = [(s, 2 * ((s // 2 + steps) % n) + s % 2) for s in range(2 * n)]
        return lax.ppermute(array, "seq", route)

    def cross(self, array, turn):
        n = 2 * self.depth
        route = []
        for r in range(4):
            for s in range(n):
                to = (r ^ 2, s) if r % 2 == turn else (r, s ^ 1)
                route.append((r * n + s, to[0] * n + to[1]))
        return lax.ppermute(array, ("rep", "seq"), route)

    def collect(self, piece):
        return jnp.concatenate([piece] + [self.along(piece, k) for k in (1, 2, 3)], axis=0)

    def share(self, rows):
        once = self.cross(rows, 0)
        other = self.cross(rows, 1)
        last = self.cross(once, 1)
        return rows, once, other, last

    def to_near(self, grid):
        n = self.depth
        turned = [pick(self.y == 0, grid[z], grid[z][::-1]) for z in range(n)]
        near = []
        for y in (0, 1):
            line = [turned[-k % n][y] for k in range(n)]
            line = pick(self.z % 2 == 1, line[-1:] + line[:-1], line)
            near.append(pick(self.z // 2 == 1, line[-2:] + line[:-2], line))
        return near

    def to_mesh(self, near):
        n = self.depth
        lines = []
        for line in near:
            line = pick(self.z // 2 == 1, line[2:] + line[:2], line)
            line = pick(self.z % 2 == 1, line[1:] + line[:1], line)
            lines.append([line[-z % n] for z in range(n)])
        return [pick(self.y == 0, [lines[0][z], lines[1][z]], [lines[1][z], lines[0][z]]) for z in range(n)]

    def rows_of(self, size):
        n = self.depth
        return [
            (2 * ((self.z - k) % n) + (self.y + y) % 2) * size for y in (0, 1) for k in range(n)
        ]

    def order(self, array, size):
        n = self.depth
        cut = lambda s: array[..., s * size : (s + 1) * size]
        near = self.to_near([[cut(2 * z), cut(2 * z + 1)] for z in range(n)])
        return jnp.concatenate(near[0] + near[1], axis=-1)

    def restore(self, array, size):
        n = self.depth
        cut = lambda j: array[..., j * size : (j + 1) * size]
        grid = self.to_mesh([[cut(n * y + k) for k in range(n)] for y in (0, 1)])
        return jnp.concatenate([part for pair in grid for part in pair], axis=-1)

    def down(self, blocks):
        total = blocks[0].astype(F32)
        for k in (1, 2, 3):
            total = total + self.along(blocks[k], -k).astype(F32)
        return total.astype(BF)

    def reduce(self, left, near, far):
        half = left.shape[1] // 2
        rows = half // self.depth
        top, bottom = left[:, :half], left[:, half:]
        last = inner_rows(bottom, far).astype(BF)
        other = inner_rows(
            jnp.where(self.front, bottom, top), jnp.where(self.front, near, far)
        ).astype(BF)
        last_in = self.cross(last, 1)
        other_in = self.cross(other, 1)
        once = inner_rows(jnp.where(self.front, top, bottom), jnp.where(self.front, far, near))
        once_in = self.cross((once + last_in).astype(BF), 0)
        mine = (inner_rows(top, near) + other_in + once_in).astype(BF)
        return self.down([mine[k * rows : (k + 1) * rows] for k in range(self.depth)])

    def reduce_rows(self, left, near, far):
        rows = left.shape[1] // (2 * self.depth)
        blocks = []
        for part in (near, far):
            whole = inner_rows(left, part).astype(BF)
            cut = lambda s: whole[s * rows : (s + 1) * rows]
            lines = self.to_near([[cut(2 * z), cut(2 * z + 1)] for z in range(self.depth)])
            blocks.append([jnp.concatenate(line, axis=0) for line in lines])
        last_in = self.cross(blocks[1][1], 1)
        other_in = self.cross(jnp.where(self.front, blocks[0][1], blocks[1][0]), 1)
        once = jnp.where(self.front, blocks[1][0], blocks[0][1])
        once_in = self.cross((once.astype(F32) + last_in).astype(BF), 0)
        mine = (blocks[0][0].astype(F32) + other_in + once_in).astype(BF)
        return self.down([mine[k * rows : (k + 1) * rows] for k in range(self.depth)])


class Plain:
    def __init__(self):
        self.x = lax.axis_index("rep") // 2
        self.core = lax.axis_index("rep") % 2
        self.front = jnp.bool_(True)

    def collect(self, piece):
        return lax.all_gather(piece, "seq", axis=0, tiled=True)

    def share(self, near):
        far = swap_far(near)
        half = near.shape[0] // 2
        return near[:half], far[:half], near[half:], far[half:]

    def halves(self, four):
        return (four[0], four[2]), (four[1], four[3])

    def rows_of(self, size):
        return [jnp.int32(0), jnp.int32(lax.axis_size("seq") // 2 * size)]

    def order(self, array, size):
        return array

    def restore(self, array, size):
        return array

    def reduce(self, left, near, far):
        mine = inner_rows(left, near) + swap_far(inner_rows(left, far).astype(BF))
        return lax.psum_scatter(mine, "seq", scatter_dimension=0, tiled=True).astype(BF)

    reduce_rows = reduce


def times_back(near_grads, far_grads, near, far):
    return jnp.concatenate(
        [
            outer_rows(near_grads, near[0]) + outer_rows(far_grads, far[0]),
            outer_rows(near_grads, near[1]) + outer_rows(far_grads, far[1]),
        ],
        axis=-1,
    )


def lane_masks():
    lane = lax.broadcasted_iota(jnp.int32, (1, GROUP), 1)
    turned = [(lane % LANES) // (HEAD_DIM // 2) == i for i in range(4)]
    plain = [lane // HEAD_DIM == i for i in range(4)]
    return turned, plain


def only(mask, array):
    return jnp.where(mask, array, jnp.zeros_like(array))


def mix_kernel(rows, near_top, near_bottom, far_top, far_bottom, cosine, sine, near, far):
    half = near_top.shape[0]
    c, s = cosine[...], sine[...]
    for top, bottom, out in ((near_top, near_bottom, near), (far_top, far_bottom, far)):
        raw = dot(rows[:, :half], top[...]) + dot(rows[:, half:], bottom[...])
        for kind, scale in ((0, SCALE), (1, 1.0)):
            at = kind * GROUP
            a, b = raw[:, at : at + LANES], raw[:, at + LANES : at + GROUP]
            out[:, at : at + LANES] = ((a * c - b * s) * scale).astype(BF)
            out[:, at + LANES : at + GROUP] = ((b * c + a * s) * scale).astype(BF)
        out[:, 2 * GROUP :] = raw[:, 2 * GROUP :].astype(BF)


def attend_kernel(q0, k0, v0, q1, k1, v1, doc_row, doc_column, attended, logs):
    turned, plain = lane_masks()
    allowed = doc_column[...] == doc_row[...]
    lane = lax.broadcasted_iota(jnp.int32, (1, LANES), 1)
    totals = jnp.zeros((q0.shape[0], LANES), F32)
    for group, (q, k, v) in enumerate(((q0, k0, v0), (q1, k1, v1))):
        queries, keys, values = q[...], k[...], v[...]
        kept = jnp.zeros(queries.shape, F32)
        for i in range(4):
            raw = outer_rows(only(turned[i], queries), keys)
            raw = jnp.where(allowed, raw, -jnp.inf)
            top = jnp.max(raw, axis=-1, keepdims=True)
            weights = jnp.exp(raw - top)
            total = jnp.sum(weights, axis=-1, keepdims=True)
            found = dot(weights.astype(BF), values) / total
            kept = jnp.where(plain[i], found, kept)
            totals = jnp.where(lane == 4 * group + i, top + jnp.log(total), totals)
        attended[:, group * GROUP : (group + 1) * GROUP] = kept
    logs[...] = totals


def query_kernel(q0, k0, v0, q1, k1, v1, d_out, doc_row, doc_column, logs, delta, d_q):
    turned, plain = lane_masks()
    allowed = doc_column[...] == doc_row[...]
    for group, (q, k, v) in enumerate(((q0, k0, v0), (q1, k1, v1))):
        queries, keys, values = q[...], k[...], v[...]
        grads = d_out[:, group * GROUP : (group + 1) * GROUP]
        kept = jnp.zeros(queries.shape, F32)
        for i in range(4):
            at = 4 * group + i
            raw = outer_rows(only(turned[i], queries), keys)
            weights = jnp.where(allowed, jnp.exp(raw - logs[:, at : at + 1]), 0.0)
            d_weights = outer_rows(only(plain[i], grads), values)
            d_raw = (weights * (d_weights - delta[:, at : at + 1])).astype(BF)
            kept = jnp.where(turned[i], dot(d_raw, keys), kept)
        d_q[:, group * GROUP : (group + 1) * GROUP] = kept * SCALE


def key_kernel(q0, k0, v0, q1, k1, v1, d_out, doc_row, doc_column, logs, delta, d_k, d_v):
    turned, plain = lane_masks()
    allowed = doc_column[...] == doc_row[...]
    for group, (q, k, v) in enumerate(((q0, k0, v0), (q1, k1, v1))):
        queries, keys, values = q[...], k[...], v[...]
        grads = d_out[:, group * GROUP : (group + 1) * GROUP]
        kept_k = jnp.zeros(keys.shape, F32)
        kept_v = jnp.zeros(keys.shape, F32)
        for i in range(4):
            at = 4 * group + i
            raw = outer_rows(only(turned[i], keys), queries)
            weights = jnp.where(allowed, jnp.exp(raw - logs[at : at + 1, :]), 0.0)
            kept_v = jnp.where(plain[i], dot(weights.astype(BF), grads), kept_v)
            d_weights = outer_rows(only(plain[i], values), grads)
            d_raw = (weights * (d_weights - delta[at : at + 1, :])).astype(BF)
            kept_k = jnp.where(turned[i], dot(d_raw, queries), kept_k)
        d_k[:, group * GROUP : (group + 1) * GROUP] = kept_k
        d_v[:, group * GROUP : (group + 1) * GROUP] = kept_v


def call_kernel(kernel, ins, outs, flops, grid=(1,)):
    moving = lambda i: (i, 0)
    specs = [
        pl.BlockSpec(block, moving if at is None else functools.partial(lambda at, i: at, at))
        for _, block, at in ins
    ]
    return pl.pallas_call(
        kernel,
        grid=grid,
        in_specs=specs,
        out_specs=tuple(pl.BlockSpec((s[0] // grid[0], s[1]), moving) for s, _ in outs),
        out_shape=tuple(jax.ShapeDtypeStruct(s, t) for s, t in outs),
        compiler_params=pltpu.CompilerParams(vmem_limit_bytes=40 * 2**20),
        cost_estimate=pl.CostEstimate(
            flops=flops, bytes_accessed=8 * 2**20, transcendentals=3 * 2**20
        ),
    )(*[a for a, _, _ in ins])


def gelu_parts(inner):
    share = 0.5 * (1.0 + lax.erf(inner * 0.7071067811865476))
    return inner * share, share + inner * (0.3989422804014327 * jnp.exp(-0.5 * inner * inner))


def hidden_kernel(marks, rows, grads, *refs):
    expand, shrink = refs[0:4], refs[4:8]
    active, near_grads, far_grads, out, d_rows = refs[8:13]
    near_w, far_w, shrink_w, semaphore = refs[13:]
    units = near_w.shape[1]
    half = near_w.shape[0] // 2
    wide = shrink[0].shape[1]
    places = marks.shape[0] - 2
    block = units // places
    front = marks[0] == 1
    near_x = marks[1] == 0

    def settled():
        found = [(expand[0], near_w.at[:half]), (expand[3], far_w.at[half:])]
        for j in range(places // 2):
            part = pl.ds(j * block, block)
            low = pl.multiple_of(marks[2 + places // 2 + j], 16)
            high = pl.multiple_of(marks[2 + j], 16)
            found.append((shrink[0].at[part], shrink_w.at[pl.ds(high, block), pl.ds(0, wide)]))
            found.append((shrink[3].at[part], shrink_w.at[pl.ds(low, block), pl.ds(wide, wide)]))
        return found

    def crossed(one, two):
        found = [(expand[two], near_w.at[half:]), (expand[one], far_w.at[:half])]
        for j in range(places // 2):
            part = pl.ds(j * block, block)
            low = pl.multiple_of(marks[2 + places // 2 + j], 16)
            high = pl.multiple_of(marks[2 + j], 16)
            found.append((shrink[two].at[part], shrink_w.at[pl.ds(low, block), pl.ds(0, wide)]))
            found.append(
                (shrink[one].at[part], shrink_w.at[pl.ds(high, block), pl.ds(wide, wide)])
            )
        return found

    @pl.when(pl.program_id(0) == 0)
    def _():
        always = [
            pltpu.make_async_copy(s, t, semaphore.at[k]) for k, (s, t) in enumerate(settled())
        ]
        for copy in always:
            copy.start()
        shift = len(always)
        for flag, one, two in ((front, 1, 2), (jnp.logical_not(front), 2, 1)):

            @pl.when(flag)
            def _():
                moved = [
                    pltpu.make_async_copy(s, t, semaphore.at[shift + k])
                    for k, (s, t) in enumerate(crossed(one, two))
                ]
                for copy in moved:
                    copy.start()
                for copy in moved:
                    copy.wait()

        for copy in always:
            copy.wait()

    x, dy = rows[...], grads[...]
    tile = 256
    for at in range(0, units, tile):
        cut = slice(at, min(at + tile, units))
        first = dot(x, near_w[:, cut])
        second = dot(x, far_w[:, cut])
        d_active = outer_rows(dy, shrink_w[cut, :])
        inner = jnp.where(near_x, first, second)
        gate = jnp.where(near_x, second, first)
        value, slope = gelu_parts(inner)
        active[:, cut] = (value * gate).astype(BF)
        d_inner = d_active * gate * slope
        d_gate = d_active * value
        near_grads[:, cut] = jnp.where(near_x, d_inner, d_gate).astype(BF)
        far_grads[:, cut] = jnp.where(near_x, d_gate, d_inner).astype(BF)
    out[...] = dot(active[...], shrink_w[...])
    d_rows[...] = outer_rows(near_grads[...], near_w[...]) + outer_rows(far_grads[...], far_w[...])


def hidden(marks, rows, grads, expand, shrink):
    count, width = rows.shape
    units = expand[0].shape[1]
    size = count // 2
    moving = lambda i: (i, 0)
    held = pl.BlockSpec(memory_space=pl.ANY)
    outs = [(units, BF), (units, BF), (units, BF), (width, F32), (width, F32)]
    return pl.pallas_call(
        hidden_kernel,
        grid=(2,),
        in_specs=[pl.BlockSpec(memory_space=pltpu.SMEM)]
        + [pl.BlockSpec((size, width), moving)] * 2
        + [held] * 8,
        out_specs=tuple(pl.BlockSpec((size, w), moving) for w, _ in outs),
        out_shape=tuple(jax.ShapeDtypeStruct((count, w), t) for w, t in outs),
        scratch_shapes=[
            pltpu.VMEM((width, units), BF),
            pltpu.VMEM((width, units), BF),
            pltpu.VMEM((units, width), BF),
            pltpu.SemaphoreType.DMA((2 * marks.shape[0],)),
        ],
        compiler_params=pltpu.CompilerParams(vmem_limit_bytes=48 * 2**20),
        cost_estimate=pl.CostEstimate(
            flops=12 * count * width * units,
            bytes_accessed=20 * 2**20,
            transcendentals=2 * count * units,
        ),
    )(marks, rows, grads, *expand, *shrink)


def after(array, *earlier):
    return lax.optimization_barrier((array,) + earlier)[0]


def on_device(
    direct,
    tokens,
    norm_first,
    joint_weight,
    output_weight,
    norm_second,
    expand_weight,
    shrink_weight,
    document_start,
    cotangent,
):
    plan = Direct() if direct else Plain()
    rows, width = tokens.shape
    length = lax.axis_size("seq")
    reach = min(HALO // rows, length - 1)
    block_count = 2 * reach + 1
    span = block_count * rows
    here = lax.axis_index("seq")
    x, core = plan.x, plan.core
    near_x = x == 0
    heads_wide = width // 2
    depth = joint_weight.shape[0]
    unit_rows = shrink_weight.shape[0]
    unit_half = (unit_rows + 1) // 2
    units = -(-unit_half * length // LANES) * LANES
    while units % length:
        units += LANES
    unit_pad = units // length
    half_width = width // 2

    def mine(array, start):
        parts = [array[:, start + i * GROUP : start + (i + 1) * GROUP] for i in range(4)]
        low, high = pick(near_x, parts[0::2], parts[1::2])
        return jnp.where(core == 0, low, high)

    source = jnp.arange(GROUP)
    turn = (
        source[:, None]
        == ((source % LANES) // 32 * HEAD_DIM + source // LANES * 32 + source % 32)[None, :]
    ).astype(BF)
    gain_one = norm_first.astype(F32)[:, None]
    gain_two = norm_second.astype(F32)[:, None]
    joint_piece = jnp.concatenate(
        [
            (dot(mine(joint_weight, 0), turn) * gain_one).astype(BF),
            (dot(mine(joint_weight, width), turn) * gain_one).astype(BF),
            (mine(joint_weight, 2 * width).astype(F32) * gain_one).astype(BF),
            mine(output_weight, 0),
        ],
        axis=1,
    )
    slot = jnp.arange(units)
    inner = core * unit_half + slot % unit_pad
    fits = (slot % unit_pad < unit_half) & (inner < unit_rows)
    unit_of = jnp.where(fits, slot // unit_pad * unit_rows + inner, -2 * FF)
    spread_units = (jnp.arange(2 * FF)[:, None] == (unit_of + x * FF)[None, :]).astype(BF)
    expand_piece = (dot(expand_weight, spread_units) * gain_two).astype(BF)
    slot_row = jnp.arange(unit_pad)

    def picked(c):
        row = c * unit_half + slot_row
        row = jnp.where((slot_row < unit_half) & (row < unit_rows), row, -1)
        return (row[:, None] == jnp.arange(unit_rows)[None, :]).astype(BF)

    shrink_piece = dot(
        picked(core),
        jnp.where(near_x, shrink_weight[:, :half_width], shrink_weight[:, half_width:]),
    ).astype(BF)

    joint_rows = plan.collect(joint_piece)
    anchor = (lax.axis_index("rep") * length + here) * rows
    position = anchor + jnp.arange(rows, dtype=jnp.int32) - document_start
    marks = jnp.pad(
        jnp.stack([(position + 1) // 16, (position + 1) % 16], axis=1), ((0, 0), (0, LANES - 2))
    ).astype(BF)
    packed = jnp.concatenate([tokens, marks], axis=1)
    offsets = [0]
    blocks = [packed]
    for offset in list(range(-reach, 0)) + list(range(1, reach + 1)):
        route = [(i + offset, i) for i in range(length) if 0 <= i + offset < length]
        offsets.append(offset)
        blocks.append(lax.ppermute(packed, "seq", route))
    sent = []
    for block in blocks:
        normal = centre(block[:, :width].astype(F32))[0].astype(BF)
        sent.append(jnp.concatenate([plan.order(normal, depth), block[:, width:]], axis=1))
    sent = jnp.concatenate(sent, axis=0)
    first = (sent, swap_core(sent))
    offset_rows = jnp.repeat(jnp.array(offsets, jnp.int32), rows) * rows
    index = (here * rows + offset_rows + jnp.tile(jnp.arange(rows), block_count)).astype(F32)
    halves = HEAD_DIM // 2
    frequency = THETA ** (-(jnp.arange(halves, dtype=F32) * 2.0) / HEAD_DIM)
    frequency = jnp.tile(frequency, LANES // halves)
    document_rows, document_columns, cosines, sines = [], [], [], []
    for rows_in in first:
        code = rows_in[:, width : width + 2].astype(F32)
        code = code[:, :1] * 16.0 + code[:, 1:]
        document = jnp.where(code > 0, index[:, None] - (code - 1.0), FAR)
        document_rows.append(document.reshape(1, span))
        document_columns.append(document[:rows])
        angle = (code - 1.0) * frequency[None, :]
        cosines.append(jnp.cos(angle))
        sines.append(jnp.sin(angle))
    cotangents = jnp.concatenate([cotangent, swap_core(cotangent)], axis=0)

    expand_rows = plan.collect(after(expand_piece, joint_rows))
    shrink_rows = plan.collect(after(shrink_piece, expand_rows))
    joint_near, joint_far = plan.halves(plan.share(joint_rows))
    expand_four = plan.share(expand_rows)
    shrink_four = plan.share(shrink_rows)
    output_mine = jnp.concatenate(
        [
            jnp.concatenate([part[:, 3 * GROUP :] for part in pair], axis=0)
            for pair in (joint_near, joint_far)
        ],
        axis=1,
    )
    output_all = jnp.concatenate([output_mine, swap_core(output_mine)], axis=1)

    def turn_columns(array):
        parts = [array[:, i * GROUP : (i + 1) * GROUP] for i in range(4)]
        parts = pick(core == 0, parts, parts[2:] + parts[:2])
        left, right = pick(near_x, parts[:2], parts[1::-1]), pick(near_x, parts[2:], parts[:1:-1])
        return jnp.concatenate(left + right, axis=-1)

    def turn_halves(array):
        left, right = array[:, :half_width], array[:, half_width:]
        return jnp.concatenate(
            [jnp.where(near_x, left, right), jnp.where(near_x, right, left)], axis=-1
        )

    mixed = []
    wide = 3 * GROUP
    half_depth = joint_near[0].shape[0]
    for t in (0, 1):
        mixed.append(
            call_kernel(
                mix_kernel,
                [(first[t], (rows, width), None)]
                + [(part, (half_depth, wide), (0, 0)) for part in joint_near + joint_far]
                + [(cosines[t], (rows, LANES), None), (sines[t], (rows, LANES), None)],
                [((span, wide), BF), ((span, wide), BF)],
                2 * span * width * 2 * wide,
                (block_count,),
            )
        )
    score_flops = 2 * rows * span * GROUP * 8
    own, every = (rows, GROUP), (span, GROUP)

    def operands(t, sizes):
        found = [
            (array, size, (0, column))
            for array in mixed[t]
            for column, size in enumerate(sizes)
        ]
        return found, [
            (document_rows[t], (1, span), (0, 0)),
            (document_columns[t], (rows, 1), (0, 0)),
        ]

    attended, logs = [], []
    for t in (0, 1):
        wide_keys, documents = operands(t, (own, every, every))
        found, found_logs = call_kernel(
            attend_kernel,
            wide_keys + documents,
            [((rows, 2 * GROUP), F32), ((rows, LANES), F32)],
            2 * score_flops,
        )
        attended.append(found)
        logs.append(found_logs)
    attended_low = jnp.concatenate(attended, axis=0).astype(BF)
    attended_there = swap_core(jnp.concatenate(attended[::-1], axis=0).astype(BF))
    attended_rows = plan.order(
        turn_columns(jnp.concatenate([attended_low, attended_there], axis=1)), depth
    )
    middle = tokens.astype(F32) + turn_columns(dot(attended_rows[:rows], output_all))
    second, second_scale = centre(middle)
    second_low = plan.order(second.astype(BF), depth)
    second_both = jnp.concatenate([second_low, swap_core(second_low)], axis=0)

    cotangents_turned = turn_halves(cotangents)
    where = jnp.stack(
        [plan.front.astype(jnp.int32), x.astype(jnp.int32)]
        + [row.astype(jnp.int32) for row in plan.rows_of(unit_pad)]
    )
    active_low, lifted_near_grad, lifted_far_grad, part, second_part = hidden(
        where, second_both, cotangents_turned, expand_four, shrink_four
    )
    part = turn_halves(part)
    result = middle + part[:rows] + swap_core(part[rows:].astype(BF)).astype(F32)
    second_grad = second_part[:rows] + swap_core(second_part[rows:].astype(BF)).astype(F32)
    middle_grad = cotangent.astype(F32) + centre_back(
        second, second_scale, plan.restore(second_grad, depth)
    )
    branch = middle_grad.astype(BF)
    branch_both = turn_columns(jnp.concatenate([branch, swap_core(branch)], axis=0))
    attended_grad = turn_columns(plan.restore(outer_rows(branch_both, output_all), depth))
    attended_grad = attended_grad[:, : 2 * GROUP].astype(BF)
    arounds, deltas = [], []
    for t in (0, 1):
        grads = attended_grad[t * rows : (t + 1) * rows]
        delta = jnp.sum(
            (grads.astype(F32) * attended[t]).reshape(rows, HEADS // 2, HEAD_DIM), axis=-1
        )
        deltas.append(delta)
        log_high, log_low = two_parts(logs[t][:, : HEADS // 2])
        delta_high, delta_low = two_parts(delta)
        around = jnp.concatenate([grads, log_high, log_low, delta_high, delta_low], axis=1)
        arounds.append(jnp.pad(around, ((0, 0), (0, -around.shape[1] % LANES))))
    around = jnp.stack(arounds)
    blocks = [around]
    for offset in offsets[1:]:
        route = [(i + offset, i) for i in range(length) if 0 <= i + offset < length]
        blocks.append(lax.ppermute(around, "seq", route))

    mixed_grads = [[], []]
    for t in (0, 1):
        wide_keys, documents = operands(t, (own, every, every))
        (query_grad,) = call_kernel(
            query_kernel,
            wide_keys
            + [(arounds[t], (rows, 2 * GROUP), (0, 0))]
            + documents
            + [(logs[t], (rows, LANES), (0, 0)), (deltas[t], (rows, HEADS // 2), (0, 0))],
            [((rows, 2 * GROUP), F32)],
            3 * score_flops,
        )
        there = jnp.concatenate([block[t] for block in blocks], axis=0)
        numbers = there[:, 2 * GROUP : 2 * GROUP + 32].astype(F32).T
        wide_keys, documents = operands(t, (every, own, own))
        key_grad, value_grad = call_kernel(
            key_kernel,
            wide_keys
            + [(there, (span, 2 * GROUP), (0, 0))]
            + documents
            + [
                (numbers[:8] + numbers[8:16], (HEADS // 2, span), (0, 0)),
                (numbers[16:24] + numbers[24:], (HEADS // 2, span), (0, 0)),
            ],
            [((rows, 2 * GROUP), F32), ((rows, 2 * GROUP), F32)],
            4 * score_flops,
        )
        c, s = cosines[t][:rows], sines[t][:rows]
        for i in (0, 1):
            parts = []
            for grads in (query_grad, key_grad):
                a = grads[:, i * GROUP : i * GROUP + LANES]
                b = grads[:, i * GROUP + LANES : (i + 1) * GROUP]
                parts += [a * c + b * s, b * c - a * s]
            parts.append(value_grad[:, i * GROUP : (i + 1) * GROUP])
            mixed_grads[i].append(jnp.concatenate(parts, axis=1).astype(BF))
    mixed_grads = [jnp.concatenate(pair, axis=0) for pair in mixed_grads]
    first_part = times_back(
        mixed_grads[0],
        mixed_grads[1],
        [part[:, :wide] for part in joint_near],
        [part[:, :wide] for part in joint_far],
    )
    first_grad = first_part[:rows] + swap_core(first_part[rows:].astype(BF)).astype(F32)
    normal, normal_scale = centre(tokens.astype(F32))
    tokens_grad = middle_grad + centre_back(
        normal, normal_scale, plan.restore(first_grad, depth)
    )

    shrink_share = plan.reduce_rows(
        active_low, cotangents_turned[:, :half_width], cotangents_turned[:, half_width:]
    )
    expand_share = plan.reduce(second_both, lifted_near_grad, lifted_far_grad)
    output_share = plan.reduce(
        attended_rows, branch_both[:, :GROUP], branch_both[:, GROUP : 2 * GROUP]
    )
    joint_share = plan.reduce(
        jnp.concatenate([rows_in[:rows, :width] for rows_in in first], axis=0),
        mixed_grads[0],
        mixed_grads[1],
    )

    def spread(share):
        pair = [share, swap_far(share)]
        low, high = pick(near_x, pair, pair[::-1])
        both = jnp.concatenate([low, high], axis=1)
        there = swap_core(both)
        size = share.shape[1]
        cores = pick(core == 0, [both, there], [there, both])
        return [[part[:, :size], part[:, size:]] for part in cores]

    shrink_shares = spread(shrink_share)
    shrink_grad = jnp.concatenate(
        [
            inner_rows(picked(0), shrink_shares[0][i]) + inner_rows(picked(1), shrink_shares[1][i])
            for i in (0, 1)
        ],
        axis=1,
    )
    expand_shares = spread(expand_share)
    expand_halves = []
    for i in (0, 1):
        total = 0.0
        for c in (0, 1):
            inner = c * unit_half + slot % unit_pad
            fits = (slot % unit_pad < unit_half) & (inner < unit_rows)
            unit_at = jnp.where(fits, slot // unit_pad * unit_rows + inner, -1)
            back = (unit_at[:, None] == jnp.arange(FF)[None, :]).astype(BF)
            total = total + dot(expand_shares[c][i], back)
        expand_halves.append(total)
    expand_raw = jnp.concatenate(expand_halves, axis=1)
    expand_grad = expand_raw * gain_two
    second_gain_grad = jnp.sum(expand_raw * expand_weight.astype(F32), axis=1)
    output_shares = spread(output_share)
    output_grad = jnp.concatenate(output_shares[0] + output_shares[1], axis=1).astype(F32)
    joint_four = spread(joint_share)
    columns = []
    for kind in range(3):
        for c in (0, 1):
            for i in (0, 1):
                piece = joint_four[c][i][:, kind * GROUP : (kind + 1) * GROUP]
                columns.append(
                    lax.dot_general(
                        piece, turn, (((1,), (1,)), ((), ())), preferred_element_type=F32
                    )
                    if kind < 2
                    else piece.astype(F32)
                )
    joint_raw = jnp.concatenate(columns, axis=1)
    joint_grad = joint_raw * gain_one
    first_gain_grad = jnp.sum(joint_raw * joint_weight.astype(F32), axis=1)
    return (
        result.astype(BF),
        tokens_grad.astype(BF),
        first_gain_grad,
        joint_grad,
        output_grad,
        second_gain_grad,
        expand_grad,
        shrink_grad,
    )


def solution(mesh):
    placed = (
        P(("rep", "seq"), None),
        P("seq"),
        P("seq", None),
        P("seq", None),
        P("seq"),
        P("seq", None),
        P("seq", None),
        P(("rep", "seq")),
        P(("rep", "seq"), None),
    )
    return jax.shard_map(
        functools.partial(on_device, mesh.shape["seq"] == 8),
        mesh=mesh,
        in_specs=placed,
        out_specs=(
            P(("rep", "seq"), None),
            P(("rep", "seq"), None),
            P("seq"),
            P("seq", None),
            P("seq", None),
            P("seq"),
            P("seq", None),
            P("seq", None),
        ),
        check_vma=False,
    )
```

```python
import functools

import jax
import jax.numpy as jnp
from jax import lax
from jax.experimental import pallas as pl
from jax.experimental.pallas import tpu as pltpu
from jax.sharding import PartitionSpec as P

HEADS = 16
HEAD_DIM = 64
FF = 2624
HALO = 512
EPSILON = 1e-05
THETA = 160000.0
SCALE = 0.125
LANES = 128
GROUP = 256
FAR = -1e6
BF = jnp.bfloat16
F32 = jnp.float32


def dot(left, right):
    return jnp.dot(left, right, preferred_element_type=F32)


def inner_rows(left, right):
    return lax.dot_general(left, right, (((0,), (0,)), ((), ())), preferred_element_type=F32)


def outer_rows(left, right):
    return lax.dot_general(left, right, (((1,), (1,)), ((), ())), preferred_element_type=F32)


def pick(flag, one, two):
    return [jnp.where(flag, a, b) for a, b in zip(one, two)]


def centre(rows):
    middle = jnp.mean(rows, axis=-1, keepdims=True)
    centered = rows - middle
    spread = jnp.mean(centered * centered, axis=-1, keepdims=True)
    scale = lax.rsqrt(spread + EPSILON)
    return centered * scale, scale


def centre_back(normal, scale, grads):
    return scale * (
        grads
        - jnp.mean(grads, axis=-1, keepdims=True)
        - normal * jnp.mean(grads * normal, axis=-1, keepdims=True)
    )


def two_parts(values):
    high = lax.reduce_precision(values, 8, 7)
    return high.astype(BF), (values - high).astype(BF)


def swap_core(array):
    return lax.ppermute(array, "rep", [(i, i ^ 1) for i in range(lax.axis_size("rep"))])


def swap_far(array):
    return lax.ppermute(array, "rep", [(i, i ^ 2) for i in range(lax.axis_size("rep"))])


def after(array, *earlier):
    return lax.optimization_barrier((array,) + earlier)[0]


class Direct:
    depth = 4

    def __init__(self):
        self.place = lax.axis_index("seq")
        self.z = self.place // 2
        self.y = self.place % 2
        self.x = lax.axis_index("rep") // 2
        self.core = lax.axis_index("rep") % 2
        self.front = self.core == 0

    def along(self, array, flip):
        route = [(s, s ^ (2 * flip)) for s in range(2 * self.depth)]
        return lax.ppermute(array, "seq", route)

    def cross(self, array, turn):
        n = 2 * self.depth
        route = []
        for r in range(4):
            for s in range(n):
                to = (r ^ 2, s) if r % 2 == turn else (r, s ^ 1)
                route.append((r * n + s, to[0] * n + to[1]))
        return lax.ppermute(array, ("rep", "seq"), route)

    def around(self, array):
        rows = array.shape[0]
        last = 2 * self.depth
        low = lax.ppermute(array, "seq", [(s, s + 2) for s in range(last - 2)])
        high = lax.ppermute(array, "seq", [(s, s - 2) for s in range(2, last)])
        sent = jnp.concatenate([array, jnp.where(self.y == 0, high, low)], axis=0)
        beside = lax.ppermute(sent, "seq", [(s, s ^ 1) for s in range(last)])
        step = 1 - 2 * self.y
        return [array, low, high, beside[:rows], beside[rows:]], [0, -2, 2, step, -step]

    def collect(self, piece, at_once):
        if at_once:
            return jnp.concatenate([piece] + [self.along(piece, k) for k in (1, 2, 3)], axis=0)
        pair = jnp.concatenate([piece, self.along(piece, 1)], axis=0)
        return jnp.concatenate([pair, self.along(pair, 2)], axis=0)

    def share(self, rows):
        pair = jnp.concatenate([rows, self.cross(rows, 0)], axis=0)
        return pair, self.cross(pair, 1)

    def to_near(self, grid):
        turned = [pick(self.y == 0, pair, pair[::-1]) for pair in grid]
        near = []
        for y in (0, 1):
            a, b, c, d = [pair[y] for pair in turned]
            a, b, c, d = pick(self.z % 2 == 0, [a, b, c, d], [b, a, d, c])
            near.append(pick(self.z // 2 == 0, [a, b, c, d], [c, d, a, b]))
        return near

    def to_mesh(self, near):
        lines = []
        for a, b, c, d in near:
            a, b, c, d = pick(self.z % 2 == 0, [a, b, c, d], [b, a, d, c])
            lines.append(pick(self.z // 2 == 0, [a, b, c, d], [c, d, a, b]))
        return [pick(self.y == 0, list(pair), list(pair)[::-1]) for pair in zip(*lines)]

    def rows_of(self, size):
        return [
            (2 * (self.z ^ k) + (self.y ^ y)) * size for y in (0, 1) for k in range(self.depth)
        ]

    def columns(self, count):
        z, y = jnp.arange(count) // 2, jnp.arange(count) % 2
        return (4 * (y ^ self.y) + (z ^ self.z)).astype(jnp.int32)

    def order(self, array, size):
        n = self.depth
        cut = lambda s: array[..., s * size : (s + 1) * size]
        near = self.to_near([[cut(2 * z), cut(2 * z + 1)] for z in range(n)])
        return jnp.concatenate(near[0] + near[1], axis=-1)

    def restore(self, array, size):
        n = self.depth
        cut = lambda j: array[..., j * size : (j + 1) * size]
        grid = self.to_mesh([[cut(n * y + k) for k in range(n)] for y in (0, 1)])
        return jnp.concatenate([part for pair in grid for part in pair], axis=-1)

    def down(self, mine, at_once):
        rows = mine.shape[0] // 4
        cut = lambda k, n: mine[k * rows : (k + n) * rows]
        if at_once:
            total = cut(0, 1).astype(F32)
            for k in (1, 2, 3):
                total = total + self.along(cut(k, 1), k).astype(F32)
            return total.astype(BF)
        pair = (cut(0, 2).astype(F32) + self.along(cut(2, 2), 2).astype(F32)).astype(BF)
        return (pair[:rows].astype(F32) + self.along(pair[rows:], 1).astype(F32)).astype(BF)

    def reduce(self, left, near, far, at_once=False):
        half = left.shape[1] // 2
        top, bottom = left[:, :half], left[:, half:]
        sent = lax.dot_general(
            jnp.stack([jnp.where(self.front, bottom, top), bottom]),
            jnp.stack([jnp.where(self.front, near, far), far]),
            (((1,), (1,)), ((0,), (0,))),
            preferred_element_type=F32,
        ).astype(BF)
        back = self.cross(sent, 1)
        once = inner_rows(jnp.where(self.front, top, bottom), jnp.where(self.front, far, near))
        once_in = self.cross((once + back[1]).astype(BF), 0)
        mine = (inner_rows(top, near) + back[0] + once_in).astype(BF)
        return self.down(mine, at_once)

    def reduce_rows(self, left, near, far):
        rows = left.shape[1] // (2 * self.depth)
        blocks = []
        for part in (near, far):
            whole = inner_rows(left, part).astype(BF)
            cut = lambda s: whole[s * rows : (s + 1) * rows]
            lines = self.to_near([[cut(2 * z), cut(2 * z + 1)] for z in range(self.depth)])
            blocks.append([jnp.concatenate(line, axis=0) for line in lines])
        half = self.depth * rows
        sent = jnp.concatenate(
            [jnp.where(self.front, blocks[0][1], blocks[1][0]), blocks[1][1]], axis=0
        )
        back = self.cross(sent, 1)
        once = jnp.where(self.front, blocks[1][0], blocks[0][1])
        once_in = self.cross((once.astype(F32) + back[half:]).astype(BF), 0)
        mine = (blocks[0][0].astype(F32) + back[:half] + once_in).astype(BF)
        return self.down(mine, False)


class Plain:
    def __init__(self, rows):
        self.rows = rows
        self.x = lax.axis_index("rep") // 2
        self.core = lax.axis_index("rep") % 2
        self.front = jnp.bool_(True)

    def around(self, array):
        length = lax.axis_size("seq")
        reach = min(HALO // self.rows, length - 1)
        blocks, offsets = [array], [0]
        for offset in list(range(-reach, 0)) + list(range(1, reach + 1)):
            route = [(i + offset, i) for i in range(length) if 0 <= i + offset < length]
            blocks.append(lax.ppermute(array, "seq", route))
            offsets.append(offset)
        return blocks, offsets

    def collect(self, piece, at_once):
        return lax.all_gather(piece, "seq", axis=0, tiled=True)

    def share(self, near):
        far = swap_far(near)
        half = near.shape[0] // 2
        return (
            jnp.concatenate([near[:half], far[:half]], axis=0),
            jnp.concatenate([near[half:], far[half:]], axis=0),
        )

    def rows_of(self, size):
        return [jnp.int32(0), jnp.int32(lax.axis_size("seq") // 2 * size)]

    def columns(self, count):
        return jnp.zeros((1,), jnp.int32)

    def order(self, array, size):
        return array

    def restore(self, array, size):
        return array

    def reduce(self, left, near, far, at_once=False):
        mine = inner_rows(left, near) + swap_far(inner_rows(left, far).astype(BF))
        return lax.psum_scatter(mine, "seq", scatter_dimension=0, tiled=True).astype(BF)

    reduce_rows = reduce


def halves(front, pair, other):
    half = pair.shape[0] // 2
    one, two = pair[half:], other[:half]
    near = jnp.concatenate([pair[:half], jnp.where(front, two, one)], axis=0)
    far = jnp.concatenate([jnp.where(front, one, two), other[half:]], axis=0)
    return near, far


def lane_masks():
    lane = lax.broadcasted_iota(jnp.int32, (1, GROUP), 1)
    turned = [(lane % LANES) // (HEAD_DIM // 2) == i for i in range(4)]
    plain = [lane // HEAD_DIM == i for i in range(4)]
    return turned, plain


def only(mask, array):
    return jnp.where(mask, array, jnp.zeros_like(array))


def spin(raw, c, s, way):
    a, b = raw[:, :LANES], raw[:, LANES:]
    return a * c - way * (b * s), b * c + way * (a * s)


def prepare_kernel(places, *refs):
    *blocks, out = refs
    width = blocks[0].shape[1] - LANES
    rows = out.shape[0] // len(blocks)
    count = places.shape[0]
    size = width // count
    for i, block in enumerate(blocks):
        normal = centre(block[:, :width].astype(F32))[0].astype(BF)
        at = slice(i * rows, (i + 1) * rows)
        out[at, width:] = block[:, width:]
        for s in range(count):
            to = pl.multiple_of(places[s] * size, LANES)
            out[at, pl.ds(to, size)] = normal[:, s * size : (s + 1) * size]


def mix_kernel(rows, near, far, tables, *refs):
    near_out, far_out, cosine, sine = refs[-4:]
    half = near.shape[0]
    marks = rows[:, half : half + LANES].astype(F32)
    lane = lax.broadcasted_iota(jnp.int32, (1, LANES), 1).astype(F32)
    exact = lambda flags, table: jnp.dot(
        flags.astype(F32), table, preferred_element_type=F32, precision=lax.Precision.HIGHEST
    )
    coarse = exact(marks[:, 0:1] == lane, tables[:LANES])
    fine = exact(marks[:, 1:2] == lane, tables[LANES:])
    c = coarse[:, :LANES] * fine[:, :LANES] - coarse[:, LANES:] * fine[:, LANES:]
    s = coarse[:, LANES:] * fine[:, :LANES] + coarse[:, :LANES] * fine[:, LANES:]
    for weight, out in ((near, near_out), (far, far_out)):
        raw = dot(rows[:, :half], weight[...])
        for kind, scale in ((0, SCALE), (1, 1.0)):
            at = kind * GROUP
            a, b = spin(raw[:, at : at + GROUP], c, s, 1.0)
            out[:, at : at + LANES] = (a * scale).astype(BF)
            out[:, at + LANES : at + GROUP] = (b * scale).astype(BF)
        out[:, 2 * GROUP :] = raw[:, 2 * GROUP :].astype(BF)

    @pl.when(pl.program_id(0) == 0)
    def _():
        cosine[...] = c
        sine[...] = s


def attend_kernel(q0, k0, v0, q1, k1, v1, doc_row, doc_column, attended, attended_low, logs):
    turned, plain = lane_masks()
    allowed = doc_column[...] == doc_row[0]
    lane = lax.broadcasted_iota(jnp.int32, (1, LANES), 1)
    totals = jnp.zeros((q0.shape[0], LANES), F32)
    for group, (q, k, v) in enumerate(((q0, k0, v0), (q1, k1, v1))):
        queries, keys, values = q[...], k[...], v[...]
        kept = jnp.zeros(queries.shape, F32)
        for i in range(4):
            raw = outer_rows(only(turned[i], queries), keys)
            raw = jnp.where(allowed, raw, -jnp.inf)
            top = jnp.max(raw, axis=-1, keepdims=True)
            weights = jnp.exp(raw - top)
            total = jnp.sum(weights, axis=-1, keepdims=True)
            found = dot(weights.astype(BF), values) / total
            kept = jnp.where(plain[i], found, kept)
            totals = jnp.where(lane == 4 * group + i, top + jnp.log(total), totals)
        attended[:, group * GROUP : (group + 1) * GROUP] = kept
        attended_low[:, group * GROUP : (group + 1) * GROUP] = kept.astype(BF)
    logs[...] = totals


def around_kernel(grads, attended, logs, around, numbers):
    heads = HEADS // 2
    width = grads.shape[1]
    row = lax.broadcasted_iota(jnp.int32, (width, LANES), 0)
    lane = lax.broadcasted_iota(jnp.int32, (width, LANES), 1)
    low = grads[...].astype(BF)
    delta = jnp.dot(
        low.astype(F32) * attended[...],
        (row // HEAD_DIM == lane - 2 * heads).astype(F32),
        preferred_element_type=F32,
        precision=lax.Precision.HIGHEST,
    )
    both = logs[...] + delta
    numbers[...] = both
    high = both.astype(BF).astype(F32)
    around[:, :width] = low
    around[:, width:] = (high + pltpu.roll(both - high, heads, 1)).astype(BF)


def query_kernel(q0, k0, v0, q1, k1, v1, around, numbers, doc_row, doc_column, cosine, sine, d_q):
    turned, plain = lane_masks()
    allowed = doc_column[...] == doc_row[0]
    c, s = cosine[...] * SCALE, sine[...] * SCALE
    for group, (q, k, v) in enumerate(((q0, k0, v0), (q1, k1, v1))):
        queries, keys, values = q[...], k[...], v[...]
        grads = around[:, group * GROUP : (group + 1) * GROUP]
        kept = jnp.zeros(queries.shape, F32)
        for i in range(4):
            at = 4 * group + i
            raw = outer_rows(only(turned[i], queries), keys)
            weights = jnp.where(allowed, jnp.exp(raw - numbers[:, at : at + 1]), 0.0)
            d_weights = outer_rows(only(plain[i], grads), values)
            d_raw = (weights * (d_weights - numbers[:, 16 + at : 17 + at])).astype(BF)
            kept = jnp.where(turned[i], dot(d_raw, keys), kept)
        a, b = spin(kept, c, s, -1.0)
        d_q[:, group * GROUP : group * GROUP + LANES] = a.astype(BF)
        d_q[:, group * GROUP + LANES : (group + 1) * GROUP] = b.astype(BF)


def key_kernel(q0, k0, v0, q1, k1, v1, d_q, doc_row, doc_column, cosine, sine, *refs):
    *around, near, far = refs
    turned, plain = lane_masks()
    rows = k0.shape[0]
    c, s = cosine[...], sine[...]
    column = doc_column[...]
    kept = [[jnp.zeros(k0.shape, F32), jnp.zeros(k0.shape, F32)] for _ in (0, 1)]
    for j, block in enumerate(around):
        part = slice(j * rows, (j + 1) * rows)
        allowed = column == doc_row[0, :, part]
        numbers = block[:, 2 * GROUP :].astype(F32)
        numbers = (numbers + pltpu.roll(numbers, LANES - HEADS // 2, 1)).T
        for group, (q, k, v) in enumerate(((q0, k0, v0), (q1, k1, v1))):
            queries, keys, values = q[part, :], k[...], v[...]
            grads = block[:, group * GROUP : (group + 1) * GROUP]
            add_k = jnp.zeros(k0.shape, F32)
            add_v = jnp.zeros(k0.shape, F32)
            for i in range(4):
                at = 4 * group + i
                raw = outer_rows(only(turned[i], keys), queries)
                weights = jnp.where(allowed, jnp.exp(raw - numbers[at : at + 1, :]), 0.0)
                add_v = jnp.where(plain[i], dot(weights.astype(BF), grads), add_v)
                d_weights = outer_rows(only(plain[i], values), grads)
                d_raw = (weights * (d_weights - numbers[16 + at : 17 + at, :])).astype(BF)
                add_k = jnp.where(turned[i], dot(d_raw, queries), add_k)
            kept[group][0] += add_k
            kept[group][1] += add_v
    for group, out in enumerate((near, far)):
        a, b = spin(kept[group][0], c, s, -1.0)
        out[:, :GROUP] = d_q[:, group * GROUP : (group + 1) * GROUP]
        out[:, GROUP : GROUP + LANES] = a.astype(BF)
        out[:, GROUP + LANES : 2 * GROUP] = b.astype(BF)
        out[:, 2 * GROUP :] = kept[group][1].astype(BF)


def call_kernel(kernel, ins, outs, flops, grid=1, aliases=None):
    spec = lambda block, at: (
        pl.BlockSpec(memory_space=pltpu.SMEM if block is None else pl.ANY)
        if at is None
        else pl.BlockSpec(block, at)
    )
    return pl.pallas_call(
        kernel,
        grid=(grid,),
        in_specs=[spec(block, at) for _, block, at in ins],
        out_specs=tuple(pl.BlockSpec(block, at) for _, _, block, at in outs),
        out_shape=tuple(jax.ShapeDtypeStruct(shape, kind) for shape, kind, _, _ in outs),
        input_output_aliases=aliases or {},
        compiler_params=pltpu.CompilerParams(vmem_limit_bytes=40 * 2**20),
        cost_estimate=pl.CostEstimate(
            flops=flops, bytes_accessed=8 * 2**20, transcendentals=3 * 2**20
        ),
    )(*[a for a, _, _ in ins])


def gelu_parts(inner):
    share = 0.5 * (1.0 + lax.erf(inner * 0.7071067811865476))
    return inner * share, share + inner * (0.3989422804014327 * jnp.exp(-0.5 * inner * inner))


def hidden_kernel(marks, rows, grads, pair, other, shrink_pair, shrink_other, *refs):
    active, lifted_grads, out, out_there, d_rows, d_there = refs[:6]
    expand_w, shrink_w, semaphore = refs[6:]
    units = shrink_w.shape[0]
    half = pair.shape[0] // 2
    wide = shrink_pair.shape[1]
    places = marks.shape[0] - 2
    block = units // places
    front = marks[0] == 1
    x = marks[1]
    step = pl.program_id(0)

    def weights(source, start, at, row):
        return source.at[pl.ds(start, half)], expand_w.at[at, pl.ds(row, half)]

    def shrinks(source, high, at, low):
        found = []
        for j in range(places // 2):
            start = high * (units // 2) + j * block
            row = pl.multiple_of(marks[2 + low * (places // 2) + j], 16)
            column = pl.multiple_of(at * wide, LANES)
            found.append(
                (
                    source.at[pl.ds(start, block)],
                    shrink_w.at[pl.ds(row, block), pl.ds(column, wide)],
                )
            )
        return found

    def begin(moves, first):
        copies = [
            pltpu.make_async_copy(a, b, semaphore.at[first + k]) for k, (a, b) in enumerate(moves)
        ]
        for copy in copies:
            copy.start()
        return copies

    @pl.when(step == 0)
    def _():
        moves = [weights(pair, 0, x, 0), weights(other, half, 1 - x, half)]
        moves += shrinks(shrink_pair, 0, x, 0) + shrinks(shrink_other, 1, 1 - x, 1)
        copies = begin(moves, 0)
        for flag, low, high in ((front, other, pair), (jnp.logical_not(front), pair, other)):

            @pl.when(flag)
            def _():
                start = 0 if low is other else half
                back = half - start
                shrink_low = shrink_other if low is other else shrink_pair
                shrink_high = shrink_pair if low is other else shrink_other
                crossed = [weights(low, start, x, half), weights(high, back, 1 - x, 0)]
                crossed += shrinks(shrink_low, start // half, x, 1)
                crossed += shrinks(shrink_high, back // half, 1 - x, 0)
                for copy in begin(crossed, len(moves)):
                    copy.wait()

        for copy in copies:
            copy.wait()

    values, dy = rows[...], grads[...]
    tile = 256
    for at in range(0, units, tile):
        cut = slice(at, min(at + tile, units))
        inner = dot(values, expand_w[0, :, cut])
        gate = dot(values, expand_w[1, :, cut])
        d_active = outer_rows(dy, shrink_w[cut, :])
        value, slope = gelu_parts(inner)
        active[:, cut] = (value * gate).astype(BF)
        lifted_grads[x, :, cut] = (d_active * gate * slope).astype(BF)
        lifted_grads[1 - x, :, cut] = (d_active * value).astype(BF)
    result = dot(active[...], shrink_w[...])
    back = outer_rows(lifted_grads[x], expand_w[0]) + outer_rows(lifted_grads[1 - x], expand_w[1])

    @pl.when(step == 0)
    def _():
        out[...] = result
        d_rows[...] = back

    @pl.when(step == 1)
    def _():
        out_there[...] = result.astype(BF)
        d_there[...] = back.astype(BF)


def hidden(marks, rows, grads, expand, shrink):
    count, width = rows.shape
    units = expand[0].shape[1]
    size = count // 2
    moving = lambda i: (i, 0)
    still = lambda i: (0, 0)
    held = pl.BlockSpec(memory_space=pl.ANY)
    outs = [
        ((count, units), BF, (size, units), moving),
        ((2, count, units), BF, (2, size, units), lambda i: (0, i, 0)),
        ((size, width), F32, (size, width), still),
        ((size, width), BF, (size, width), still),
        ((size, width), F32, (size, width), still),
        ((size, width), BF, (size, width), still),
    ]
    return pl.pallas_call(
        hidden_kernel,
        grid=(2,),
        in_specs=[pl.BlockSpec(memory_space=pltpu.SMEM)]
        + [pl.BlockSpec((size, width), moving)] * 2
        + [held] * 4,
        out_specs=tuple(pl.BlockSpec(block, at) for _, _, block, at in outs),
        out_shape=tuple(jax.ShapeDtypeStruct(shape, kind) for shape, kind, _, _ in outs),
        scratch_shapes=[
            pltpu.VMEM((2, width, units), BF),
            pltpu.VMEM((units, width), BF),
            pltpu.SemaphoreType.DMA((2 * marks.shape[0],)),
        ],
        compiler_params=pltpu.CompilerParams(vmem_limit_bytes=48 * 2**20),
        cost_estimate=pl.CostEstimate(
            flops=12 * count * width * units,
            bytes_accessed=20 * 2**20,
            transcendentals=2 * count * units,
        ),
    )(marks, rows, grads, *expand, *shrink)


def on_device(
    direct,
    tokens,
    norm_first,
    joint_weight,
    output_weight,
    norm_second,
    expand_weight,
    shrink_weight,
    document_start,
    cotangent,
):
    rows, width = tokens.shape
    plan = Direct() if direct else Plain(rows)
    length = lax.axis_size("seq")
    here = lax.axis_index("seq")
    x, core = plan.x, plan.core
    near_x = x == 0
    depth = joint_weight.shape[0]
    unit_rows = shrink_weight.shape[0]
    unit_half = (unit_rows + 1) // 2
    units = -(-unit_half * length // LANES) * LANES
    while units % length:
        units += LANES
    unit_pad = units // length
    half_width = width // 2

    def mine(array, start):
        parts = [array[:, start + i * GROUP : start + (i + 1) * GROUP] for i in range(4)]
        low, high = pick(near_x, parts[0::2], parts[1::2])
        return jnp.where(core == 0, low, high)

    source = jnp.arange(GROUP)
    turn = (
        source[:, None]
        == ((source % LANES) // 32 * HEAD_DIM + source // LANES * 32 + source % 32)[None, :]
    ).astype(BF)
    gain_one = norm_first.astype(F32)[:, None]
    gain_two = norm_second.astype(F32)[:, None]
    joint_piece = jnp.concatenate(
        [
            (dot(mine(joint_weight, 0), turn) * gain_one).astype(BF),
            (dot(mine(joint_weight, width), turn) * gain_one).astype(BF),
            (mine(joint_weight, 2 * width).astype(F32) * gain_one).astype(BF),
            mine(output_weight, 0),
        ],
        axis=1,
    )
    slot = jnp.arange(units)
    inner = core * unit_half + slot % unit_pad
    fits = (slot % unit_pad < unit_half) & (inner < unit_rows)
    unit_of = jnp.where(fits, slot // unit_pad * unit_rows + inner, -2 * FF)
    spread_units = (jnp.arange(2 * FF)[:, None] == (unit_of + x * FF)[None, :]).astype(BF)
    expand_piece = (dot(expand_weight, spread_units) * gain_two).astype(BF)
    slot_row = jnp.arange(unit_pad)

    def picked(c):
        row = c * unit_half + slot_row
        row = jnp.where((slot_row < unit_half) & (row < unit_rows), row, -1)
        return (row[:, None] == jnp.arange(unit_rows)[None, :]).astype(BF)

    shrink_piece = dot(
        picked(core),
        jnp.where(near_x, shrink_weight[:, :half_width], shrink_weight[:, half_width:]),
    ).astype(BF)

    joint_rows = plan.collect(joint_piece, True)
    anchor = (lax.axis_index("rep") * length + here) * rows
    position = anchor + jnp.arange(rows, dtype=jnp.int32) - document_start
    marks = jnp.pad(
        jnp.stack([(position + 1) // 16, (position + 1) % 16], axis=1), ((0, 0), (0, LANES - 2))
    ).astype(BF)
    blocks, offsets = plan.around(jnp.concatenate([tokens, marks], axis=1))
    block_count = len(blocks)
    span = block_count * rows
    still = lambda i: (0, 0)
    moving = lambda i: (i, 0)
    (sent,) = call_kernel(
        prepare_kernel,
        [(plan.columns(width // depth), None, None)]
        + [(block, (rows, width + LANES), still) for block in blocks],
        [((span, width + LANES), BF, (span, width + LANES), still)],
        20 * span * width,
    )
    first = (sent, swap_core(sent))
    offset_rows = jnp.stack([jnp.int32(offset) for offset in offsets]) * rows
    index = (here * rows + offset_rows[:, None] + jnp.arange(rows)[None, :]).reshape(1, span)
    document_rows = []
    for rows_in in first:
        code = rows_in[:, width : width + 2].astype(F32).T
        code = code[:1] * 16.0 + code[1:]
        document_rows.append(jnp.where(code > 0, index.astype(F32) - (code - 1.0), FAR))
    document_row = jnp.stack(document_rows)
    document_column = jnp.concatenate([row[:, :rows] for row in document_rows], axis=1).T
    halves_of_head = HEAD_DIM // 2
    frequency = THETA ** (-(jnp.arange(halves_of_head, dtype=F32) * 2.0) / HEAD_DIM)
    frequency = jnp.tile(frequency, LANES // halves_of_head)[None, :]
    steps = jnp.arange(LANES, dtype=F32)[:, None]
    angle = jnp.concatenate([16.0 * steps * frequency, (steps - 1.0) * frequency], axis=0)
    tables = jnp.concatenate([jnp.cos(angle), jnp.sin(angle)], axis=1)
    cotangents = jnp.concatenate([cotangent, swap_core(cotangent)], axis=0)

    expand_rows = plan.collect(after(expand_piece, joint_rows), False)
    shrink_rows = plan.collect(after(shrink_piece, expand_rows), False)
    joint_near, joint_far = halves(plan.front, *plan.share(joint_rows))
    expand_both = plan.share(expand_rows)
    shrink_both = plan.share(shrink_rows)
    output_mine = jnp.concatenate([joint_near[:, 3 * GROUP :], joint_far[:, 3 * GROUP :]], axis=1)
    output_all = jnp.concatenate([output_mine, swap_core(output_mine)], axis=1)

    def turn_columns(array):
        parts = [array[:, i * GROUP : (i + 1) * GROUP] for i in range(4)]
        parts = pick(core == 0, parts, parts[2:] + parts[:2])
        left, right = pick(near_x, parts[:2], parts[1::-1]), pick(near_x, parts[2:], parts[:1:-1])
        return jnp.concatenate(left + right, axis=-1)

    wide = 3 * GROUP
    mixed = ()
    turns = []
    for t in (0, 1):
        there = functools.partial(lambda shift, i: (i + shift, 0), t * block_count)
        *mixed, cosine, sine = call_kernel(
            mix_kernel,
            [
                (first[t], (rows, width + LANES), moving),
                (joint_near, (width, wide), still),
                (joint_far, (width, wide), still),
                (tables, (2 * LANES, 2 * LANES), still),
            ]
            + [(array, (8, LANES), None) for array in mixed],
            [((2 * span, wide), BF, (rows, wide), there)] * 2
            + [((rows, LANES), F32, (rows, LANES), still)] * 2,
            2 * span * width * 2 * wide,
            block_count,
            {4 + i: i for i in range(len(mixed))},
        )
        turns.append((cosine, sine))
    cosine, sine = [jnp.concatenate(pair, axis=0) for pair in zip(*turns)]
    score_flops = 2 * 2 * rows * span * GROUP * 8
    column = lambda kind, every: (
        ((span, GROUP), lambda i: (i, kind))
        if every
        else ((rows, GROUP), lambda i: (i * block_count, kind))
    )
    wide_keys = [
        (array, *column(kind, kind > 0)) for array in mixed for kind in range(3)
    ]
    wide_queries = [
        (array, *column(kind, kind == 0)) for array in mixed for kind in range(3)
    ]
    documents = [
        (document_row, (1, 1, span), lambda i: (i, 0, 0)),
        (document_column, (rows, 1), moving),
    ]
    both = lambda w, kind: ((2 * rows, w), kind, (rows, w), moving)
    attended, attended_low, logs = call_kernel(
        attend_kernel,
        wide_keys + documents,
        [both(2 * GROUP, F32), both(2 * GROUP, BF), both(LANES, F32)],
        2 * score_flops,
        2,
    )
    attended_there = swap_core(attended_low)
    attended_there = jnp.concatenate([attended_there[rows:], attended_there[:rows]], axis=0)
    attended_rows = plan.order(
        turn_columns(jnp.concatenate([attended_low, attended_there], axis=1)), depth
    )
    middle = tokens.astype(F32) + turn_columns(dot(attended_rows[:rows], output_all))
    second, second_scale = centre(middle)
    second_low = plan.order(second.astype(BF), depth)
    second_both = jnp.concatenate([second_low, swap_core(second_low)], axis=0)

    where = jnp.stack(
        [plan.front.astype(jnp.int32), x.astype(jnp.int32)]
        + [row.astype(jnp.int32) for row in plan.rows_of(unit_pad)]
    )
    active_low, lifted_grads, out, out_there, second_grad, second_there = hidden(
        where, second_both, cotangents, expand_both, shrink_both
    )
    result = middle + out + swap_core(out_there).astype(F32)
    second_grad = second_grad + swap_core(second_there).astype(F32)
    middle_grad = cotangent.astype(F32) + centre_back(
        second, second_scale, plan.restore(second_grad, depth)
    )
    branch = middle_grad.astype(BF)
    branch_both = turn_columns(jnp.concatenate([branch, swap_core(branch)], axis=0))
    attended_grad = turn_columns(plan.restore(outer_rows(branch_both, output_all), depth))
    around, numbers = call_kernel(
        around_kernel,
        [
            (attended_grad[:, : 2 * GROUP], (rows, 2 * GROUP), moving),
            (attended, (rows, 2 * GROUP), moving),
            (logs, (rows, LANES), moving),
        ],
        [both(2 * GROUP + LANES, BF), both(LANES, F32)],
        2**28,
        2,
    )
    arounds, _ = plan.around(around)
    turning = [(cosine, (rows, LANES), moving), (sine, (rows, LANES), moving)]
    (query_grad,) = call_kernel(
        query_kernel,
        wide_keys
        + [
            (around, (rows, 2 * GROUP), moving),
            (numbers, (rows, LANES), moving),
        ]
        + documents
        + turning,
        [both(2 * GROUP, BF)],
        3 * score_flops,
        2,
    )
    mixed_grads = call_kernel(
        key_kernel,
        wide_queries
        + [(query_grad, (rows, 2 * GROUP), moving)]
        + documents
        + turning
        + [(block, (rows, 2 * GROUP + LANES), moving) for block in arounds],
        [both(wide, BF), both(wide, BF)],
        4 * score_flops,
        2,
    )
    first_part = outer_rows(mixed_grads[0], joint_near[:, :wide]) + outer_rows(
        mixed_grads[1], joint_far[:, :wide]
    )
    first_grad = first_part[:rows] + swap_core(first_part[rows:].astype(BF)).astype(F32)
    normal, normal_scale = centre(tokens.astype(F32))
    tokens_grad = middle_grad + centre_back(
        normal, normal_scale, plan.restore(first_grad, depth)
    )

    left, right = cotangents[:, :half_width], cotangents[:, half_width:]
    shrink_share = plan.reduce_rows(active_low, *pick(near_x, [left, right], [right, left]))
    expand_share = plan.reduce(second_both, lifted_grads[0], lifted_grads[1])
    output_share = plan.reduce(
        attended_rows, branch_both[:, :GROUP], branch_both[:, GROUP : 2 * GROUP]
    )
    joint_share = plan.reduce(
        jnp.concatenate([rows_in[:rows, :width] for rows_in in first], axis=0),
        mixed_grads[0],
        mixed_grads[1],
        True,
    )

    def spread(share):
        pair = [share, swap_far(share)]
        low, high = pick(near_x, pair, pair[::-1])
        both = jnp.concatenate([low, high], axis=1)
        there = swap_core(both)
        size = share.shape[1]
        cores = pick(core == 0, [both, there], [there, both])
        return [[part[:, :size], part[:, size:]] for part in cores]

    shrink_shares = spread(shrink_share)
    shrink_grad = jnp.concatenate(
        [
            inner_rows(picked(0), shrink_shares[0][i]) + inner_rows(picked(1), shrink_shares[1][i])
            for i in (0, 1)
        ],
        axis=1,
    )
    expand_shares = spread(expand_share)
    expand_raw = 0.0
    for c in (0, 1):
        inner = c * unit_half + slot % unit_pad
        fits = (slot % unit_pad < unit_half) & (inner < unit_rows)
        unit_at = jnp.where(fits, slot // unit_pad * unit_rows + inner, -1)
        back = (unit_at[:, None] == jnp.arange(FF)[None, :]).astype(BF)
        expand_raw = expand_raw + dot(jnp.concatenate(expand_shares[c], axis=0), back)
    expand_raw = jnp.concatenate([expand_raw[:depth], expand_raw[depth:]], axis=1)
    expand_grad = expand_raw * gain_two
    second_gain_grad = jnp.sum(expand_raw * expand_weight.astype(F32), axis=1)
    output_shares = spread(output_share)
    output_grad = jnp.concatenate(output_shares[0] + output_shares[1], axis=1).astype(F32)
    joint_four = spread(joint_share)
    columns = []
    for kind in range(3):
        for c in (0, 1):
            for i in (0, 1):
                piece = joint_four[c][i][:, kind * GROUP : (kind + 1) * GROUP]
                columns.append(
                    lax.dot_general(
                        piece, turn, (((1,), (1,)), ((), ())), preferred_element_type=F32
                    )
                    if kind < 2
                    else piece.astype(F32)
                )
    joint_raw = jnp.concatenate(columns, axis=1)
    joint_grad = joint_raw * gain_one
    first_gain_grad = jnp.sum(joint_raw * joint_weight.astype(F32), axis=1)
    return (
        result.astype(BF),
        tokens_grad.astype(BF),
        first_gain_grad,
        joint_grad,
        output_grad,
        second_gain_grad,
        expand_grad,
        shrink_grad,
    )


def solution(mesh):
    placed = (
        P(("rep", "seq"), None),
        P("seq"),
        P("seq", None),
        P("seq", None),
        P("seq"),
        P("seq", None),
        P("seq", None),
        P(("rep", "seq")),
        P(("rep", "seq"), None),
    )
    return jax.shard_map(
        functools.partial(on_device, mesh.shape["seq"] == 8),
        mesh=mesh,
        in_specs=placed,
        out_specs=(
            P(("rep", "seq"), None),
            P(("rep", "seq"), None),
            P("seq"),
            P("seq", None),
            P("seq", None),
            P("seq"),
            P("seq", None),
            P("seq", None),
        ),
        check_vma=False,
    )
```

```python
import functools

import jax
import jax.numpy as jnp
from jax import lax
from jax.experimental import pallas as pl
from jax.experimental.pallas import tpu as pltpu
from jax.sharding import PartitionSpec as P

HEADS = 16
HEAD_DIM = 64
FF = 2624
HALO = 512
EPSILON = 1e-05
THETA = 160000.0
SCALE = 0.125
LANES = 128
GROUP = 256
FAR = -1e6
LONG = 10**11
BF = jnp.bfloat16
F32 = jnp.float32


def dot(left, right):
    return jnp.dot(left, right, preferred_element_type=F32)


def inner_rows(left, right):
    return lax.dot_general(left, right, (((0,), (0,)), ((), ())), preferred_element_type=F32)


def outer_rows(left, right):
    return lax.dot_general(left, right, (((1,), (1,)), ((), ())), preferred_element_type=F32)


def pick(flag, one, two):
    return [jnp.where(flag, a, b) for a, b in zip(one, two)]


def centre(rows):
    middle = jnp.mean(rows, axis=-1, keepdims=True)
    centered = rows - middle
    spread = jnp.mean(centered * centered, axis=-1, keepdims=True)
    scale = lax.rsqrt(spread + EPSILON)
    return centered * scale, scale


def centre_back(normal, scale, grads):
    return scale * (
        grads
        - jnp.mean(grads, axis=-1, keepdims=True)
        - normal * jnp.mean(grads * normal, axis=-1, keepdims=True)
    )


def two_parts(values):
    high = lax.reduce_precision(values, 8, 7)
    return high.astype(BF), (values - high).astype(BF)


def swap_core(array):
    return lax.ppermute(array, "rep", [(i, i ^ 1) for i in range(lax.axis_size("rep"))])


def swap_far(array):
    return lax.ppermute(array, "rep", [(i, i ^ 2) for i in range(lax.axis_size("rep"))])


class Moves:
    def __init__(self):
        self.recent = []

    def send(self, array, axes, route):
        self.recent.append(array)
        return lax.ppermute(array, axes, route)

    def across(self, array, flip):
        return self.send(array, "rep", [(i, i ^ flip) for i in range(lax.axis_size("rep"))])

    def given(self):
        found, self.recent = self.recent, []
        return found


class Direct(Moves):
    depth = 4

    def __init__(self):
        super().__init__()
        self.place = lax.axis_index("seq")
        self.z = self.place // 2
        self.y = self.place % 2
        self.x = lax.axis_index("rep") // 2
        self.core = lax.axis_index("rep") % 2
        self.front = self.core == 0

    def along(self, array, flip):
        route = [(s, s ^ (2 * flip)) for s in range(2 * self.depth)]
        return self.send(array, "seq", route)

    def cross(self, array, turn):
        n = 2 * self.depth
        route = []
        for r in range(4):
            for s in range(n):
                to = (r ^ 2, s) if r % 2 == turn else (r, s ^ 1)
                route.append((r * n + s, to[0] * n + to[1]))
        return self.send(array, ("rep", "seq"), route)

    def around(self, array):
        rows = array.shape[0]
        last = 2 * self.depth
        low = self.send(array, "seq", [(s, s + 2) for s in range(last - 2)])
        high = self.send(array, "seq", [(s, s - 2) for s in range(2, last)])
        low = yield low
        high = yield high
        sent = jnp.concatenate([array, jnp.where(self.y == 0, high, low)], axis=0)
        beside = yield self.send(sent, "seq", [(s, s ^ 1) for s in range(last)])
        step = 1 - 2 * self.y
        return [array, low, high, beside[:rows], beside[rows:]], [0, -2, 2, step, -step]

    def gather(self, piece, at_once):
        if at_once:
            sent = [self.along(piece, k) for k in (1, 2, 3)]
            found = [piece]
            for array in sent:
                array = yield array
                found.append(array)
            rows = jnp.concatenate(found, axis=0)
        else:
            there = yield self.along(piece, 1)
            pair = jnp.concatenate([piece, there], axis=0)
            there = yield self.along(pair, 2)
            rows = jnp.concatenate([pair, there], axis=0)
        once = yield self.cross(rows, 0)
        pair = jnp.concatenate([rows, once], axis=0)
        other = yield self.cross(pair, 1)
        return pair, other

    def to_near(self, grid):
        turned = [pick(self.y == 0, pair, pair[::-1]) for pair in grid]
        near = []
        for y in (0, 1):
            a, b, c, d = [pair[y] for pair in turned]
            a, b, c, d = pick(self.z % 2 == 0, [a, b, c, d], [b, a, d, c])
            near.append(pick(self.z // 2 == 0, [a, b, c, d], [c, d, a, b]))
        return near

    def to_mesh(self, near):
        lines = []
        for a, b, c, d in near:
            a, b, c, d = pick(self.z % 2 == 0, [a, b, c, d], [b, a, d, c])
            lines.append(pick(self.z // 2 == 0, [a, b, c, d], [c, d, a, b]))
        return [pick(self.y == 0, list(pair), list(pair)[::-1]) for pair in zip(*lines)]

    def rows_of(self, size):
        return [
            (2 * (self.z ^ k) + (self.y ^ y)) * size for y in (0, 1) for k in range(self.depth)
        ]

    def columns(self, count):
        z, y = jnp.arange(count) // 2, jnp.arange(count) % 2
        return (4 * (y ^ self.y) + (z ^ self.z)).astype(jnp.int32)

    def order(self, array, size):
        n = self.depth
        cut = lambda s: array[..., s * size : (s + 1) * size]
        near = self.to_near([[cut(2 * z), cut(2 * z + 1)] for z in range(n)])
        return jnp.concatenate(near[0] + near[1], axis=-1)

    def restore(self, array, size):
        n = self.depth
        cut = lambda j: array[..., j * size : (j + 1) * size]
        grid = self.to_mesh([[cut(n * y + k) for k in range(n)] for y in (0, 1)])
        return jnp.concatenate([part for pair in grid for part in pair], axis=-1)

    def down(self, mine, at_once):
        rows = mine.shape[0] // 4
        cut = lambda k, n: mine[k * rows : (k + n) * rows]
        if at_once:
            sent = [self.along(cut(k, 1), k) for k in (1, 2, 3)]
            total = cut(0, 1).astype(F32)
            for array in sent:
                array = yield array
                total = total + array.astype(F32)
            share = total.astype(BF)
        else:
            there = yield self.along(cut(2, 2), 2)
            pair = (cut(0, 2).astype(F32) + there.astype(F32)).astype(BF)
            there = yield self.along(pair[rows:], 1)
            share = (pair[:rows].astype(F32) + there.astype(F32)).astype(BF)
        return (yield from self.spread(share))

    def reduce(self, left, near, far, at_once):
        half = left.shape[1] // 2
        top, bottom = left[:, :half], left[:, half:]
        sent = lax.dot_general(
            jnp.stack([jnp.where(self.front, bottom, top), bottom]),
            jnp.stack([jnp.where(self.front, near, far), far]),
            (((1,), (1,)), ((0,), (0,))),
            preferred_element_type=F32,
        ).astype(BF)
        back = yield self.cross(sent, 1)
        once = inner_rows(jnp.where(self.front, top, bottom), jnp.where(self.front, far, near))
        once_in = yield self.cross((once + back[1]).astype(BF), 0)
        mine = (inner_rows(top, near) + back[0] + once_in).astype(BF)
        return (yield from self.down(mine, at_once))

    def reduce_blocks(self, near, far):
        back = yield self.across(far, 2)
        total = (near.astype(F32) + back.astype(F32)).astype(BF)
        lines = self.to_near([total[2 * z : 2 * z + 2] for z in range(self.depth)])
        mine, sent = [jnp.concatenate(line, axis=0) for line in lines]
        route = [(s, s ^ 1) for s in range(2 * self.depth)]
        back = yield self.send(sent, "seq", route)
        mine = (mine.astype(F32) + back.astype(F32)).astype(BF)
        return (yield from self.down(mine, False))

    def spread(self, share):
        there = yield self.across(share, 2)
        pair = [share, there]
        low, high = pick(self.x == 0, pair, pair[::-1])
        both = jnp.concatenate([low, high], axis=1)
        there = yield self.across(both, 1)
        size = share.shape[1]
        cores = pick(self.core == 0, [both, there], [there, both])
        return [[part[:, :size], part[:, size:]] for part in cores]


class Plain(Moves):
    def __init__(self, rows):
        super().__init__()
        self.rows = rows
        self.x = lax.axis_index("rep") // 2
        self.core = lax.axis_index("rep") % 2
        self.front = jnp.bool_(True)

    def around(self, array):
        length = lax.axis_size("seq")
        reach = min(HALO // self.rows, length - 1)
        blocks, offsets = [array], [0]
        for offset in list(range(-reach, 0)) + list(range(1, reach + 1)):
            route = [(i + offset, i) for i in range(length) if 0 <= i + offset < length]
            blocks.append((yield self.send(array, "seq", route)))
            offsets.append(offset)
        return blocks, offsets

    def gather(self, piece, at_once):
        near = yield lax.all_gather(piece, "seq", axis=0, tiled=True)
        far = yield self.across(near, 2)
        half = near.shape[0] // 2
        return (
            jnp.concatenate([near[:half], far[:half]], axis=0),
            jnp.concatenate([near[half:], far[half:]], axis=0),
        )

    def rows_of(self, size):
        return [jnp.int32(0), jnp.int32(lax.axis_size("seq") // 2 * size)]

    def columns(self, count):
        return jnp.zeros((1,), jnp.int32)

    def order(self, array, size):
        return array

    def restore(self, array, size):
        return array

    def reduce(self, left, near, far, at_once=False):
        back = yield self.across(inner_rows(left, far).astype(BF), 2)
        mine = inner_rows(left, near) + back
        share = lax.psum_scatter(mine, "seq", scatter_dimension=0, tiled=True).astype(BF)
        return (yield from self.spread(share))

    def reduce_blocks(self, near, far):
        back = yield self.across(far, 2)
        mine = (near.astype(F32) + back).reshape(-1, near.shape[2])
        share = lax.psum_scatter(mine, "seq", scatter_dimension=0, tiled=True).astype(BF)
        return (yield from self.spread(share))

    spread = Direct.spread


def gate(array, *earlier):
    return lax.optimization_barrier((array,) + earlier)[0]


class Chain:
    def __init__(self, plan, steps):
        self.plan, self.steps = plan, steps
        self.value = None
        self.sent = next(steps)
        self.operands = tuple(plan.given())

    def hold(self, *earlier):
        if self.sent is not None:
            self.sent = gate(self.sent, *earlier)

    def step(self, count=1):
        for _ in range(count):
            if self.sent is not None:
                try:
                    self.sent = self.steps.send(self.sent)
                except StopIteration as end:
                    self.sent, self.value = None, end.value
                self.operands = tuple(self.plan.given())

    def end(self):
        while self.sent is not None:
            self.step()
        return self.value


def halves(front, pair, other):
    half = pair.shape[0] // 2
    one, two = pair[half:], other[:half]
    near = jnp.concatenate([pair[:half], jnp.where(front, two, one)], axis=0)
    far = jnp.concatenate([jnp.where(front, one, two), other[half:]], axis=0)
    return near, far


def lane_masks():
    lane = lax.broadcasted_iota(jnp.int32, (1, GROUP), 1)
    turned = [(lane % LANES) // (HEAD_DIM // 2) == i for i in range(4)]
    plain = [lane // HEAD_DIM == i for i in range(4)]
    return turned, plain


def only(mask, array):
    return jnp.where(mask, array, jnp.zeros_like(array))


def spin(raw, c, s, way):
    a, b = raw[:, :LANES], raw[:, LANES:]
    return a * c - way * (b * s), b * c + way * (a * s)


def prepare_kernel(places, *refs):
    *blocks, out = refs
    width = blocks[0].shape[1] - LANES
    rows = out.shape[0] // len(blocks)
    count = places.shape[0]
    size = width // count
    for i, block in enumerate(blocks):
        normal = centre(block[:, :width].astype(F32))[0].astype(BF)
        at = slice(i * rows, (i + 1) * rows)
        out[at, width:] = block[:, width:]
        for s in range(count):
            to = pl.multiple_of(places[s] * size, LANES)
            out[at, pl.ds(to, size)] = normal[:, s * size : (s + 1) * size]


def mix_kernel(ours, theirs, near, far, tables, near_out, far_out, cosine, sine):
    count = pl.num_programs(0) // 2
    step = pl.program_id(0)
    half = near.shape[0]
    rows = jnp.where(step < count, ours[...], theirs[...])
    marks = rows[:, half : half + LANES].astype(F32)
    lane = lax.broadcasted_iota(jnp.int32, (1, LANES), 1).astype(F32)
    exact = lambda flags, table: jnp.dot(
        flags.astype(F32), table, preferred_element_type=F32, precision=lax.Precision.HIGHEST
    )
    coarse = exact(marks[:, 0:1] == lane, tables[:LANES])
    fine = exact(marks[:, 1:2] == lane, tables[LANES:])
    c = coarse[:, :LANES] * fine[:, :LANES] - coarse[:, LANES:] * fine[:, LANES:]
    s = coarse[:, LANES:] * fine[:, :LANES] + coarse[:, :LANES] * fine[:, LANES:]
    for weight, out in ((near, near_out), (far, far_out)):
        raw = dot(rows[:, :half], weight[...])
        for kind, scale in ((0, SCALE), (1, 1.0)):
            at = kind * GROUP
            a, b = spin(raw[:, at : at + GROUP], c, s, 1.0)
            out[:, at : at + LANES] = (a * scale).astype(BF)
            out[:, at + LANES : at + GROUP] = (b * scale).astype(BF)
        out[:, 2 * GROUP :] = raw[:, 2 * GROUP :].astype(BF)

    @pl.when(step % count == 0)
    def _():
        cosine[...] = c
        sine[...] = s


def attend_kernel(q0, k0, v0, q1, k1, v1, doc_row, doc_column, attended, attended_low, logs):
    turned, plain = lane_masks()
    allowed = doc_column[...] == doc_row[0]
    lane = lax.broadcasted_iota(jnp.int32, (1, LANES), 1)
    totals = jnp.zeros((q0.shape[0], LANES), F32)
    for group, (q, k, v) in enumerate(((q0, k0, v0), (q1, k1, v1))):
        queries, keys, values = q[...], k[...], v[...]
        kept = jnp.zeros(queries.shape, F32)
        for i in range(4):
            raw = outer_rows(only(turned[i], queries), keys)
            raw = jnp.where(allowed, raw, -jnp.inf)
            top = jnp.max(raw, axis=-1, keepdims=True)
            weights = jnp.exp(raw - top)
            total = jnp.sum(weights, axis=-1, keepdims=True)
            found = dot(weights.astype(BF), values) / total
            kept = jnp.where(plain[i], found, kept)
            totals = jnp.where(lane == 4 * group + i, top + jnp.log(total), totals)
        attended[:, group * GROUP : (group + 1) * GROUP] = kept
        attended_low[:, group * GROUP : (group + 1) * GROUP] = kept.astype(BF)
    logs[...] = totals


def around_kernel(grads, attended, logs, around, numbers):
    heads = HEADS // 2
    width = grads.shape[1]
    row = lax.broadcasted_iota(jnp.int32, (width, LANES), 0)
    lane = lax.broadcasted_iota(jnp.int32, (width, LANES), 1)
    low = grads[...].astype(BF)
    delta = jnp.dot(
        low.astype(F32) * attended[...],
        (row // HEAD_DIM == lane - 2 * heads).astype(F32),
        preferred_element_type=F32,
        precision=lax.Precision.HIGHEST,
    )
    both = logs[...] + delta
    numbers[...] = both
    high = both.astype(BF).astype(F32)
    around[:, :width] = low
    around[:, width:] = (high + pltpu.roll(both - high, heads, 1)).astype(BF)


def query_kernel(q0, k0, v0, q1, k1, v1, around, numbers, doc_row, doc_column, cosine, sine, d_q):
    turned, plain = lane_masks()
    allowed = doc_column[...] == doc_row[0]
    c, s = cosine[...] * SCALE, sine[...] * SCALE
    for group, (q, k, v) in enumerate(((q0, k0, v0), (q1, k1, v1))):
        queries, keys, values = q[...], k[...], v[...]
        grads = around[:, group * GROUP : (group + 1) * GROUP]
        kept = jnp.zeros(queries.shape, F32)
        for i in range(4):
            at = 4 * group + i
            raw = outer_rows(only(turned[i], queries), keys)
            weights = jnp.where(allowed, jnp.exp(raw - numbers[:, at : at + 1]), 0.0)
            d_weights = outer_rows(only(plain[i], grads), values)
            d_raw = (weights * (d_weights - numbers[:, 16 + at : 17 + at])).astype(BF)
            kept = jnp.where(turned[i], dot(d_raw, keys), kept)
        a, b = spin(kept, c, s, -1.0)
        d_q[:, group * GROUP : group * GROUP + LANES] = a.astype(BF)
        d_q[:, group * GROUP + LANES : (group + 1) * GROUP] = b.astype(BF)


def key_kernel(q0, k0, v0, q1, k1, v1, d_q, doc_row, doc_column, cosine, sine, *refs):
    *around, near, far = refs
    turned, plain = lane_masks()
    rows = k0.shape[0]
    c, s = cosine[...], sine[...]
    column = doc_column[...]
    kept = [[jnp.zeros(k0.shape, F32), jnp.zeros(k0.shape, F32)] for _ in (0, 1)]
    for j, block in enumerate(around):
        part = slice(j * rows, (j + 1) * rows)
        allowed = column == doc_row[0, :, part]
        numbers = block[:, 2 * GROUP :].astype(F32)
        numbers = (numbers + pltpu.roll(numbers, LANES - HEADS // 2, 1)).T
        for group, (q, k, v) in enumerate(((q0, k0, v0), (q1, k1, v1))):
            queries, keys, values = q[part, :], k[...], v[...]
            grads = block[:, group * GROUP : (group + 1) * GROUP]
            add_k = jnp.zeros(k0.shape, F32)
            add_v = jnp.zeros(k0.shape, F32)
            for i in range(4):
                at = 4 * group + i
                raw = outer_rows(only(turned[i], keys), queries)
                weights = jnp.where(allowed, jnp.exp(raw - numbers[at : at + 1, :]), 0.0)
                add_v = jnp.where(plain[i], dot(weights.astype(BF), grads), add_v)
                d_weights = outer_rows(only(plain[i], values), grads)
                d_raw = (weights * (d_weights - numbers[16 + at : 17 + at, :])).astype(BF)
                add_k = jnp.where(turned[i], dot(d_raw, queries), add_k)
            kept[group][0] += add_k
            kept[group][1] += add_v
    for group, out in enumerate((near, far)):
        a, b = spin(kept[group][0], c, s, -1.0)
        out[:, :GROUP] = d_q[:, group * GROUP : (group + 1) * GROUP]
        out[:, GROUP : GROUP + LANES] = a.astype(BF)
        out[:, GROUP + LANES : 2 * GROUP] = b.astype(BF)
        out[:, 2 * GROUP :] = kept[group][1].astype(BF)


def pack_kernel(place, active, grads, attended, branch, near, far):
    count, depth = near.shape[0], attended.shape[1] // near.shape[0]
    rows = active.shape[1] // count
    wide = near.shape[2]
    for i in (0, 1):
        one = inner_rows(active[...], grads[:, i * wide : (i + 1) * wide]).astype(BF)
        two = inner_rows(attended[...], branch[i]).astype(BF)

        def store(out):
            for s in range(count):
                out[s, :rows] = one[s * rows : (s + 1) * rows]
                at = s * depth
                out[s, rows:, :GROUP] = two[at : at + depth // 2]
                out[s, rows:, GROUP:] = two[at + depth // 2 : at + depth]

        @pl.when(place[0] == i)
        def _():
            store(near)

        @pl.when(place[0] != i)
        def _():
            store(far)


def call_kernel(kernel, ins, outs, grid=1, room=56, micros=5):
    spec = lambda block, at: (
        pl.BlockSpec(memory_space=pltpu.SMEM) if block is None else pl.BlockSpec(block, at)
    )
    return pl.pallas_call(
        kernel,
        grid=(grid,),
        in_specs=[spec(block, at) for _, block, at in ins],
        out_specs=tuple(pl.BlockSpec(block, at) for _, _, block, at in outs),
        out_shape=tuple(jax.ShapeDtypeStruct(shape, kind) for shape, kind, _, _ in outs),
        compiler_params=pltpu.CompilerParams(vmem_limit_bytes=room * 2**20),
        cost_estimate=pl.CostEstimate(flops=micros * 10**9, bytes_accessed=1, transcendentals=0),
    )(*[a for a, _, _ in ins])


def gelu_parts(inner):
    share = 0.5 * (1.0 + lax.erf(inner * 0.7071067811865476))
    return inner * share, share + inner * (0.3989422804014327 * jnp.exp(-0.5 * inner * inner))


def hidden_kernel(marks, rows, grads, pair, other, shrink_pair, shrink_other, *refs):
    active, lifted_grads, out, out_there, d_rows, d_there = refs[:6]
    expand_w, shrink_w, semaphore = refs[6:]
    units = shrink_w.shape[0]
    half = pair.shape[0] // 2
    wide = shrink_pair.shape[1]
    places = marks.shape[0] - 2
    block = units // places
    front = marks[0] == 1
    x = marks[1]
    step = pl.program_id(0)

    def weights(source, start, at, row):
        return source.at[pl.ds(start, half)], expand_w.at[at, pl.ds(row, half)]

    def shrinks(source, high, at, low):
        found = []
        for j in range(places // 2):
            start = high * (source.shape[0] // 2) + j * block
            row = pl.multiple_of(marks[2 + low * (places // 2) + j], 16)
            column = pl.multiple_of(at * wide, LANES)
            found.append(
                (
                    source.at[pl.ds(start, block)],
                    shrink_w.at[pl.ds(row, block), pl.ds(column, wide)],
                )
            )
        return found

    def begin(moves, first):
        copies = [
            pltpu.make_async_copy(a, b, semaphore.at[first + k]) for k, (a, b) in enumerate(moves)
        ]
        for copy in copies:
            copy.start()
        return copies

    @pl.when(step == 0)
    def _():
        moves = [weights(pair, 0, x, 0), weights(other, half, 1 - x, half)]
        moves += shrinks(shrink_pair, 0, x, 0) + shrinks(shrink_other, 1, 1 - x, 1)
        copies = begin(moves, 0)
        for flag, low, high in ((front, other, pair), (jnp.logical_not(front), pair, other)):

            @pl.when(flag)
            def _():
                start = 0 if low is other else half
                back = half - start
                shrink_low = shrink_other if low is other else shrink_pair
                shrink_high = shrink_pair if low is other else shrink_other
                crossed = [weights(low, start, x, half), weights(high, back, 1 - x, 0)]
                crossed += shrinks(shrink_low, start // half, x, 1)
                crossed += shrinks(shrink_high, back // half, 1 - x, 0)
                for copy in begin(crossed, len(moves)):
                    copy.wait()

        for copy in copies:
            copy.wait()

    values, dy = rows[...], grads[...]
    tile = 256
    for at in range(0, units, tile):
        cut = slice(at, min(at + tile, units))
        inner = dot(values, expand_w[0, :, cut])
        gate = dot(values, expand_w[1, :, cut])
        d_active = outer_rows(dy, shrink_w[cut, :])
        value, slope = gelu_parts(inner)
        active[:, cut] = (value * gate).astype(BF)
        lifted_grads[x, :, cut] = (d_active * gate * slope).astype(BF)
        lifted_grads[1 - x, :, cut] = (d_active * value).astype(BF)
    result = dot(active[...], shrink_w[...])
    back = outer_rows(lifted_grads[x], expand_w[0]) + outer_rows(lifted_grads[1 - x], expand_w[1])

    @pl.when(step == 0)
    def _():
        out[...] = result
        d_rows[...] = back

    @pl.when(step == 1)
    def _():
        out_there[...] = result.astype(BF)
        d_there[...] = back.astype(BF)


def hidden(marks, rows, grads, expand, shrink):
    count, width = rows.shape
    units = expand[0].shape[1]
    size = count // 2
    moving = lambda i: (i, 0)
    still = lambda i: (0, 0)
    held = pl.BlockSpec(memory_space=pl.ANY)
    outs = [
        ((count, units), BF, (size, units), moving),
        ((2, count, units), BF, (2, size, units), lambda i: (0, i, 0)),
        ((size, width), F32, (size, width), still),
        ((size, width), BF, (size, width), still),
        ((size, width), F32, (size, width), still),
        ((size, width), BF, (size, width), still),
    ]
    return pl.pallas_call(
        hidden_kernel,
        grid=(2,),
        in_specs=[pl.BlockSpec(memory_space=pltpu.SMEM)]
        + [pl.BlockSpec((size, width), moving)] * 2
        + [held] * 4,
        out_specs=tuple(pl.BlockSpec(block, at) for _, _, block, at in outs),
        out_shape=tuple(jax.ShapeDtypeStruct(shape, kind) for shape, kind, _, _ in outs),
        scratch_shapes=[
            pltpu.VMEM((2, width, units), BF),
            pltpu.VMEM((units, width), BF),
            pltpu.SemaphoreType.DMA((2 * marks.shape[0],)),
        ],
        compiler_params=pltpu.CompilerParams(vmem_limit_bytes=36 * 2**20),
        cost_estimate=pl.CostEstimate(flops=8 * 10**9, bytes_accessed=1, transcendentals=0),
    )(marks, rows, grads, *expand, *shrink)


def on_device(
    direct,
    tokens,
    norm_first,
    joint_weight,
    output_weight,
    norm_second,
    expand_weight,
    shrink_weight,
    document_start,
    cotangent,
):
    rows, width = tokens.shape
    plan = Direct() if direct else Plain(rows)
    length = lax.axis_size("seq")
    here = lax.axis_index("seq")
    x, core = plan.x, plan.core
    near_x = x == 0
    depth = joint_weight.shape[0]
    unit_rows = shrink_weight.shape[0]
    unit_half = (unit_rows + 1) // 2
    units = -(-unit_half * length // LANES) * LANES
    while units % length:
        units += LANES
    unit_pad = units // length
    half_width = width // 2

    def mine(array, start):
        parts = [array[:, start + i * GROUP : start + (i + 1) * GROUP] for i in range(4)]
        low, high = pick(near_x, parts[0::2], parts[1::2])
        return jnp.where(core == 0, low, high)

    source = jnp.arange(GROUP)
    turn = (
        source[:, None]
        == ((source % LANES) // 32 * HEAD_DIM + source // LANES * 32 + source % 32)[None, :]
    ).astype(BF)
    gain_one = norm_first.astype(F32)[:, None]
    gain_two = norm_second.astype(F32)[:, None]
    joint_piece = jnp.concatenate(
        [
            (dot(mine(joint_weight, 0), turn) * gain_one).astype(BF),
            (dot(mine(joint_weight, width), turn) * gain_one).astype(BF),
            (mine(joint_weight, 2 * width).astype(F32) * gain_one).astype(BF),
            mine(output_weight, 0),
        ],
        axis=1,
    )
    slot = jnp.arange(units)
    inner = core * unit_half + slot % unit_pad
    fits = (slot % unit_pad < unit_half) & (inner < unit_rows)
    unit_of = jnp.where(fits, slot // unit_pad * unit_rows + inner, -2 * FF)
    spread_units = (jnp.arange(2 * FF)[:, None] == (unit_of + x * FF)[None, :]).astype(BF)
    expand_piece = (dot(expand_weight, spread_units) * gain_two).astype(BF)
    slot_row = jnp.arange(unit_pad)

    def picked(c):
        row = c * unit_half + slot_row
        row = jnp.where((slot_row < unit_half) & (row < unit_rows), row, -1)
        return (row[:, None] == jnp.arange(unit_rows)[None, :]).astype(BF)

    shrink_piece = dot(
        picked(core),
        jnp.where(near_x, shrink_weight[:, :half_width], shrink_weight[:, half_width:]),
    ).astype(BF)

    anchor = (lax.axis_index("rep") * length + here) * rows
    position = anchor + jnp.arange(rows, dtype=jnp.int32) - document_start
    marks = jnp.pad(
        jnp.stack([(position + 1) // 16, (position + 1) % 16], axis=1), ((0, 0), (0, LANES - 2))
    ).astype(BF)
    packed = jnp.concatenate([tokens, marks], axis=1)
    joint = Chain(plan, plan.gather(joint_piece, True))
    near_tokens = Chain(plan, plan.around(packed))
    joint.step(3)
    expand = Chain(plan, plan.gather(gate(expand_piece, *joint.operands), False))
    joint.step(2)
    blocks, offsets = near_tokens.end()
    expand.step(2)
    shrink = Chain(plan, plan.gather(gate(shrink_piece, *expand.operands), False))
    block_count = len(blocks)
    span = block_count * rows
    still = lambda i: (0, 0)
    moving = lambda i: (i, 0)
    (sent,) = call_kernel(
        prepare_kernel,
        [(plan.columns(width // depth), None, None)]
        + [(block, (rows, width + LANES), still) for block in blocks],
        [((span, width + LANES), BF, (span, width + LANES), still)],
        micros=2,
    )
    first = (sent, swap_core(sent))
    offset_rows = jnp.stack([jnp.int32(offset) for offset in offsets]) * rows
    index = (here * rows + offset_rows[:, None] + jnp.arange(rows)[None, :]).reshape(1, span)
    document_rows = []
    for rows_in in first:
        code = rows_in[:, width : width + 2].astype(F32).T
        code = code[:1] * 16.0 + code[1:]
        document_rows.append(jnp.where(code > 0, index.astype(F32) - (code - 1.0), FAR))
    document_row = jnp.stack(document_rows)
    document_column = jnp.concatenate([row[:, :rows] for row in document_rows], axis=1).T
    halves_of_head = HEAD_DIM // 2
    frequency = THETA ** (-(jnp.arange(halves_of_head, dtype=F32) * 2.0) / HEAD_DIM)
    frequency = jnp.tile(frequency, LANES // halves_of_head)[None, :]
    steps = jnp.arange(LANES, dtype=F32)[:, None]
    angle = jnp.concatenate([16.0 * steps * frequency, (steps - 1.0) * frequency], axis=0)
    tables = jnp.concatenate([jnp.cos(angle), jnp.sin(angle)], axis=1)
    cotangents = jnp.concatenate([cotangent, swap_core(cotangent)], axis=0)

    joint_near, joint_far = halves(plan.front, *joint.value)
    output_mine = jnp.concatenate([joint_near[:, 3 * GROUP :], joint_far[:, 3 * GROUP :]], axis=1)
    output_all = jnp.concatenate([output_mine, swap_core(output_mine)], axis=1)

    def turn_columns(array):
        parts = [array[:, i * GROUP : (i + 1) * GROUP] for i in range(4)]
        parts = pick(core == 0, parts, parts[2:] + parts[:2])
        left, right = pick(near_x, parts[:2], parts[1::-1]), pick(near_x, parts[2:], parts[:1:-1])
        return jnp.concatenate(left + right, axis=-1)

    wide = 3 * GROUP
    *mixed, cosine, sine = call_kernel(
        mix_kernel,
        [
            (first[0], (rows, width + LANES), lambda i: (jnp.minimum(i, block_count - 1), 0)),
            (first[1], (rows, width + LANES), lambda i: (jnp.maximum(i - block_count, 0), 0)),
            (joint_near, (width, wide), still),
            (joint_far, (width, wide), still),
            (tables, (2 * LANES, 2 * LANES), still),
        ],
        [((2 * span, wide), BF, (rows, wide), moving)] * 2
        + [((2 * rows, LANES), F32, (rows, LANES), lambda i: (i // block_count, 0))] * 2,
        2 * block_count,
        micros=7,
    )
    expand.step()
    shrink.step(2)
    column = lambda kind, every: (
        ((span, GROUP), lambda i: (i, kind))
        if every
        else ((rows, GROUP), lambda i: (i * block_count, kind))
    )
    wide_keys = [
        (array, *column(kind, kind > 0)) for array in mixed for kind in range(3)
    ]
    wide_queries = [
        (array, *column(kind, kind == 0)) for array in mixed for kind in range(3)
    ]
    documents = [
        (document_row, (1, 1, span), lambda i: (i, 0, 0)),
        (document_column, (rows, 1), moving),
    ]
    both = lambda w, kind: ((2 * rows, w), kind, (rows, w), moving)
    attended, attended_low, logs = call_kernel(
        attend_kernel,
        wide_keys + documents,
        [both(2 * GROUP, F32), both(2 * GROUP, BF), both(LANES, F32)],
        2,
        micros=5,
    )
    shrink.step()
    shrink.step()
    attended_there = swap_core(attended_low)
    attended_there = jnp.concatenate([attended_there[rows:], attended_there[:rows]], axis=0)
    attended_rows = plan.order(
        turn_columns(jnp.concatenate([attended_low, attended_there], axis=1)), depth
    )
    middle = tokens.astype(F32) + turn_columns(dot(attended_rows[:rows], output_all))
    second, second_scale = centre(middle)
    second_low = plan.order(second.astype(BF), depth)
    second_both = jnp.concatenate([second_low, swap_core(second_low)], axis=0)
    expand_both = expand.end()
    shrink_both = shrink.end()

    where = jnp.stack(
        [plan.front.astype(jnp.int32), x.astype(jnp.int32)]
        + [row.astype(jnp.int32) for row in plan.rows_of(unit_pad)]
    )
    active_low, lifted_grads, out, out_there, second_grad, second_there = hidden(
        where, second_both, cotangents, expand_both, shrink_both
    )
    expand = Chain(plan, plan.reduce(second_both, lifted_grads[0], lifted_grads[1], False))
    result = middle + out + swap_core(out_there).astype(F32)
    second_grad = second_grad + swap_core(second_there).astype(F32)
    middle_grad = cotangent.astype(F32) + centre_back(
        second, second_scale, plan.restore(second_grad, depth)
    )
    branch = middle_grad.astype(BF)
    branch_both = turn_columns(jnp.concatenate([branch, swap_core(branch)], axis=0))
    attended_grad = turn_columns(plan.restore(outer_rows(branch_both, output_all), depth))
    around, numbers = call_kernel(
        around_kernel,
        [
            (attended_grad[:, : 2 * GROUP], (rows, 2 * GROUP), moving),
            (attended, (rows, 2 * GROUP), moving),
            (logs, (rows, LANES), moving),
        ],
        [both(2 * GROUP + LANES, BF), both(LANES, F32)],
        2,
    )
    near_grads = Chain(plan, plan.around(around))
    branch_sides = jnp.stack(
        pick(near_x, *[[branch_both[:, i * GROUP : (i + 1) * GROUP] for i in o] for o in ((0, 1), (1, 0))])
    )
    kinds = [
        ((length, unit_pad + depth // 2, half_width), BF),
        (length, unit_pad + depth // 2, half_width),
        lambda i: (0, 0, 0),
    ]
    sums = call_kernel(
        pack_kernel,
        [
            (x.astype(jnp.int32)[None], None, 0),
            (active_low, (2 * rows, units), still),
            (cotangents, (2 * rows, width), still),
            (plan.restore(attended_rows, depth), (2 * rows, width), still),
            (branch_sides, (2, 2 * rows, GROUP), lambda i: (0, 0, 0)),
        ],
        [(*kinds[0], kinds[1], kinds[2])] * 2,
    )
    near_grads.step(2)
    shrink = Chain(plan, plan.reduce_blocks(*sums))
    turning = [(cosine, (rows, LANES), moving), (sine, (rows, LANES), moving)]
    (query_grad,) = call_kernel(
        query_kernel,
        wide_keys
        + [
            (around, (rows, 2 * GROUP), moving),
            (numbers, (rows, LANES), moving),
        ]
        + documents
        + turning,
        [both(2 * GROUP, BF)],
        2,
        micros=13,
    )
    expand.step()
    arounds, _ = near_grads.end()
    mixed_grads = call_kernel(
        key_kernel,
        wide_queries
        + [(query_grad, (rows, 2 * GROUP), moving)]
        + documents
        + turning
        + [(block, (rows, 2 * GROUP + LANES), moving) for block in arounds],
        [both(wide, BF), both(wide, BF)],
        2,
        micros=16,
    )
    own_first = jnp.concatenate([rows_in[:rows, :width] for rows_in in first], axis=0)
    joint = Chain(plan, plan.reduce(own_first, *mixed_grads, True))
    expand.step()
    shrink.step()
    joint.step()
    moved = joint.operands + expand.operands
    expand.hold(*moved)
    shrink.hold(*moved)
    first_part = outer_rows(mixed_grads[0], joint_near[:, :wide]) + outer_rows(
        mixed_grads[1], joint_far[:, :wide]
    )
    first_grad = first_part[:rows] + swap_core(first_part[rows:].astype(BF)).astype(F32)
    normal, normal_scale = centre(tokens.astype(F32))
    tokens_grad = middle_grad + centre_back(
        normal, normal_scale, plan.restore(first_grad, depth)
    )

    expand.step()
    shrink.step()
    joint.step()
    shrink.hold(*joint.operands)
    expand.step()
    expand.step()
    joint.step(3)
    shrink.step()
    expand_shares = expand.end()
    expand_raw = 0.0
    for c in (0, 1):
        inner = c * unit_half + slot % unit_pad
        fits = (slot % unit_pad < unit_half) & (inner < unit_rows)
        unit_at = jnp.where(fits, slot // unit_pad * unit_rows + inner, -1)
        back = (unit_at[:, None] == jnp.arange(FF)[None, :]).astype(BF)
        expand_raw = expand_raw + dot(jnp.concatenate(expand_shares[c], axis=0), back)
    expand_raw = jnp.concatenate([expand_raw[:depth], expand_raw[depth:]], axis=1)
    shrink.step()
    joint.step()
    shrink_shares = shrink.end()
    joint_four = joint.end()

    shrink_grad = jnp.concatenate(
        [
            inner_rows(picked(0), shrink_shares[0][i][:unit_pad])
            + inner_rows(picked(1), shrink_shares[1][i][:unit_pad])
            for i in (0, 1)
        ],
        axis=1,
    )
    expand_grad = expand_raw * gain_two
    second_gain_grad = jnp.sum(expand_raw * expand_weight.astype(F32), axis=1)
    output_grad = []
    for pair in shrink_shares:
        for share in pair:
            share = share[unit_pad:]
            output_grad.append(jnp.concatenate([share[:, :GROUP], share[:, GROUP:]], axis=0))
    output_grad = jnp.concatenate(output_grad, axis=1).astype(F32)
    columns = []
    for kind in range(3):
        for c in (0, 1):
            for i in (0, 1):
                piece = joint_four[c][i][:, kind * GROUP : (kind + 1) * GROUP]
                columns.append(outer_rows(piece, turn) if kind < 2 else piece.astype(F32))
    joint_raw = jnp.concatenate(columns, axis=1)
    joint_grad = joint_raw * gain_one
    first_gain_grad = jnp.sum(joint_raw * joint_weight.astype(F32), axis=1)
    return (
        result.astype(BF),
        tokens_grad.astype(BF),
        first_gain_grad,
        joint_grad,
        output_grad,
        second_gain_grad,
        expand_grad,
        shrink_grad,
    )


def solution(mesh):
    placed = (
        P(("rep", "seq"), None),
        P("seq"),
        P("seq", None),
        P("seq", None),
        P("seq"),
        P("seq", None),
        P("seq", None),
        P(("rep", "seq")),
        P(("rep", "seq"), None),
    )
    return jax.shard_map(
        functools.partial(on_device, mesh.shape["seq"] == 8),
        mesh=mesh,
        in_specs=placed,
        out_specs=(
            P(("rep", "seq"), None),
            P(("rep", "seq"), None),
            P("seq"),
            P("seq", None),
            P("seq", None),
            P("seq"),
            P("seq", None),
            P("seq", None),
        ),
        check_vma=False,
    )
```

```python
import functools

import jax
import jax.numpy as jnp
from jax import lax
from jax.experimental import pallas as pl
from jax.experimental.pallas import tpu as pltpu
from jax.sharding import PartitionSpec as P

HEADS = 16
HEAD_DIM = 64
FF = 2624
HALO = 512
EPSILON = 1e-05
THETA = 160000.0
SCALE = 0.125
LANES = 128
GROUP = 256
FAR = -1e6
LONG = 10**11
BF = jnp.bfloat16
F32 = jnp.float32


def dot(left, right):
    return jnp.dot(left, right, preferred_element_type=F32)


def inner_rows(left, right):
    return lax.dot_general(left, right, (((0,), (0,)), ((), ())), preferred_element_type=F32)


def outer_rows(left, right):
    return lax.dot_general(left, right, (((1,), (1,)), ((), ())), preferred_element_type=F32)


def pick(flag, one, two):
    return [jnp.where(flag, a, b) for a, b in zip(one, two)]


def centre(rows):
    middle = jnp.mean(rows, axis=-1, keepdims=True)
    centered = rows - middle
    spread = jnp.mean(centered * centered, axis=-1, keepdims=True)
    scale = lax.rsqrt(spread + EPSILON)
    return centered * scale, scale


def centre_back(normal, scale, grads):
    return scale * (
        grads
        - jnp.mean(grads, axis=-1, keepdims=True)
        - normal * jnp.mean(grads * normal, axis=-1, keepdims=True)
    )


def two_parts(values):
    high = lax.reduce_precision(values, 8, 7)
    return high.astype(BF), (values - high).astype(BF)


def swap_core(array):
    return lax.ppermute(array, "rep", [(i, i ^ 1) for i in range(lax.axis_size("rep"))])


def swap_far(array):
    return lax.ppermute(array, "rep", [(i, i ^ 2) for i in range(lax.axis_size("rep"))])


class Moves:
    def __init__(self):
        self.recent = []

    def send(self, array, axes, route):
        self.recent.append(array)
        return lax.ppermute(array, axes, route)

    def across(self, array, flip):
        return self.send(array, "rep", [(i, i ^ flip) for i in range(lax.axis_size("rep"))])

    def given(self):
        found, self.recent = self.recent, []
        return found


class Direct(Moves):
    depth = 4

    def __init__(self):
        super().__init__()
        self.place = lax.axis_index("seq")
        self.z = self.place // 2
        self.y = self.place % 2
        self.x = lax.axis_index("rep") // 2
        self.core = lax.axis_index("rep") % 2
        self.front = self.core == 0

    def along(self, array, flip):
        route = [(s, s ^ (2 * flip)) for s in range(2 * self.depth)]
        return self.send(array, "seq", route)

    def cross(self, array, turn):
        n = 2 * self.depth
        route = []
        for r in range(4):
            for s in range(n):
                to = (r ^ 2, s) if r % 2 == turn else (r, s ^ 1)
                route.append((r * n + s, to[0] * n + to[1]))
        return self.send(array, ("rep", "seq"), route)

    def around(self, array):
        rows = array.shape[0]
        last = 2 * self.depth
        low = self.send(array, "seq", [(s, s + 2) for s in range(last - 2)])
        high = self.send(array, "seq", [(s, s - 2) for s in range(2, last)])
        low = yield low
        high = yield high
        sent = jnp.concatenate([array, jnp.where(self.y == 0, high, low)], axis=0)
        beside = yield self.send(sent, "seq", [(s, s ^ 1) for s in range(last)])
        step = 1 - 2 * self.y
        return [array, low, high, beside[:rows], beside[rows:]], [0, -2, 2, step, -step]

    def gather(self, piece, at_once):
        if at_once:
            sent = [self.along(piece, k) for k in (1, 2, 3)]
            found = [piece]
            for array in sent:
                array = yield array
                found.append(array)
            rows = jnp.concatenate(found, axis=0)
        else:
            there = yield self.along(piece, 1)
            pair = jnp.concatenate([piece, there], axis=0)
            there = yield self.along(pair, 2)
            rows = jnp.concatenate([pair, there], axis=0)
        once = yield self.cross(rows, 0)
        pair = jnp.concatenate([rows, once], axis=0)
        other = yield self.cross(pair, 1)
        return pair, other

    def to_near(self, grid):
        turned = [pick(self.y == 0, pair, pair[::-1]) for pair in grid]
        near = []
        for y in (0, 1):
            a, b, c, d = [pair[y] for pair in turned]
            a, b, c, d = pick(self.z % 2 == 0, [a, b, c, d], [b, a, d, c])
            near.append(pick(self.z // 2 == 0, [a, b, c, d], [c, d, a, b]))
        return near

    def to_mesh(self, near):
        lines = []
        for a, b, c, d in near:
            a, b, c, d = pick(self.z % 2 == 0, [a, b, c, d], [b, a, d, c])
            lines.append(pick(self.z // 2 == 0, [a, b, c, d], [c, d, a, b]))
        return [pick(self.y == 0, list(pair), list(pair)[::-1]) for pair in zip(*lines)]

    def rows_of(self, size):
        return [
            (2 * (self.z ^ k) + (self.y ^ y)) * size for y in (0, 1) for k in range(self.depth)
        ]

    def columns(self, count):
        z, y = jnp.arange(count) // 2, jnp.arange(count) % 2
        return (4 * (y ^ self.y) + (z ^ self.z)).astype(jnp.int32)

    def order(self, array, size):
        n = self.depth
        cut = lambda s: array[..., s * size : (s + 1) * size]
        near = self.to_near([[cut(2 * z), cut(2 * z + 1)] for z in range(n)])
        return jnp.concatenate(near[0] + near[1], axis=-1)

    def restore(self, array, size):
        n = self.depth
        cut = lambda j: array[..., j * size : (j + 1) * size]
        grid = self.to_mesh([[cut(n * y + k) for k in range(n)] for y in (0, 1)])
        return jnp.concatenate([part for pair in grid for part in pair], axis=-1)

    def down(self, mine, at_once):
        rows = mine.shape[0] // 4
        cut = lambda k, n: mine[k * rows : (k + n) * rows]
        if at_once:
            sent = [self.along(cut(k, 1), k) for k in (1, 2, 3)]
            total = cut(0, 1).astype(F32)
            for array in sent:
                array = yield array
                total = total + array.astype(F32)
            share = total.astype(BF)
        else:
            there = yield self.along(cut(2, 2), 2)
            pair = (cut(0, 2).astype(F32) + there.astype(F32)).astype(BF)
            there = yield self.along(pair[rows:], 1)
            share = (pair[:rows].astype(F32) + there.astype(F32)).astype(BF)
        return (yield from self.spread(share))

    def reduce(self, left, near, far, at_once):
        half = left.shape[1] // 2
        top, bottom = left[:, :half], left[:, half:]
        sent = lax.dot_general(
            jnp.stack([jnp.where(self.front, bottom, top), bottom]),
            jnp.stack([jnp.where(self.front, near, far), far]),
            (((1,), (1,)), ((0,), (0,))),
            preferred_element_type=F32,
        ).astype(BF)
        back = yield self.cross(sent, 1)
        once = inner_rows(jnp.where(self.front, top, bottom), jnp.where(self.front, far, near))
        once_in = yield self.cross((once + back[1]).astype(BF), 0)
        mine = (inner_rows(top, near) + back[0] + once_in).astype(BF)
        return (yield from self.down(mine, at_once))

    def reduce_blocks(self, near, far):
        back = yield self.across(far, 2)
        total = (near.astype(F32) + back.astype(F32)).astype(BF)
        lines = self.to_near([total[2 * z : 2 * z + 2] for z in range(self.depth)])
        mine, sent = [jnp.concatenate(line, axis=0) for line in lines]
        route = [(s, s ^ 1) for s in range(2 * self.depth)]
        back = yield self.send(sent, "seq", route)
        mine = (mine.astype(F32) + back.astype(F32)).astype(BF)
        return (yield from self.down(mine, False))

    def spread(self, share):
        there = yield self.across(share, 2)
        pair = [share, there]
        low, high = pick(self.x == 0, pair, pair[::-1])
        both = jnp.concatenate([low, high], axis=1)
        there = yield self.across(both, 1)
        size = share.shape[1]
        cores = pick(self.core == 0, [both, there], [there, both])
        return [[part[:, :size], part[:, size:]] for part in cores]


class Plain(Moves):
    def __init__(self, rows):
        super().__init__()
        self.rows = rows
        self.x = lax.axis_index("rep") // 2
        self.core = lax.axis_index("rep") % 2
        self.front = jnp.bool_(True)

    def around(self, array):
        length = lax.axis_size("seq")
        reach = min(HALO // self.rows, length - 1)
        blocks, offsets = [array], [0]
        for offset in list(range(-reach, 0)) + list(range(1, reach + 1)):
            route = [(i + offset, i) for i in range(length) if 0 <= i + offset < length]
            blocks.append((yield self.send(array, "seq", route)))
            offsets.append(offset)
        return blocks, offsets

    def gather(self, piece, at_once):
        near = yield lax.all_gather(piece, "seq", axis=0, tiled=True)
        far = yield self.across(near, 2)
        half = near.shape[0] // 2
        return (
            jnp.concatenate([near[:half], far[:half]], axis=0),
            jnp.concatenate([near[half:], far[half:]], axis=0),
        )

    def rows_of(self, size):
        return [jnp.int32(0), jnp.int32(lax.axis_size("seq") // 2 * size)]

    def columns(self, count):
        return jnp.zeros((1,), jnp.int32)

    def order(self, array, size):
        return array

    def restore(self, array, size):
        return array

    def reduce(self, left, near, far, at_once=False):
        back = yield self.across(inner_rows(left, far).astype(BF), 2)
        mine = inner_rows(left, near) + back
        share = lax.psum_scatter(mine, "seq", scatter_dimension=0, tiled=True).astype(BF)
        return (yield from self.spread(share))

    def reduce_blocks(self, near, far):
        back = yield self.across(far, 2)
        mine = (near.astype(F32) + back).reshape(-1, near.shape[2])
        share = lax.psum_scatter(mine, "seq", scatter_dimension=0, tiled=True).astype(BF)
        return (yield from self.spread(share))

    spread = Direct.spread


def gate(array, *earlier):
    return lax.optimization_barrier((array,) + earlier)[0]


class Chain:
    def __init__(self, plan, steps):
        self.plan, self.steps = plan, steps
        self.value = None
        self.sent = next(steps)
        self.operands = tuple(plan.given())

    def hold(self, *earlier):
        if self.sent is not None:
            self.sent = gate(self.sent, *earlier)

    def step(self, count=1):
        for _ in range(count):
            if self.sent is not None:
                try:
                    self.sent = self.steps.send(self.sent)
                except StopIteration as end:
                    self.sent, self.value = None, end.value
                self.operands = tuple(self.plan.given())

    def end(self):
        while self.sent is not None:
            self.step()
        return self.value


def halves(front, pair, other):
    half = pair.shape[0] // 2
    one, two = pair[half:], other[:half]
    near = jnp.concatenate([pair[:half], jnp.where(front, two, one)], axis=0)
    far = jnp.concatenate([jnp.where(front, one, two), other[half:]], axis=0)
    return near, far


def lane_masks():
    lane = lax.broadcasted_iota(jnp.int32, (1, GROUP), 1)
    turned = [(lane % LANES) // (HEAD_DIM // 2) == i for i in range(4)]
    plain = [lane // HEAD_DIM == i for i in range(4)]
    return turned, plain


def only(mask, array):
    return jnp.where(mask, array, jnp.zeros_like(array))


def spin(raw, c, s, way):
    a, b = raw[:, :LANES], raw[:, LANES:]
    return a * c - way * (b * s), b * c + way * (a * s)


def prepare_kernel(places, *refs):
    *blocks, out = refs
    width = blocks[0].shape[1] - LANES
    rows = out.shape[0] // len(blocks)
    count = places.shape[0]
    size = width // count
    for i, block in enumerate(blocks):
        normal = centre(block[:, :width].astype(F32))[0].astype(BF)
        at = slice(i * rows, (i + 1) * rows)
        out[at, width:] = block[:, width:]
        for s in range(count):
            to = pl.multiple_of(places[s] * size, LANES)
            out[at, pl.ds(to, size)] = normal[:, s * size : (s + 1) * size]


def mix_kernel(ours, theirs, near, far, tables, near_out, far_out, cosine, sine):
    count = pl.num_programs(0) // 2
    step = pl.program_id(0)
    half = near.shape[0]
    rows = jnp.where(step < count, ours[...], theirs[...])
    marks = rows[:, half : half + LANES].astype(F32)
    lane = lax.broadcasted_iota(jnp.int32, (1, LANES), 1).astype(F32)
    exact = lambda flags, table: jnp.dot(
        flags.astype(F32), table, preferred_element_type=F32, precision=lax.Precision.HIGHEST
    )
    coarse = exact(marks[:, 0:1] == lane, tables[:LANES])
    fine = exact(marks[:, 1:2] == lane, tables[LANES:])
    c = coarse[:, :LANES] * fine[:, :LANES] - coarse[:, LANES:] * fine[:, LANES:]
    s = coarse[:, LANES:] * fine[:, :LANES] + coarse[:, :LANES] * fine[:, LANES:]
    for weight, out in ((near, near_out), (far, far_out)):
        raw = dot(rows[:, :half], weight[...])
        for kind, scale in ((0, SCALE), (1, 1.0)):
            at = kind * GROUP
            a, b = spin(raw[:, at : at + GROUP], c, s, 1.0)
            out[:, at : at + LANES] = (a * scale).astype(BF)
            out[:, at + LANES : at + GROUP] = (b * scale).astype(BF)
        out[:, 2 * GROUP :] = raw[:, 2 * GROUP :].astype(BF)

    @pl.when(step % count == 0)
    def _():
        cosine[...] = c
        sine[...] = s


def attend_kernel(q0, k0, v0, q1, k1, v1, doc_row, doc_column, attended, attended_low, logs):
    turned, plain = lane_masks()
    allowed = doc_column[...] == doc_row[0]
    lane = lax.broadcasted_iota(jnp.int32, (1, LANES), 1)
    totals = jnp.zeros((q0.shape[0], LANES), F32)
    for group, (q, k, v) in enumerate(((q0, k0, v0), (q1, k1, v1))):
        queries, keys, values = q[...], k[...], v[...]
        kept = jnp.zeros(queries.shape, F32)
        for i in range(4):
            raw = outer_rows(only(turned[i], queries), keys)
            raw = jnp.where(allowed, raw, -jnp.inf)
            top = jnp.max(raw, axis=-1, keepdims=True)
            weights = jnp.exp(raw - top)
            total = jnp.sum(weights, axis=-1, keepdims=True)
            found = dot(weights.astype(BF), values) / total
            kept = jnp.where(plain[i], found, kept)
            totals = jnp.where(lane == 4 * group + i, top + jnp.log(total), totals)
        attended[:, group * GROUP : (group + 1) * GROUP] = kept
        attended_low[:, group * GROUP : (group + 1) * GROUP] = kept.astype(BF)
    logs[...] = totals


def around_kernel(grads, attended, logs, around, numbers):
    heads = HEADS // 2
    width = grads.shape[1]
    row = lax.broadcasted_iota(jnp.int32, (width, LANES), 0)
    lane = lax.broadcasted_iota(jnp.int32, (width, LANES), 1)
    low = grads[...].astype(BF)
    delta = jnp.dot(
        low.astype(F32) * attended[...],
        (row // HEAD_DIM == lane - 2 * heads).astype(F32),
        preferred_element_type=F32,
        precision=lax.Precision.HIGHEST,
    )
    both = logs[...] + delta
    numbers[...] = both
    high = both.astype(BF).astype(F32)
    around[:, :width] = low
    around[:, width:] = (high + pltpu.roll(both - high, heads, 1)).astype(BF)


def query_kernel(q0, k0, v0, q1, k1, v1, around, numbers, doc_row, doc_column, cosine, sine, d_q):
    turned, plain = lane_masks()
    allowed = doc_column[...] == doc_row[0]
    c, s = cosine[...] * SCALE, sine[...] * SCALE
    for group, (q, k, v) in enumerate(((q0, k0, v0), (q1, k1, v1))):
        queries, keys, values = q[...], k[...], v[...]
        grads = around[:, group * GROUP : (group + 1) * GROUP]
        kept = jnp.zeros(queries.shape, F32)
        for i in range(4):
            at = 4 * group + i
            raw = outer_rows(only(turned[i], queries), keys)
            weights = jnp.where(allowed, jnp.exp(raw - numbers[:, at : at + 1]), 0.0)
            d_weights = outer_rows(only(plain[i], grads), values)
            d_raw = (weights * (d_weights - numbers[:, 16 + at : 17 + at])).astype(BF)
            kept = jnp.where(turned[i], dot(d_raw, keys), kept)
        a, b = spin(kept, c, s, -1.0)
        d_q[:, group * GROUP : group * GROUP + LANES] = a.astype(BF)
        d_q[:, group * GROUP + LANES : (group + 1) * GROUP] = b.astype(BF)


def key_kernel(q0, k0, v0, q1, k1, v1, d_q, doc_row, doc_column, cosine, sine, *refs):
    *around, near, far = refs
    turned, plain = lane_masks()
    rows = k0.shape[0]
    c, s = cosine[...], sine[...]
    column = doc_column[...]
    kept = [[jnp.zeros(k0.shape, F32), jnp.zeros(k0.shape, F32)] for _ in (0, 1)]
    for j, block in enumerate(around):
        part = slice(j * rows, (j + 1) * rows)
        allowed = column == doc_row[0, :, part]
        numbers = block[:, 2 * GROUP :].astype(F32)
        numbers = (numbers + pltpu.roll(numbers, LANES - HEADS // 2, 1)).T
        for group, (q, k, v) in enumerate(((q0, k0, v0), (q1, k1, v1))):
            queries, keys, values = q[part, :], k[...], v[...]
            grads = block[:, group * GROUP : (group + 1) * GROUP]
            add_k = jnp.zeros(k0.shape, F32)
            add_v = jnp.zeros(k0.shape, F32)
            for i in range(4):
                at = 4 * group + i
                raw = outer_rows(only(turned[i], keys), queries)
                weights = jnp.where(allowed, jnp.exp(raw - numbers[at : at + 1, :]), 0.0)
                add_v = jnp.where(plain[i], dot(weights.astype(BF), grads), add_v)
                d_weights = outer_rows(only(plain[i], values), grads)
                d_raw = (weights * (d_weights - numbers[16 + at : 17 + at, :])).astype(BF)
                add_k = jnp.where(turned[i], dot(d_raw, queries), add_k)
            kept[group][0] += add_k
            kept[group][1] += add_v
    for group, out in enumerate((near, far)):
        a, b = spin(kept[group][0], c, s, -1.0)
        out[:, :GROUP] = d_q[:, group * GROUP : (group + 1) * GROUP]
        out[:, GROUP : GROUP + LANES] = a.astype(BF)
        out[:, GROUP + LANES : 2 * GROUP] = b.astype(BF)
        out[:, 2 * GROUP :] = kept[group][1].astype(BF)


def pack_kernel(place, active, grads, attended, branch, near, far):
    count, depth = near.shape[0], attended.shape[1] // near.shape[0]
    rows = active.shape[1] // count
    wide = near.shape[2]
    for i in (0, 1):
        one = inner_rows(active[...], grads[:, i * wide : (i + 1) * wide]).astype(BF)
        two = inner_rows(attended[...], branch[i]).astype(BF)

        def store(out):
            for s in range(count):
                out[s, :rows] = one[s * rows : (s + 1) * rows]
                at = s * depth
                out[s, rows:, :GROUP] = two[at : at + depth // 2]
                out[s, rows:, GROUP:] = two[at + depth // 2 : at + depth]

        @pl.when(place[0] == i)
        def _():
            store(near)

        @pl.when(place[0] != i)
        def _():
            store(far)


def place_kernel(rest, one_low, one_high, two_low, two_high, weight, gain, grads, gains):
    length, half, rows, pad = rest
    full = weight.shape[1] // 2
    for i, pair in enumerate(((one_low, two_low), (one_high, two_high))):
        for s in range(length):
            for c, share in enumerate(pair):
                size = min(half, rows - c * half)
                at = i * full + s * rows + c * half
                grads[:, at : at + size] = share[:, s * pad : s * pad + size].astype(F32)
    raw = grads[...]
    total = jnp.sum(raw * weight[...].astype(F32), axis=1, keepdims=True)
    gains[...] = jnp.broadcast_to(total, gains.shape)
    grads[...] = raw * gain[...]


def call_kernel(kernel, ins, outs, grid=1, room=56, micros=5):
    spec = lambda block, at: (
        pl.BlockSpec(memory_space=pltpu.SMEM) if block is None else pl.BlockSpec(block, at)
    )
    return pl.pallas_call(
        kernel,
        grid=(grid,),
        in_specs=[spec(block, at) for _, block, at in ins],
        out_specs=tuple(pl.BlockSpec(block, at) for _, _, block, at in outs),
        out_shape=tuple(jax.ShapeDtypeStruct(shape, kind) for shape, kind, _, _ in outs),
        compiler_params=pltpu.CompilerParams(vmem_limit_bytes=room * 2**20),
        cost_estimate=pl.CostEstimate(flops=micros * 10**9, bytes_accessed=1, transcendentals=0),
    )(*[a for a, _, _ in ins])


def gelu_parts(inner):
    share = 0.5 * (1.0 + lax.erf(inner * 0.7071067811865476))
    return inner * share, share + inner * (0.3989422804014327 * jnp.exp(-0.5 * inner * inner))


def hidden_kernel(marks, rows, grads, pair, other, shrink_pair, shrink_other, *refs):
    active, lifted_grads, out, out_there, d_rows, d_there = refs[:6]
    expand_w, shrink_w, semaphore = refs[6:]
    units = shrink_w.shape[0]
    half = pair.shape[0] // 2
    wide = shrink_pair.shape[1]
    places = marks.shape[0] - 2
    block = units // places
    front = marks[0] == 1
    x = marks[1]
    step = pl.program_id(0)

    def weights(source, start, at, row):
        return source.at[pl.ds(start, half)], expand_w.at[at, pl.ds(row, half)]

    def shrinks(source, high, at, low):
        found = []
        for j in range(places // 2):
            start = high * (source.shape[0] // 2) + j * block
            row = pl.multiple_of(marks[2 + low * (places // 2) + j], 16)
            column = pl.multiple_of(at * wide, LANES)
            found.append(
                (
                    source.at[pl.ds(start, block)],
                    shrink_w.at[pl.ds(row, block), pl.ds(column, wide)],
                )
            )
        return found

    def begin(moves, first):
        copies = [
            pltpu.make_async_copy(a, b, semaphore.at[first + k]) for k, (a, b) in enumerate(moves)
        ]
        for copy in copies:
            copy.start()
        return copies

    @pl.when(step == 0)
    def _():
        moves = [weights(pair, 0, x, 0), weights(other, half, 1 - x, half)]
        moves += shrinks(shrink_pair, 0, x, 0) + shrinks(shrink_other, 1, 1 - x, 1)
        copies = begin(moves, 0)
        for flag, low, high in ((front, other, pair), (jnp.logical_not(front), pair, other)):

            @pl.when(flag)
            def _():
                start = 0 if low is other else half
                back = half - start
                shrink_low = shrink_other if low is other else shrink_pair
                shrink_high = shrink_pair if low is other else shrink_other
                crossed = [weights(low, start, x, half), weights(high, back, 1 - x, 0)]
                crossed += shrinks(shrink_low, start // half, x, 1)
                crossed += shrinks(shrink_high, back // half, 1 - x, 0)
                for copy in begin(crossed, len(moves)):
                    copy.wait()

        for copy in copies:
            copy.wait()

    values, dy = rows[...], grads[...]
    tile = 256
    for at in range(0, units, tile):
        cut = slice(at, min(at + tile, units))
        inner = dot(values, expand_w[0, :, cut])
        gate = dot(values, expand_w[1, :, cut])
        d_active = outer_rows(dy, shrink_w[cut, :])
        value, slope = gelu_parts(inner)
        active[:, cut] = (value * gate).astype(BF)
        lifted_grads[x, :, cut] = (d_active * gate * slope).astype(BF)
        lifted_grads[1 - x, :, cut] = (d_active * value).astype(BF)
    result = dot(active[...], shrink_w[...])
    back = outer_rows(lifted_grads[x], expand_w[0]) + outer_rows(lifted_grads[1 - x], expand_w[1])

    @pl.when(step == 0)
    def _():
        out[...] = result
        d_rows[...] = back

    @pl.when(step == 1)
    def _():
        out_there[...] = result.astype(BF)
        d_there[...] = back.astype(BF)


def hidden(marks, rows, grads, expand, shrink):
    count, width = rows.shape
    units = expand[0].shape[1]
    size = count // 2
    moving = lambda i: (i, 0)
    still = lambda i: (0, 0)
    held = pl.BlockSpec(memory_space=pl.ANY)
    outs = [
        ((count, units), BF, (size, units), moving),
        ((2, count, units), BF, (2, size, units), lambda i: (0, i, 0)),
        ((size, width), F32, (size, width), still),
        ((size, width), BF, (size, width), still),
        ((size, width), F32, (size, width), still),
        ((size, width), BF, (size, width), still),
    ]
    return pl.pallas_call(
        hidden_kernel,
        grid=(2,),
        in_specs=[pl.BlockSpec(memory_space=pltpu.SMEM)]
        + [pl.BlockSpec((size, width), moving)] * 2
        + [held] * 4,
        out_specs=tuple(pl.BlockSpec(block, at) for _, _, block, at in outs),
        out_shape=tuple(jax.ShapeDtypeStruct(shape, kind) for shape, kind, _, _ in outs),
        scratch_shapes=[
            pltpu.VMEM((2, width, units), BF),
            pltpu.VMEM((units, width), BF),
            pltpu.SemaphoreType.DMA((2 * marks.shape[0],)),
        ],
        compiler_params=pltpu.CompilerParams(vmem_limit_bytes=36 * 2**20),
        cost_estimate=pl.CostEstimate(flops=8 * 10**9, bytes_accessed=1, transcendentals=0),
    )(marks, rows, grads, *expand, *shrink)


def on_device(
    direct,
    tokens,
    norm_first,
    joint_weight,
    output_weight,
    norm_second,
    expand_weight,
    shrink_weight,
    document_start,
    cotangent,
):
    rows, width = tokens.shape
    plan = Direct() if direct else Plain(rows)
    length = lax.axis_size("seq")
    here = lax.axis_index("seq")
    x, core = plan.x, plan.core
    near_x = x == 0
    depth = joint_weight.shape[0]
    unit_rows = shrink_weight.shape[0]
    unit_half = (unit_rows + 1) // 2
    units = -(-unit_half * length // LANES) * LANES
    while units % length:
        units += LANES
    unit_pad = units // length
    half_width = width // 2

    def mine(array, start):
        parts = [array[:, start + i * GROUP : start + (i + 1) * GROUP] for i in range(4)]
        low, high = pick(near_x, parts[0::2], parts[1::2])
        return jnp.where(core == 0, low, high)

    source = jnp.arange(GROUP)
    turn = (
        source[:, None]
        == ((source % LANES) // 32 * HEAD_DIM + source // LANES * 32 + source % 32)[None, :]
    ).astype(BF)
    gain_one = norm_first.astype(F32)[:, None]
    gain_two = norm_second.astype(F32)[:, None]
    joint_piece = jnp.concatenate(
        [
            (dot(mine(joint_weight, 0), turn) * gain_one).astype(BF),
            (dot(mine(joint_weight, width), turn) * gain_one).astype(BF),
            (mine(joint_weight, 2 * width).astype(F32) * gain_one).astype(BF),
            mine(output_weight, 0),
        ],
        axis=1,
    )
    slot = jnp.arange(units)
    inner = core * unit_half + slot % unit_pad
    fits = (slot % unit_pad < unit_half) & (inner < unit_rows)
    unit_of = jnp.where(fits, slot // unit_pad * unit_rows + inner, -2 * FF)
    spread_units = (jnp.arange(2 * FF)[:, None] == (unit_of + x * FF)[None, :]).astype(BF)
    expand_piece = (dot(expand_weight, spread_units) * gain_two).astype(BF)
    slot_row = jnp.arange(unit_pad)

    def picked(c):
        row = c * unit_half + slot_row
        row = jnp.where((slot_row < unit_half) & (row < unit_rows), row, -1)
        return (row[:, None] == jnp.arange(unit_rows)[None, :]).astype(BF)

    shrink_piece = dot(
        picked(core),
        jnp.where(near_x, shrink_weight[:, :half_width], shrink_weight[:, half_width:]),
    ).astype(BF)

    anchor = (lax.axis_index("rep") * length + here) * rows
    position = anchor + jnp.arange(rows, dtype=jnp.int32) - document_start
    marks = jnp.pad(
        jnp.stack([(position + 1) // 16, (position + 1) % 16], axis=1), ((0, 0), (0, LANES - 2))
    ).astype(BF)
    packed = jnp.concatenate([tokens, marks], axis=1)
    joint = Chain(plan, plan.gather(joint_piece, True))
    near_tokens = Chain(plan, plan.around(packed))
    joint.step(3)
    expand = Chain(plan, plan.gather(gate(expand_piece, *joint.operands), False))
    joint.step(2)
    blocks, offsets = near_tokens.end()
    expand.step(2)
    shrink = Chain(plan, plan.gather(gate(shrink_piece, *expand.operands), False))
    block_count = len(blocks)
    span = block_count * rows
    still = lambda i: (0, 0)
    moving = lambda i: (i, 0)
    (sent,) = call_kernel(
        prepare_kernel,
        [(plan.columns(width // depth), None, None)]
        + [(block, (rows, width + LANES), still) for block in blocks],
        [((span, width + LANES), BF, (span, width + LANES), still)],
        micros=2,
    )
    first = (sent, swap_core(sent))
    offset_rows = jnp.stack([jnp.int32(offset) for offset in offsets]) * rows
    index = (here * rows + offset_rows[:, None] + jnp.arange(rows)[None, :]).reshape(1, span)
    document_rows = []
    for rows_in in first:
        code = rows_in[:, width : width + 2].astype(F32).T
        code = code[:1] * 16.0 + code[1:]
        document_rows.append(jnp.where(code > 0, index.astype(F32) - (code - 1.0), FAR))
    document_row = jnp.stack(document_rows)
    document_column = jnp.concatenate([row[:, :rows] for row in document_rows], axis=1).T
    halves_of_head = HEAD_DIM // 2
    frequency = THETA ** (-(jnp.arange(halves_of_head, dtype=F32) * 2.0) / HEAD_DIM)
    frequency = jnp.tile(frequency, LANES // halves_of_head)[None, :]
    steps = jnp.arange(LANES, dtype=F32)[:, None]
    angle = jnp.concatenate([16.0 * steps * frequency, (steps - 1.0) * frequency], axis=0)
    tables = jnp.concatenate([jnp.cos(angle), jnp.sin(angle)], axis=1)
    cotangents = jnp.concatenate([cotangent, swap_core(cotangent)], axis=0)

    joint_near, joint_far = halves(plan.front, *joint.value)
    output_mine = jnp.concatenate([joint_near[:, 3 * GROUP :], joint_far[:, 3 * GROUP :]], axis=1)
    output_all = jnp.concatenate([output_mine, swap_core(output_mine)], axis=1)

    def turn_columns(array):
        parts = [array[:, i * GROUP : (i + 1) * GROUP] for i in range(4)]
        parts = pick(core == 0, parts, parts[2:] + parts[:2])
        left, right = pick(near_x, parts[:2], parts[1::-1]), pick(near_x, parts[2:], parts[:1:-1])
        return jnp.concatenate(left + right, axis=-1)

    wide = 3 * GROUP
    *mixed, cosine, sine = call_kernel(
        mix_kernel,
        [
            (first[0], (rows, width + LANES), lambda i: (jnp.minimum(i, block_count - 1), 0)),
            (first[1], (rows, width + LANES), lambda i: (jnp.maximum(i - block_count, 0), 0)),
            (joint_near, (width, wide), still),
            (joint_far, (width, wide), still),
            (tables, (2 * LANES, 2 * LANES), still),
        ],
        [((2 * span, wide), BF, (rows, wide), moving)] * 2
        + [((2 * rows, LANES), F32, (rows, LANES), lambda i: (i // block_count, 0))] * 2,
        2 * block_count,
        micros=7,
    )
    expand.step()
    shrink.step(2)
    document_row = gate(document_row, *expand.operands)
    column = lambda kind, every: (
        ((span, GROUP), lambda i: (i, kind))
        if every
        else ((rows, GROUP), lambda i: (i * block_count, kind))
    )
    wide_keys = [
        (array, *column(kind, kind > 0)) for array in mixed for kind in range(3)
    ]
    wide_queries = [
        (array, *column(kind, kind == 0)) for array in mixed for kind in range(3)
    ]
    documents = [
        (document_row, (1, 1, span), lambda i: (i, 0, 0)),
        (document_column, (rows, 1), moving),
    ]
    both = lambda w, kind: ((2 * rows, w), kind, (rows, w), moving)
    attended, attended_low, logs = call_kernel(
        attend_kernel,
        wide_keys + documents,
        [both(2 * GROUP, F32), both(2 * GROUP, BF), both(LANES, F32)],
        2,
        micros=5,
    )
    shrink.step()
    shrink.step()
    expand_both = expand.end()
    attended_there = gate(swap_core(attended_low), *expand_both)
    attended_there = jnp.concatenate([attended_there[rows:], attended_there[:rows]], axis=0)
    attended_rows = plan.order(
        turn_columns(jnp.concatenate([attended_low, attended_there], axis=1)), depth
    )
    middle = tokens.astype(F32) + turn_columns(dot(attended_rows[:rows], output_all))
    second, second_scale = centre(middle)
    second_low = plan.order(second.astype(BF), depth)
    second_both = jnp.concatenate([second_low, swap_core(second_low)], axis=0)
    shrink_both = shrink.end()

    where = jnp.stack(
        [plan.front.astype(jnp.int32), x.astype(jnp.int32)]
        + [row.astype(jnp.int32) for row in plan.rows_of(unit_pad)]
    )
    active_low, lifted_grads, out, out_there, second_grad, second_there = hidden(
        where, second_both, cotangents, expand_both, shrink_both
    )
    expand = Chain(plan, plan.reduce(second_both, lifted_grads[0], lifted_grads[1], False))
    result = middle + out + swap_core(out_there).astype(F32)
    second_grad = second_grad + swap_core(second_there).astype(F32)
    middle_grad = cotangent.astype(F32) + centre_back(
        second, second_scale, plan.restore(second_grad, depth)
    )
    branch = middle_grad.astype(BF)
    branch_both = turn_columns(jnp.concatenate([branch, swap_core(branch)], axis=0))
    attended_grad = turn_columns(plan.restore(outer_rows(branch_both, output_all), depth))
    around, numbers = call_kernel(
        around_kernel,
        [
            (attended_grad[:, : 2 * GROUP], (rows, 2 * GROUP), moving),
            (attended, (rows, 2 * GROUP), moving),
            (logs, (rows, LANES), moving),
        ],
        [both(2 * GROUP + LANES, BF), both(LANES, F32)],
        2,
    )
    near_grads = Chain(plan, plan.around(around))
    branch_sides = jnp.stack(
        pick(near_x, *[[branch_both[:, i * GROUP : (i + 1) * GROUP] for i in o] for o in ((0, 1), (1, 0))])
    )
    kinds = [
        ((length, unit_pad + depth // 2, half_width), BF),
        (length, unit_pad + depth // 2, half_width),
        lambda i: (0, 0, 0),
    ]
    sums = call_kernel(
        pack_kernel,
        [
            (x.astype(jnp.int32)[None], None, 0),
            (active_low, (2 * rows, units), still),
            (cotangents, (2 * rows, width), still),
            (plan.restore(attended_rows, depth), (2 * rows, width), still),
            (branch_sides, (2, 2 * rows, GROUP), lambda i: (0, 0, 0)),
        ],
        [(*kinds[0], kinds[1], kinds[2])] * 2,
    )
    near_grads.step(2)
    shrink = Chain(plan, plan.reduce_blocks(*sums))
    turning = [(cosine, (rows, LANES), moving), (sine, (rows, LANES), moving)]
    (query_grad,) = call_kernel(
        query_kernel,
        wide_keys
        + [
            (around, (rows, 2 * GROUP), moving),
            (numbers, (rows, LANES), moving),
        ]
        + documents
        + turning,
        [both(2 * GROUP, BF)],
        2,
        micros=13,
    )
    expand.step()
    arounds, _ = near_grads.end()
    mixed_grads = call_kernel(
        key_kernel,
        wide_queries
        + [(query_grad, (rows, 2 * GROUP), moving)]
        + documents
        + turning
        + [(block, (rows, 2 * GROUP + LANES), moving) for block in arounds],
        [both(wide, BF), both(wide, BF)],
        2,
        micros=16,
    )
    own_first = jnp.concatenate([rows_in[:rows, :width] for rows_in in first], axis=0)
    joint = Chain(plan, plan.reduce(own_first, *mixed_grads, True))
    expand.step()
    shrink.step()
    joint.step()
    moved = joint.operands + expand.operands
    expand.hold(*moved)
    shrink.hold(*moved)
    first_part = outer_rows(mixed_grads[0], joint_near[:, :wide]) + outer_rows(
        mixed_grads[1], joint_far[:, :wide]
    )
    first_grad = first_part[:rows] + swap_core(first_part[rows:].astype(BF)).astype(F32)
    normal, normal_scale = centre(tokens.astype(F32))
    tokens_grad = middle_grad + centre_back(
        normal, normal_scale, plan.restore(first_grad, depth)
    )

    expand.step()
    shrink.hold(*expand.operands)
    shrink.step()
    joint.step()
    waits = joint.operands
    expand.step()
    shrink.hold(*waits, *expand.operands)
    expand.step()
    joint.step(3)
    shrink.step()
    expand_shares = expand.end()
    share_parts = [share for pair in expand_shares for share in pair]
    expand_grad, second_gains = call_kernel(
        functools.partial(place_kernel, (length, unit_half, unit_rows, unit_pad)),
        [(part, (depth, units), still) for part in share_parts]
        + [(expand_weight, (depth, 2 * FF), still), (gain_two, (depth, 1), still)],
        [
            ((depth, 2 * FF), F32, (depth, 2 * FF), still),
            ((depth, LANES), F32, (depth, LANES), still),
        ],
        micros=3,
    )
    second_gain_grad = second_gains[:, 0]
    shrink.step()
    joint.step()
    shrink_shares = shrink.end()
    joint_four = joint.end()

    shrink_grad = jnp.concatenate(
        [
            inner_rows(picked(0), shrink_shares[0][i][:unit_pad])
            + inner_rows(picked(1), shrink_shares[1][i][:unit_pad])
            for i in (0, 1)
        ],
        axis=1,
    )
    output_grad = []
    for pair in shrink_shares:
        for share in pair:
            share = share[unit_pad:]
            output_grad.append(jnp.concatenate([share[:, :GROUP], share[:, GROUP:]], axis=0))
    output_grad = jnp.concatenate(output_grad, axis=1).astype(F32)
    columns = []
    for kind in range(3):
        for c in (0, 1):
            for i in (0, 1):
                piece = joint_four[c][i][:, kind * GROUP : (kind + 1) * GROUP]
                columns.append(outer_rows(piece, turn) if kind < 2 else piece.astype(F32))
    joint_raw = jnp.concatenate(columns, axis=1)
    joint_grad = joint_raw * gain_one
    first_gain_grad = jnp.sum(joint_raw * joint_weight.astype(F32), axis=1)
    return (
        result.astype(BF),
        tokens_grad.astype(BF),
        first_gain_grad,
        joint_grad,
        output_grad,
        second_gain_grad,
        expand_grad,
        shrink_grad,
    )


def solution(mesh):
    placed = (
        P(("rep", "seq"), None),
        P("seq"),
        P("seq", None),
        P("seq", None),
        P("seq"),
        P("seq", None),
        P("seq", None),
        P(("rep", "seq")),
        P(("rep", "seq"), None),
    )
    return jax.shard_map(
        functools.partial(on_device, mesh.shape["seq"] == 8),
        mesh=mesh,
        in_specs=placed,
        out_specs=(
            P(("rep", "seq"), None),
            P(("rep", "seq"), None),
            P("seq"),
            P("seq", None),
            P("seq", None),
            P("seq"),
            P("seq", None),
            P("seq", None),
        ),
        check_vma=False,
    )
```

```python
import functools

import jax
import jax.numpy as jnp
from jax import lax
from jax.experimental import pallas as pl
from jax.experimental.pallas import tpu as pltpu
from jax.sharding import PartitionSpec as P

HEADS = 16
HEAD_DIM = 64
FF = 2624
HALO = 512
EPSILON = 1e-05
THETA = 160000.0
SCALE = 0.125
LANES = 128
GROUP = 256
FAR = -1e6
LONG = 10**11
BF = jnp.bfloat16
F32 = jnp.float32


def dot(left, right):
    return jnp.dot(left, right, preferred_element_type=F32)


def inner_rows(left, right):
    return lax.dot_general(left, right, (((0,), (0,)), ((), ())), preferred_element_type=F32)


def outer_rows(left, right):
    return lax.dot_general(left, right, (((1,), (1,)), ((), ())), preferred_element_type=F32)


def pick(flag, one, two):
    return [jnp.where(flag, a, b) for a, b in zip(one, two)]


def centre(rows):
    middle = jnp.mean(rows, axis=-1, keepdims=True)
    centered = rows - middle
    spread = jnp.mean(centered * centered, axis=-1, keepdims=True)
    scale = lax.rsqrt(spread + EPSILON)
    return centered * scale, scale


def centre_back(normal, scale, grads):
    return scale * (
        grads
        - jnp.mean(grads, axis=-1, keepdims=True)
        - normal * jnp.mean(grads * normal, axis=-1, keepdims=True)
    )


def two_parts(values):
    high = lax.reduce_precision(values, 8, 7)
    return high.astype(BF), (values - high).astype(BF)


def swap_core(array):
    return lax.ppermute(array, "rep", [(i, i ^ 1) for i in range(lax.axis_size("rep"))])


def swap_far(array):
    return lax.ppermute(array, "rep", [(i, i ^ 2) for i in range(lax.axis_size("rep"))])


class Moves:
    def __init__(self):
        self.recent = []

    def send(self, array, axes, route):
        self.recent.append(array)
        return lax.ppermute(array, axes, route)

    def across(self, array, flip):
        return self.send(array, "rep", [(i, i ^ flip) for i in range(lax.axis_size("rep"))])

    def given(self):
        found, self.recent = self.recent, []
        return found


class Direct(Moves):
    depth = 4

    def __init__(self):
        super().__init__()
        self.place = lax.axis_index("seq")
        self.z = self.place // 2
        self.y = self.place % 2
        self.x = lax.axis_index("rep") // 2
        self.core = lax.axis_index("rep") % 2
        self.front = self.core == 0

    def along(self, array, flip):
        route = [(s, s ^ (2 * flip)) for s in range(2 * self.depth)]
        return self.send(array, "seq", route)

    def cross(self, array, turn):
        n = 2 * self.depth
        route = []
        for r in range(4):
            for s in range(n):
                to = (r ^ 2, s) if r % 2 == turn else (r, s ^ 1)
                route.append((r * n + s, to[0] * n + to[1]))
        return self.send(array, ("rep", "seq"), route)

    def around(self, array):
        rows = array.shape[0]
        last = 2 * self.depth
        low = self.send(array, "seq", [(s, s + 2) for s in range(last - 2)])
        high = self.send(array, "seq", [(s, s - 2) for s in range(2, last)])
        low = yield low
        high = yield high
        sent = jnp.concatenate([array, jnp.where(self.y == 0, high, low)], axis=0)
        beside = yield self.send(sent, "seq", [(s, s ^ 1) for s in range(last)])
        step = 1 - 2 * self.y
        return [array, low, high, beside[:rows], beside[rows:]], [0, -2, 2, step, -step]

    def gather(self, piece, at_once):
        if at_once:
            sent = [self.along(piece, k) for k in (1, 2, 3)]
            found = [piece]
            for array in sent:
                array = yield array
                found.append(array)
            rows = jnp.concatenate(found, axis=0)
        else:
            there = yield self.along(piece, 1)
            pair = jnp.concatenate([piece, there], axis=0)
            there = yield self.along(pair, 2)
            rows = jnp.concatenate([pair, there], axis=0)
        once = yield self.cross(rows, 0)
        pair = jnp.concatenate([rows, once], axis=0)
        other = yield self.cross(pair, 1)
        return pair, other

    def to_near(self, grid):
        turned = [pick(self.y == 0, pair, pair[::-1]) for pair in grid]
        near = []
        for y in (0, 1):
            a, b, c, d = [pair[y] for pair in turned]
            a, b, c, d = pick(self.z % 2 == 0, [a, b, c, d], [b, a, d, c])
            near.append(pick(self.z // 2 == 0, [a, b, c, d], [c, d, a, b]))
        return near

    def to_mesh(self, near):
        lines = []
        for a, b, c, d in near:
            a, b, c, d = pick(self.z % 2 == 0, [a, b, c, d], [b, a, d, c])
            lines.append(pick(self.z // 2 == 0, [a, b, c, d], [c, d, a, b]))
        return [pick(self.y == 0, list(pair), list(pair)[::-1]) for pair in zip(*lines)]

    def rows_of(self, size):
        return [
            (2 * (self.z ^ k) + (self.y ^ y)) * size for y in (0, 1) for k in range(self.depth)
        ]

    def columns(self, count):
        z, y = jnp.arange(count) // 2, jnp.arange(count) % 2
        return (4 * (y ^ self.y) + (z ^ self.z)).astype(jnp.int32)

    def order(self, array, size):
        n = self.depth
        cut = lambda s: array[..., s * size : (s + 1) * size]
        near = self.to_near([[cut(2 * z), cut(2 * z + 1)] for z in range(n)])
        return jnp.concatenate(near[0] + near[1], axis=-1)

    def restore(self, array, size):
        n = self.depth
        cut = lambda j: array[..., j * size : (j + 1) * size]
        grid = self.to_mesh([[cut(n * y + k) for k in range(n)] for y in (0, 1)])
        return jnp.concatenate([part for pair in grid for part in pair], axis=-1)

    def down(self, mine, at_once):
        rows = mine.shape[0] // 4
        cut = lambda k, n: mine[k * rows : (k + n) * rows]
        if at_once:
            sent = [self.along(cut(k, 1), k) for k in (1, 2, 3)]
            total = cut(0, 1).astype(F32)
            for array in sent:
                array = yield array
                total = total + array.astype(F32)
            share = total.astype(BF)
        else:
            there = yield self.along(cut(2, 2), 2)
            pair = (cut(0, 2).astype(F32) + there.astype(F32)).astype(BF)
            there = yield self.along(pair[rows:], 1)
            share = (pair[:rows].astype(F32) + there.astype(F32)).astype(BF)
        return (yield from self.spread(share))

    def reduce(self, left, near, far, at_once):
        half = left.shape[1] // 2
        top, bottom = left[:, :half], left[:, half:]
        sent = lax.dot_general(
            jnp.stack([jnp.where(self.front, bottom, top), bottom]),
            jnp.stack([jnp.where(self.front, near, far), far]),
            (((1,), (1,)), ((0,), (0,))),
            preferred_element_type=F32,
        ).astype(BF)
        back = yield self.cross(sent, 1)
        once = inner_rows(jnp.where(self.front, top, bottom), jnp.where(self.front, far, near))
        once_in = yield self.cross((once + back[1]).astype(BF), 0)
        mine = (inner_rows(top, near) + back[0] + once_in).astype(BF)
        return (yield from self.down(mine, at_once))

    def reduce_blocks(self, near, far):
        back = yield self.across(far, 2)
        total = (near.astype(F32) + back.astype(F32)).astype(BF)
        lines = self.to_near([total[2 * z : 2 * z + 2] for z in range(self.depth)])
        mine, sent = [jnp.concatenate(line, axis=0) for line in lines]
        route = [(s, s ^ 1) for s in range(2 * self.depth)]
        back = yield self.send(sent, "seq", route)
        mine = (mine.astype(F32) + back.astype(F32)).astype(BF)
        return (yield from self.down(mine, False))

    def spread(self, share):
        there = yield self.across(share, 2)
        pair = [share, there]
        low, high = pick(self.x == 0, pair, pair[::-1])
        both = jnp.concatenate([low, high], axis=1)
        there = yield self.across(both, 1)
        size = share.shape[1]
        cores = pick(self.core == 0, [both, there], [there, both])
        return [[part[:, :size], part[:, size:]] for part in cores]


class Plain(Moves):
    def __init__(self, rows):
        super().__init__()
        self.rows = rows
        self.x = lax.axis_index("rep") // 2
        self.core = lax.axis_index("rep") % 2
        self.front = jnp.bool_(True)

    def around(self, array):
        length = lax.axis_size("seq")
        reach = min(HALO // self.rows, length - 1)
        blocks, offsets = [array], [0]
        for offset in list(range(-reach, 0)) + list(range(1, reach + 1)):
            route = [(i + offset, i) for i in range(length) if 0 <= i + offset < length]
            blocks.append((yield self.send(array, "seq", route)))
            offsets.append(offset)
        return blocks, offsets

    def gather(self, piece, at_once):
        near = yield lax.all_gather(piece, "seq", axis=0, tiled=True)
        far = yield self.across(near, 2)
        half = near.shape[0] // 2
        return (
            jnp.concatenate([near[:half], far[:half]], axis=0),
            jnp.concatenate([near[half:], far[half:]], axis=0),
        )

    def rows_of(self, size):
        return [jnp.int32(0), jnp.int32(lax.axis_size("seq") // 2 * size)]

    def columns(self, count):
        return jnp.zeros((1,), jnp.int32)

    def order(self, array, size):
        return array

    def restore(self, array, size):
        return array

    def reduce(self, left, near, far, at_once=False):
        back = yield self.across(inner_rows(left, far).astype(BF), 2)
        mine = inner_rows(left, near) + back
        share = lax.psum_scatter(mine, "seq", scatter_dimension=0, tiled=True).astype(BF)
        return (yield from self.spread(share))

    def reduce_blocks(self, near, far):
        back = yield self.across(far, 2)
        mine = (near.astype(F32) + back).reshape(-1, near.shape[2])
        share = lax.psum_scatter(mine, "seq", scatter_dimension=0, tiled=True).astype(BF)
        return (yield from self.spread(share))

    spread = Direct.spread


def gate(array, *earlier):
    return lax.optimization_barrier((array,) + earlier)[0]


class Chain:
    def __init__(self, plan, steps):
        self.plan, self.steps = plan, steps
        self.value = None
        self.sent = next(steps)
        self.operands = tuple(plan.given())

    def hold(self, *earlier):
        if self.sent is not None:
            self.sent = gate(self.sent, *earlier)

    def step(self, count=1):
        for _ in range(count):
            if self.sent is not None:
                try:
                    self.sent = self.steps.send(self.sent)
                except StopIteration as end:
                    self.sent, self.value = None, end.value
                self.operands = tuple(self.plan.given())

    def end(self):
        while self.sent is not None:
            self.step()
        return self.value


def halves(front, pair, other):
    half = pair.shape[0] // 2
    one, two = pair[half:], other[:half]
    near = jnp.concatenate([pair[:half], jnp.where(front, two, one)], axis=0)
    far = jnp.concatenate([jnp.where(front, one, two), other[half:]], axis=0)
    return near, far


def lane_masks():
    lane = lax.broadcasted_iota(jnp.int32, (1, GROUP), 1)
    turned = [(lane % LANES) // (HEAD_DIM // 2) == i for i in range(4)]
    plain = [lane // HEAD_DIM == i for i in range(4)]
    return turned, plain


def only(mask, array):
    return jnp.where(mask, array, jnp.zeros_like(array))


def spin(raw, c, s, way):
    a, b = raw[:, :LANES], raw[:, LANES:]
    return a * c - way * (b * s), b * c + way * (a * s)


def prepare_kernel(places, *refs):
    *blocks, out = refs
    width = blocks[0].shape[1] - LANES
    rows = out.shape[0] // len(blocks)
    count = places.shape[0]
    size = width // count
    for i, block in enumerate(blocks):
        normal = centre(block[:, :width].astype(F32))[0].astype(BF)
        at = slice(i * rows, (i + 1) * rows)
        out[at, width:] = block[:, width:]
        for s in range(count):
            to = pl.multiple_of(places[s] * size, LANES)
            out[at, pl.ds(to, size)] = normal[:, s * size : (s + 1) * size]


def mix_kernel(ours, theirs, near, far, tables, near_out, far_out, cosine, sine):
    count = pl.num_programs(0) // 2
    step = pl.program_id(0)
    half = near.shape[0]
    rows = jnp.where(step < count, ours[...], theirs[...])
    marks = rows[:, half : half + LANES].astype(F32)
    lane = lax.broadcasted_iota(jnp.int32, (1, LANES), 1).astype(F32)
    exact = lambda flags, table: jnp.dot(
        flags.astype(F32), table, preferred_element_type=F32, precision=lax.Precision.HIGHEST
    )
    coarse = exact(marks[:, 0:1] == lane, tables[:LANES])
    fine = exact(marks[:, 1:2] == lane, tables[LANES:])
    c = coarse[:, :LANES] * fine[:, :LANES] - coarse[:, LANES:] * fine[:, LANES:]
    s = coarse[:, LANES:] * fine[:, :LANES] + coarse[:, :LANES] * fine[:, LANES:]
    for weight, out in ((near, near_out), (far, far_out)):
        raw = dot(rows[:, :half], weight[...])
        for kind, scale in ((0, SCALE), (1, 1.0)):
            at = kind * GROUP
            a, b = spin(raw[:, at : at + GROUP], c, s, 1.0)
            out[:, at : at + LANES] = (a * scale).astype(BF)
            out[:, at + LANES : at + GROUP] = (b * scale).astype(BF)
        out[:, 2 * GROUP :] = raw[:, 2 * GROUP :].astype(BF)

    @pl.when(step % count == 0)
    def _():
        cosine[...] = c
        sine[...] = s


def attend_kernel(q0, k0, v0, q1, k1, v1, doc_row, doc_column, attended, attended_low, logs):
    turned, plain = lane_masks()
    allowed = doc_column[...] == doc_row[0]
    lane = lax.broadcasted_iota(jnp.int32, (1, LANES), 1)
    totals = jnp.zeros((q0.shape[0], LANES), F32)
    for group, (q, k, v) in enumerate(((q0, k0, v0), (q1, k1, v1))):
        queries, keys, values = q[...], k[...], v[...]
        kept = jnp.zeros(queries.shape, F32)
        for i in range(4):
            raw = outer_rows(only(turned[i], queries), keys)
            raw = jnp.where(allowed, raw, -jnp.inf)
            top = jnp.max(raw, axis=-1, keepdims=True)
            weights = jnp.exp(raw - top)
            total = jnp.sum(weights, axis=-1, keepdims=True)
            found = dot(weights.astype(BF), values) / total
            kept = jnp.where(plain[i], found, kept)
            totals = jnp.where(lane == 4 * group + i, top + jnp.log(total), totals)
        attended[:, group * GROUP : (group + 1) * GROUP] = kept
        attended_low[:, group * GROUP : (group + 1) * GROUP] = kept.astype(BF)
    logs[...] = totals


def around_kernel(grads, attended, logs, around, numbers):
    heads = HEADS // 2
    width = grads.shape[1]
    row = lax.broadcasted_iota(jnp.int32, (width, LANES), 0)
    lane = lax.broadcasted_iota(jnp.int32, (width, LANES), 1)
    low = grads[...].astype(BF)
    delta = jnp.dot(
        low.astype(F32) * attended[...],
        (row // HEAD_DIM == lane - 2 * heads).astype(F32),
        preferred_element_type=F32,
        precision=lax.Precision.HIGHEST,
    )
    both = logs[...] + delta
    numbers[...] = both
    high = both.astype(BF).astype(F32)
    around[:, :width] = low
    around[:, width:] = (high + pltpu.roll(both - high, heads, 1)).astype(BF)


def query_kernel(q0, k0, v0, q1, k1, v1, around, numbers, doc_row, doc_column, cosine, sine, d_q):
    turned, plain = lane_masks()
    allowed = doc_column[...] == doc_row[0]
    c, s = cosine[...] * SCALE, sine[...] * SCALE
    for group, (q, k, v) in enumerate(((q0, k0, v0), (q1, k1, v1))):
        queries, keys, values = q[...], k[...], v[...]
        grads = around[:, group * GROUP : (group + 1) * GROUP]
        kept = jnp.zeros(queries.shape, F32)
        for i in range(4):
            at = 4 * group + i
            raw = outer_rows(only(turned[i], queries), keys)
            weights = jnp.where(allowed, jnp.exp(raw - numbers[:, at : at + 1]), 0.0)
            d_weights = outer_rows(only(plain[i], grads), values)
            d_raw = (weights * (d_weights - numbers[:, 16 + at : 17 + at])).astype(BF)
            kept = jnp.where(turned[i], dot(d_raw, keys), kept)
        a, b = spin(kept, c, s, -1.0)
        d_q[:, group * GROUP : group * GROUP + LANES] = a.astype(BF)
        d_q[:, group * GROUP + LANES : (group + 1) * GROUP] = b.astype(BF)


def key_kernel(q0, k0, v0, q1, k1, v1, d_q, doc_row, doc_column, cosine, sine, *refs):
    *around, near, far = refs
    turned, plain = lane_masks()
    rows = k0.shape[0]
    c, s = cosine[...], sine[...]
    column = doc_column[...]
    kept = [[jnp.zeros(k0.shape, F32), jnp.zeros(k0.shape, F32)] for _ in (0, 1)]
    for j, block in enumerate(around):
        part = slice(j * rows, (j + 1) * rows)
        allowed = column == doc_row[0, :, part]
        numbers = block[:, 2 * GROUP :].astype(F32)
        numbers = (numbers + pltpu.roll(numbers, LANES - HEADS // 2, 1)).T
        for group, (q, k, v) in enumerate(((q0, k0, v0), (q1, k1, v1))):
            queries, keys, values = q[part, :], k[...], v[...]
            grads = block[:, group * GROUP : (group + 1) * GROUP]
            add_k = jnp.zeros(k0.shape, F32)
            add_v = jnp.zeros(k0.shape, F32)
            for i in range(4):
                at = 4 * group + i
                raw = outer_rows(only(turned[i], keys), queries)
                weights = jnp.where(allowed, jnp.exp(raw - numbers[at : at + 1, :]), 0.0)
                add_v = jnp.where(plain[i], dot(weights.astype(BF), grads), add_v)
                d_weights = outer_rows(only(plain[i], values), grads)
                d_raw = (weights * (d_weights - numbers[16 + at : 17 + at, :])).astype(BF)
                add_k = jnp.where(turned[i], dot(d_raw, queries), add_k)
            kept[group][0] += add_k
            kept[group][1] += add_v
    for group, out in enumerate((near, far)):
        a, b = spin(kept[group][0], c, s, -1.0)
        out[:, :GROUP] = d_q[:, group * GROUP : (group + 1) * GROUP]
        out[:, GROUP : GROUP + LANES] = a.astype(BF)
        out[:, GROUP + LANES : 2 * GROUP] = b.astype(BF)
        out[:, 2 * GROUP :] = kept[group][1].astype(BF)


def pack_kernel(place, active, grads, attended, branch, near, far):
    count, depth = near.shape[0], attended.shape[1] // near.shape[0]
    rows = active.shape[1] // count
    wide = near.shape[2]
    for i in (0, 1):
        one = inner_rows(active[...], grads[:, i * wide : (i + 1) * wide]).astype(BF)
        two = inner_rows(attended[...], branch[i]).astype(BF)

        def store(out):
            for s in range(count):
                out[s, :rows] = one[s * rows : (s + 1) * rows]
                at = s * depth
                out[s, rows:, :GROUP] = two[at : at + depth // 2]
                out[s, rows:, GROUP:] = two[at + depth // 2 : at + depth]

        @pl.when(place[0] == i)
        def _():
            store(near)

        @pl.when(place[0] != i)
        def _():
            store(far)


def place_kernel(rest, one_low, one_high, two_low, two_high, weight, gain, grads, gains):
    length, half, rows, pad = rest
    full = weight.shape[1] // 2
    for i, pair in enumerate(((one_low, two_low), (one_high, two_high))):
        for s in range(length):
            for c, share in enumerate(pair):
                size = min(half, rows - c * half)
                at = i * full + s * rows + c * half
                grads[:, at : at + size] = share[:, s * pad : s * pad + size].astype(F32)
    raw = grads[...]
    total = jnp.sum(raw * weight[...].astype(F32), axis=1, keepdims=True)
    gains[...] = jnp.broadcast_to(total, gains.shape)
    grads[...] = raw * gain[...]


def call_kernel(kernel, ins, outs, grid=1, room=56, micros=5):
    spec = lambda block, at: (
        pl.BlockSpec(memory_space=pltpu.SMEM) if block is None else pl.BlockSpec(block, at)
    )
    return pl.pallas_call(
        kernel,
        grid=(grid,),
        in_specs=[spec(block, at) for _, block, at in ins],
        out_specs=tuple(pl.BlockSpec(block, at) for _, _, block, at in outs),
        out_shape=tuple(jax.ShapeDtypeStruct(shape, kind) for shape, kind, _, _ in outs),
        compiler_params=pltpu.CompilerParams(vmem_limit_bytes=room * 2**20),
        cost_estimate=pl.CostEstimate(flops=micros * 10**9, bytes_accessed=1, transcendentals=0),
    )(*[a for a, _, _ in ins])


def gelu_parts(inner):
    share = 0.5 * (1.0 + lax.erf(inner * 0.7071067811865476))
    return inner * share, share + inner * (0.3989422804014327 * jnp.exp(-0.5 * inner * inner))


def hidden_kernel(marks, rows, grads, pair, other, shrink_pair, shrink_other, *refs):
    active, lifted_grads, out, out_there, d_rows, d_there = refs[:6]
    expand_w, shrink_w, semaphore = refs[6:]
    units = shrink_w.shape[0]
    half = pair.shape[0] // 2
    wide = shrink_pair.shape[1]
    places = marks.shape[0] - 2
    block = units // places
    front = marks[0] == 1
    x = marks[1]
    step = pl.program_id(0)

    def weights(source, start, at, row):
        return source.at[pl.ds(start, half)], expand_w.at[at, pl.ds(row, half)]

    def shrinks(source, high, at, low):
        found = []
        for j in range(places // 2):
            start = high * (source.shape[0] // 2) + j * block
            row = pl.multiple_of(marks[2 + low * (places // 2) + j], 16)
            column = pl.multiple_of(at * wide, LANES)
            found.append(
                (
                    source.at[pl.ds(start, block)],
                    shrink_w.at[pl.ds(row, block), pl.ds(column, wide)],
                )
            )
        return found

    def begin(moves, first):
        copies = [
            pltpu.make_async_copy(a, b, semaphore.at[first + k]) for k, (a, b) in enumerate(moves)
        ]
        for copy in copies:
            copy.start()
        return copies

    @pl.when(step == 0)
    def _():
        moves = [weights(pair, 0, x, 0), weights(other, half, 1 - x, half)]
        moves += shrinks(shrink_pair, 0, x, 0) + shrinks(shrink_other, 1, 1 - x, 1)
        copies = begin(moves, 0)
        for flag, low, high in ((front, other, pair), (jnp.logical_not(front), pair, other)):

            @pl.when(flag)
            def _():
                start = 0 if low is other else half
                back = half - start
                shrink_low = shrink_other if low is other else shrink_pair
                shrink_high = shrink_pair if low is other else shrink_other
                crossed = [weights(low, start, x, half), weights(high, back, 1 - x, 0)]
                crossed += shrinks(shrink_low, start // half, x, 1)
                crossed += shrinks(shrink_high, back // half, 1 - x, 0)
                for copy in begin(crossed, len(moves)):
                    copy.wait()

        for copy in copies:
            copy.wait()

    values, dy = rows[...], grads[...]
    tile = 256
    for at in range(0, units, tile):
        cut = slice(at, min(at + tile, units))
        inner = dot(values, expand_w[0, :, cut])
        gate = dot(values, expand_w[1, :, cut])
        d_active = outer_rows(dy, shrink_w[cut, :])
        value, slope = gelu_parts(inner)
        active[:, cut] = (value * gate).astype(BF)
        lifted_grads[x, :, cut] = (d_active * gate * slope).astype(BF)
        lifted_grads[1 - x, :, cut] = (d_active * value).astype(BF)
    result = dot(active[...], shrink_w[...])
    back = outer_rows(lifted_grads[x], expand_w[0]) + outer_rows(lifted_grads[1 - x], expand_w[1])

    @pl.when(step == 0)
    def _():
        out[...] = result
        d_rows[...] = back

    @pl.when(step == 1)
    def _():
        out_there[...] = result.astype(BF)
        d_there[...] = back.astype(BF)


def hidden(marks, rows, grads, expand, shrink):
    count, width = rows.shape
    units = expand[0].shape[1]
    size = count // 2
    moving = lambda i: (i, 0)
    still = lambda i: (0, 0)
    held = pl.BlockSpec(memory_space=pl.ANY)
    outs = [
        ((count, units), BF, (size, units), moving),
        ((2, count, units), BF, (2, size, units), lambda i: (0, i, 0)),
        ((size, width), F32, (size, width), still),
        ((size, width), BF, (size, width), still),
        ((size, width), F32, (size, width), still),
        ((size, width), BF, (size, width), still),
    ]
    return pl.pallas_call(
        hidden_kernel,
        grid=(2,),
        in_specs=[pl.BlockSpec(memory_space=pltpu.SMEM)]
        + [pl.BlockSpec((size, width), moving)] * 2
        + [held] * 4,
        out_specs=tuple(pl.BlockSpec(block, at) for _, _, block, at in outs),
        out_shape=tuple(jax.ShapeDtypeStruct(shape, kind) for shape, kind, _, _ in outs),
        scratch_shapes=[
            pltpu.VMEM((2, width, units), BF),
            pltpu.VMEM((units, width), BF),
            pltpu.SemaphoreType.DMA((2 * marks.shape[0],)),
        ],
        compiler_params=pltpu.CompilerParams(vmem_limit_bytes=36 * 2**20),
        cost_estimate=pl.CostEstimate(flops=8 * 10**9, bytes_accessed=1, transcendentals=0),
    )(marks, rows, grads, *expand, *shrink)


def on_device(
    direct,
    tokens,
    norm_first,
    joint_weight,
    output_weight,
    norm_second,
    expand_weight,
    shrink_weight,
    document_start,
    cotangent,
):
    rows, width = tokens.shape
    plan = Direct() if direct else Plain(rows)
    length = lax.axis_size("seq")
    here = lax.axis_index("seq")
    x, core = plan.x, plan.core
    near_x = x == 0
    depth = joint_weight.shape[0]
    unit_rows = shrink_weight.shape[0]
    unit_half = (unit_rows + 1) // 2
    units = -(-unit_half * length // LANES) * LANES
    while units % length:
        units += LANES
    unit_pad = units // length
    half_width = width // 2

    def mine(array, start):
        parts = [array[:, start + i * GROUP : start + (i + 1) * GROUP] for i in range(4)]
        low, high = pick(near_x, parts[0::2], parts[1::2])
        return jnp.where(core == 0, low, high)

    source = jnp.arange(GROUP)
    turn = (
        source[:, None]
        == ((source % LANES) // 32 * HEAD_DIM + source // LANES * 32 + source % 32)[None, :]
    ).astype(BF)
    gain_one = norm_first.astype(F32)[:, None]
    gain_two = norm_second.astype(F32)[:, None]
    joint_piece = jnp.concatenate(
        [
            (dot(mine(joint_weight, 0), turn) * gain_one).astype(BF),
            (dot(mine(joint_weight, width), turn) * gain_one).astype(BF),
            (mine(joint_weight, 2 * width).astype(F32) * gain_one).astype(BF),
            mine(output_weight, 0),
        ],
        axis=1,
    )
    slot = jnp.arange(units)
    inner = core * unit_half + slot % unit_pad
    fits = (slot % unit_pad < unit_half) & (inner < unit_rows)
    unit_of = jnp.where(fits, slot // unit_pad * unit_rows + inner, -2 * FF)
    spread_units = (jnp.arange(2 * FF)[:, None] == (unit_of + x * FF)[None, :]).astype(BF)
    expand_piece = (dot(expand_weight, spread_units) * gain_two).astype(BF)
    slot_row = jnp.arange(unit_pad)

    def picked(c):
        row = c * unit_half + slot_row
        row = jnp.where((slot_row < unit_half) & (row < unit_rows), row, -1)
        return (row[:, None] == jnp.arange(unit_rows)[None, :]).astype(BF)

    shrink_piece = dot(
        picked(core),
        jnp.where(near_x, shrink_weight[:, :half_width], shrink_weight[:, half_width:]),
    ).astype(BF)

    anchor = (lax.axis_index("rep") * length + here) * rows
    position = anchor + jnp.arange(rows, dtype=jnp.int32) - document_start
    marks = jnp.pad(
        jnp.stack([(position + 1) // 16, (position + 1) % 16], axis=1), ((0, 0), (0, LANES - 2))
    ).astype(BF)
    packed = jnp.concatenate([tokens, marks], axis=1)
    joint = Chain(plan, plan.gather(joint_piece, True))
    near_tokens = Chain(plan, plan.around(packed))
    joint.step(3)
    expand = Chain(plan, plan.gather(gate(expand_piece, *joint.operands), False))
    joint.step(2)
    blocks, offsets = near_tokens.end()
    expand.step(2)
    shrink = Chain(plan, plan.gather(gate(shrink_piece, *expand.operands), False))
    block_count = len(blocks)
    span = block_count * rows
    still = lambda i: (0, 0)
    moving = lambda i: (i, 0)
    (sent,) = call_kernel(
        prepare_kernel,
        [(plan.columns(width // depth), None, None)]
        + [(block, (rows, width + LANES), still) for block in blocks],
        [((span, width + LANES), BF, (span, width + LANES), still)],
        micros=2,
    )
    first = (sent, swap_core(sent))
    offset_rows = jnp.stack([jnp.int32(offset) for offset in offsets]) * rows
    index = (here * rows + offset_rows[:, None] + jnp.arange(rows)[None, :]).reshape(1, span)
    document_rows = []
    for rows_in in first:
        code = rows_in[:, width : width + 2].astype(F32).T
        code = code[:1] * 16.0 + code[1:]
        document_rows.append(jnp.where(code > 0, index.astype(F32) - (code - 1.0), FAR))
    document_row = jnp.stack(document_rows)
    document_column = jnp.concatenate([row[:, :rows] for row in document_rows], axis=1).T
    halves_of_head = HEAD_DIM // 2
    frequency = THETA ** (-(jnp.arange(halves_of_head, dtype=F32) * 2.0) / HEAD_DIM)
    frequency = jnp.tile(frequency, LANES // halves_of_head)[None, :]
    steps = jnp.arange(LANES, dtype=F32)[:, None]
    angle = jnp.concatenate([16.0 * steps * frequency, (steps - 1.0) * frequency], axis=0)
    tables = jnp.concatenate([jnp.cos(angle), jnp.sin(angle)], axis=1)

    joint_near, joint_far = halves(plan.front, *joint.value)
    output_mine = jnp.concatenate([joint_near[:, 3 * GROUP :], joint_far[:, 3 * GROUP :]], axis=1)
    output_all = jnp.concatenate([output_mine, swap_core(output_mine)], axis=1)

    def turn_columns(array):
        parts = [array[:, i * GROUP : (i + 1) * GROUP] for i in range(4)]
        parts = pick(core == 0, parts, parts[2:] + parts[:2])
        left, right = pick(near_x, parts[:2], parts[1::-1]), pick(near_x, parts[2:], parts[:1:-1])
        return jnp.concatenate(left + right, axis=-1)

    wide = 3 * GROUP
    *mixed, cosine, sine = call_kernel(
        mix_kernel,
        [
            (first[0], (rows, width + LANES), lambda i: (jnp.minimum(i, block_count - 1), 0)),
            (first[1], (rows, width + LANES), lambda i: (jnp.maximum(i - block_count, 0), 0)),
            (joint_near, (width, wide), still),
            (joint_far, (width, wide), still),
            (tables, (2 * LANES, 2 * LANES), still),
        ],
        [((2 * span, wide), BF, (rows, wide), moving)] * 2
        + [((2 * rows, LANES), F32, (rows, LANES), lambda i: (i // block_count, 0))] * 2,
        2 * block_count,
        micros=7,
    )
    expand.step()
    shrink.step(2)
    document_row = gate(document_row, *expand.operands)
    column = lambda kind, every: (
        ((span, GROUP), lambda i: (i, kind))
        if every
        else ((rows, GROUP), lambda i: (i * block_count, kind))
    )
    wide_keys = [
        (array, *column(kind, kind > 0)) for array in mixed for kind in range(3)
    ]
    wide_queries = [
        (array, *column(kind, kind == 0)) for array in mixed for kind in range(3)
    ]
    documents = [
        (document_row, (1, 1, span), lambda i: (i, 0, 0)),
        (document_column, (rows, 1), moving),
    ]
    both = lambda w, kind: ((2 * rows, w), kind, (rows, w), moving)
    attended, attended_low, logs = call_kernel(
        attend_kernel,
        wide_keys + documents,
        [both(2 * GROUP, F32), both(2 * GROUP, BF), both(LANES, F32)],
        2,
        micros=5,
    )
    shrink.step()
    shrink.step()
    expand_both = expand.end()
    attended_there = gate(swap_core(attended_low), *expand_both)
    attended_there = jnp.concatenate([attended_there[rows:], attended_there[:rows]], axis=0)
    attended_rows = plan.order(
        turn_columns(jnp.concatenate([attended_low, attended_there], axis=1)), depth
    )
    middle = tokens.astype(F32) + turn_columns(dot(attended_rows[:rows], output_all))
    second, second_scale = centre(middle)
    second_low = plan.order(second.astype(BF), depth)
    second_both = jnp.concatenate([second_low, swap_core(second_low)], axis=0)
    shrink_both = shrink.end()

    cotangents = jnp.concatenate([cotangent, swap_core(gate(cotangent, attended_low))], axis=0)

    where = jnp.stack(
        [plan.front.astype(jnp.int32), x.astype(jnp.int32)]
        + [row.astype(jnp.int32) for row in plan.rows_of(unit_pad)]
    )
    active_low, lifted_grads, out, out_there, second_grad, second_there = hidden(
        where, second_both, cotangents, expand_both, shrink_both
    )
    expand = Chain(plan, plan.reduce(second_both, lifted_grads[0], lifted_grads[1], False))
    result = middle + out + swap_core(out_there).astype(F32)
    second_grad = second_grad + swap_core(second_there).astype(F32)
    middle_grad = cotangent.astype(F32) + centre_back(
        second, second_scale, plan.restore(second_grad, depth)
    )
    branch = middle_grad.astype(BF)
    branch_both = turn_columns(jnp.concatenate([branch, swap_core(branch)], axis=0))
    attended_grad = turn_columns(plan.restore(outer_rows(branch_both, output_all), depth))
    around, numbers = call_kernel(
        around_kernel,
        [
            (attended_grad[:, : 2 * GROUP], (rows, 2 * GROUP), moving),
            (attended, (rows, 2 * GROUP), moving),
            (logs, (rows, LANES), moving),
        ],
        [both(2 * GROUP + LANES, BF), both(LANES, F32)],
        2,
    )
    near_grads = Chain(plan, plan.around(around))
    branch_sides = jnp.stack(
        pick(near_x, *[[branch_both[:, i * GROUP : (i + 1) * GROUP] for i in o] for o in ((0, 1), (1, 0))])
    )
    kinds = [
        ((length, unit_pad + depth // 2, half_width), BF),
        (length, unit_pad + depth // 2, half_width),
        lambda i: (0, 0, 0),
    ]
    sums = call_kernel(
        pack_kernel,
        [
            (x.astype(jnp.int32)[None], None, 0),
            (active_low, (2 * rows, units), still),
            (cotangents, (2 * rows, width), still),
            (plan.restore(attended_rows, depth), (2 * rows, width), still),
            (branch_sides, (2, 2 * rows, GROUP), lambda i: (0, 0, 0)),
        ],
        [(*kinds[0], kinds[1], kinds[2])] * 2,
    )
    near_grads.step(2)
    shrink = Chain(plan, plan.reduce_blocks(*sums))
    turning = [(cosine, (rows, LANES), moving), (sine, (rows, LANES), moving)]
    (query_grad,) = call_kernel(
        query_kernel,
        wide_keys
        + [
            (around, (rows, 2 * GROUP), moving),
            (numbers, (rows, LANES), moving),
        ]
        + documents
        + turning,
        [both(2 * GROUP, BF)],
        2,
        micros=13,
    )
    expand.step()
    arounds, _ = near_grads.end()
    mixed_grads = call_kernel(
        key_kernel,
        wide_queries
        + [(query_grad, (rows, 2 * GROUP), moving)]
        + documents
        + turning
        + [(block, (rows, 2 * GROUP + LANES), moving) for block in arounds],
        [both(wide, BF), both(wide, BF)],
        2,
        micros=16,
    )
    own_first = jnp.concatenate([rows_in[:rows, :width] for rows_in in first], axis=0)
    joint = Chain(plan, plan.reduce(own_first, *mixed_grads, True))
    expand.step()
    shrink.step()
    joint.step()
    moved = joint.operands + expand.operands
    expand.hold(*moved)
    shrink.hold(*moved)
    first_part = outer_rows(mixed_grads[0], joint_near[:, :wide]) + outer_rows(
        mixed_grads[1], joint_far[:, :wide]
    )
    first_grad = first_part[:rows] + swap_core(first_part[rows:].astype(BF)).astype(F32)
    normal, normal_scale = centre(tokens.astype(F32))
    tokens_grad = middle_grad + centre_back(
        normal, normal_scale, plan.restore(first_grad, depth)
    )

    expand.step()
    shrink.hold(*expand.operands)
    shrink.step()
    joint.step()
    waits = joint.operands
    expand.step()
    shrink.hold(*waits, *expand.operands)
    expand.step()
    joint.step(3)
    shrink.step()
    expand_shares = expand.end()
    share_parts = [share for pair in expand_shares for share in pair]
    expand_grad, second_gains = call_kernel(
        functools.partial(place_kernel, (length, unit_half, unit_rows, unit_pad)),
        [(part, (depth, units), still) for part in share_parts]
        + [(expand_weight, (depth, 2 * FF), still), (gain_two, (depth, 1), still)],
        [
            ((depth, 2 * FF), F32, (depth, 2 * FF), still),
            ((depth, LANES), F32, (depth, LANES), still),
        ],
        micros=3,
    )
    second_gain_grad = second_gains[:, 0]
    shrink.step()
    joint.step()
    joint.hold(expand_grad)
    shrink_shares = shrink.end()
    joint_four = joint.end()

    shrink_grad = jnp.concatenate(
        [
            inner_rows(picked(0), shrink_shares[0][i][:unit_pad])
            + inner_rows(picked(1), shrink_shares[1][i][:unit_pad])
            for i in (0, 1)
        ],
        axis=1,
    )
    output_grad = []
    for pair in shrink_shares:
        for share in pair:
            share = share[unit_pad:]
            output_grad.append(jnp.concatenate([share[:, :GROUP], share[:, GROUP:]], axis=0))
    output_grad = jnp.concatenate(output_grad, axis=1).astype(F32)
    columns = []
    for kind in range(3):
        for c in (0, 1):
            for i in (0, 1):
                piece = joint_four[c][i][:, kind * GROUP : (kind + 1) * GROUP]
                columns.append(outer_rows(piece, turn) if kind < 2 else piece.astype(F32))
    joint_raw = jnp.concatenate(columns, axis=1)
    joint_grad = joint_raw * gain_one
    first_gain_grad = jnp.sum(joint_raw * joint_weight.astype(F32), axis=1)
    return (
        result.astype(BF),
        tokens_grad.astype(BF),
        first_gain_grad,
        joint_grad,
        output_grad,
        second_gain_grad,
        expand_grad,
        shrink_grad,
    )


def solution(mesh):
    placed = (
        P(("rep", "seq"), None),
        P("seq"),
        P("seq", None),
        P("seq", None),
        P("seq"),
        P("seq", None),
        P("seq", None),
        P(("rep", "seq")),
        P(("rep", "seq"), None),
    )
    return jax.shard_map(
        functools.partial(on_device, mesh.shape["seq"] == 8),
        mesh=mesh,
        in_specs=placed,
        out_specs=(
            P(("rep", "seq"), None),
            P(("rep", "seq"), None),
            P("seq"),
            P("seq", None),
            P("seq", None),
            P("seq"),
            P("seq", None),
            P("seq", None),
        ),
        check_vma=False,
    )
```

```python
import functools

import jax
import jax.numpy as jnp
from jax import lax
from jax.experimental import pallas as pl
from jax.experimental.pallas import tpu as pltpu
from jax.sharding import PartitionSpec as P

HEADS = 16
HEAD_DIM = 64
FF = 2624
HALO = 512
EPSILON = 1e-05
THETA = 160000.0
SCALE = 0.125
LANES = 128
GROUP = 256
FAR = -1e6
LONG = 10**11
BF = jnp.bfloat16
F32 = jnp.float32


def dot(left, right):
    return jnp.dot(left, right, preferred_element_type=F32)


def inner_rows(left, right):
    return lax.dot_general(left, right, (((0,), (0,)), ((), ())), preferred_element_type=F32)


def outer_rows(left, right):
    return lax.dot_general(left, right, (((1,), (1,)), ((), ())), preferred_element_type=F32)


def pick(flag, one, two):
    return [jnp.where(flag, a, b) for a, b in zip(one, two)]


def centre(rows):
    middle = jnp.mean(rows, axis=-1, keepdims=True)
    centered = rows - middle
    spread = jnp.mean(centered * centered, axis=-1, keepdims=True)
    scale = lax.rsqrt(spread + EPSILON)
    return centered * scale, scale


def centre_back(normal, scale, grads):
    return scale * (
        grads
        - jnp.mean(grads, axis=-1, keepdims=True)
        - normal * jnp.mean(grads * normal, axis=-1, keepdims=True)
    )


def two_parts(values):
    high = lax.reduce_precision(values, 8, 7)
    return high.astype(BF), (values - high).astype(BF)


def swap_core(array):
    return lax.ppermute(array, "rep", [(i, i ^ 1) for i in range(lax.axis_size("rep"))])


def swap_far(array):
    return lax.ppermute(array, "rep", [(i, i ^ 2) for i in range(lax.axis_size("rep"))])


class Moves:
    def __init__(self):
        self.recent = []

    def send(self, array, axes, route):
        self.recent.append(array)
        return lax.ppermute(array, axes, route)

    def across(self, array, flip):
        return self.send(array, "rep", [(i, i ^ flip) for i in range(lax.axis_size("rep"))])

    def given(self):
        found, self.recent = self.recent, []
        return found


class Direct(Moves):
    depth = 4

    def __init__(self):
        super().__init__()
        self.place = lax.axis_index("seq")
        self.z = self.place // 2
        self.y = self.place % 2
        self.x = lax.axis_index("rep") // 2
        self.core = lax.axis_index("rep") % 2
        self.front = self.core == 0

    def along(self, array, flip):
        route = [(s, s ^ (2 * flip)) for s in range(2 * self.depth)]
        return self.send(array, "seq", route)

    def cross(self, array, turn):
        n = 2 * self.depth
        route = []
        for r in range(4):
            for s in range(n):
                to = (r ^ 2, s) if r % 2 == turn else (r, s ^ 1)
                route.append((r * n + s, to[0] * n + to[1]))
        return self.send(array, ("rep", "seq"), route)

    def around(self, array):
        rows = array.shape[0]
        last = 2 * self.depth
        low = self.send(array, "seq", [(s, s + 2) for s in range(last - 2)])
        high = self.send(array, "seq", [(s, s - 2) for s in range(2, last)])
        low = yield low
        high = yield high
        sent = jnp.concatenate([array, jnp.where(self.y == 0, high, low)], axis=0)
        beside = yield self.send(sent, "seq", [(s, s ^ 1) for s in range(last)])
        step = 1 - 2 * self.y
        return [array, low, high, beside[:rows], beside[rows:]], [0, -2, 2, step, -step]

    def gather(self, piece, at_once):
        if at_once:
            sent = [self.along(piece, k) for k in (1, 2, 3)]
            found = [piece]
            for array in sent:
                array = yield array
                found.append(array)
            rows = jnp.concatenate(found, axis=0)
        else:
            there = yield self.along(piece, 1)
            pair = jnp.concatenate([piece, there], axis=0)
            there = yield self.along(pair, 2)
            rows = jnp.concatenate([pair, there], axis=0)
        once = yield self.cross(rows, 0)
        pair = jnp.concatenate([rows, once], axis=0)
        other = yield self.cross(pair, 1)
        return pair, other

    def to_near(self, grid):
        turned = [pick(self.y == 0, pair, pair[::-1]) for pair in grid]
        near = []
        for y in (0, 1):
            a, b, c, d = [pair[y] for pair in turned]
            a, b, c, d = pick(self.z % 2 == 0, [a, b, c, d], [b, a, d, c])
            near.append(pick(self.z // 2 == 0, [a, b, c, d], [c, d, a, b]))
        return near

    def to_mesh(self, near):
        lines = []
        for a, b, c, d in near:
            a, b, c, d = pick(self.z % 2 == 0, [a, b, c, d], [b, a, d, c])
            lines.append(pick(self.z // 2 == 0, [a, b, c, d], [c, d, a, b]))
        return [pick(self.y == 0, list(pair), list(pair)[::-1]) for pair in zip(*lines)]

    def rows_of(self, size):
        return [
            (2 * (self.z ^ k) + (self.y ^ y)) * size for y in (0, 1) for k in range(self.depth)
        ]

    def columns(self, count):
        z, y = jnp.arange(count) // 2, jnp.arange(count) % 2
        return (4 * (y ^ self.y) + (z ^ self.z)).astype(jnp.int32)

    def order(self, array, size):
        n = self.depth
        cut = lambda s: array[..., s * size : (s + 1) * size]
        near = self.to_near([[cut(2 * z), cut(2 * z + 1)] for z in range(n)])
        return jnp.concatenate(near[0] + near[1], axis=-1)

    def restore(self, array, size):
        n = self.depth
        cut = lambda j: array[..., j * size : (j + 1) * size]
        grid = self.to_mesh([[cut(n * y + k) for k in range(n)] for y in (0, 1)])
        return jnp.concatenate([part for pair in grid for part in pair], axis=-1)

    def down(self, mine, at_once):
        rows = mine.shape[0] // 4
        cut = lambda k, n: mine[k * rows : (k + n) * rows]
        if at_once:
            sent = [self.along(cut(k, 1), k) for k in (1, 2, 3)]
            total = cut(0, 1).astype(F32)
            for array in sent:
                array = yield array
                total = total + array.astype(F32)
            share = total.astype(BF)
        else:
            there = yield self.along(cut(2, 2), 2)
            pair = (cut(0, 2).astype(F32) + there.astype(F32)).astype(BF)
            there = yield self.along(pair[rows:], 1)
            share = (pair[:rows].astype(F32) + there.astype(F32)).astype(BF)
        return (yield from self.spread(share))

    def reduce(self, left, near, far, at_once):
        half = left.shape[1] // 2
        top, bottom = left[:, :half], left[:, half:]
        sent = lax.dot_general(
            jnp.stack([jnp.where(self.front, bottom, top), bottom]),
            jnp.stack([jnp.where(self.front, near, far), far]),
            (((1,), (1,)), ((0,), (0,))),
            preferred_element_type=F32,
        ).astype(BF)
        back = yield self.cross(sent, 1)
        once = inner_rows(jnp.where(self.front, top, bottom), jnp.where(self.front, far, near))
        once_in = yield self.cross((once + back[1]).astype(BF), 0)
        mine = (inner_rows(top, near) + back[0] + once_in).astype(BF)
        return (yield from self.down(mine, at_once))

    def reduce_blocks(self, near, far):
        back = yield self.across(far, 2)
        total = (near.astype(F32) + back.astype(F32)).astype(BF)
        lines = self.to_near([total[2 * z : 2 * z + 2] for z in range(self.depth)])
        mine, sent = [jnp.concatenate(line, axis=0) for line in lines]
        route = [(s, s ^ 1) for s in range(2 * self.depth)]
        back = yield self.send(sent, "seq", route)
        mine = (mine.astype(F32) + back.astype(F32)).astype(BF)
        return (yield from self.down(mine, False))

    def spread(self, share):
        there = yield self.across(share, 2)
        pair = [share, there]
        low, high = pick(self.x == 0, pair, pair[::-1])
        both = jnp.concatenate([low, high], axis=1)
        there = yield self.across(both, 1)
        size = share.shape[1]
        cores = pick(self.core == 0, [both, there], [there, both])
        return [[part[:, :size], part[:, size:]] for part in cores]


class Plain(Moves):
    def __init__(self, rows):
        super().__init__()
        self.rows = rows
        self.x = lax.axis_index("rep") // 2
        self.core = lax.axis_index("rep") % 2
        self.front = jnp.bool_(True)

    def around(self, array):
        length = lax.axis_size("seq")
        reach = min(HALO // self.rows, length - 1)
        blocks, offsets = [array], [0]
        for offset in list(range(-reach, 0)) + list(range(1, reach + 1)):
            route = [(i + offset, i) for i in range(length) if 0 <= i + offset < length]
            blocks.append((yield self.send(array, "seq", route)))
            offsets.append(offset)
        return blocks, offsets

    def gather(self, piece, at_once):
        near = yield lax.all_gather(piece, "seq", axis=0, tiled=True)
        far = yield self.across(near, 2)
        half = near.shape[0] // 2
        return (
            jnp.concatenate([near[:half], far[:half]], axis=0),
            jnp.concatenate([near[half:], far[half:]], axis=0),
        )

    def rows_of(self, size):
        return [jnp.int32(0), jnp.int32(lax.axis_size("seq") // 2 * size)]

    def columns(self, count):
        return jnp.zeros((1,), jnp.int32)

    def order(self, array, size):
        return array

    def restore(self, array, size):
        return array

    def reduce(self, left, near, far, at_once=False):
        back = yield self.across(inner_rows(left, far).astype(BF), 2)
        mine = inner_rows(left, near) + back
        share = lax.psum_scatter(mine, "seq", scatter_dimension=0, tiled=True).astype(BF)
        return (yield from self.spread(share))

    def reduce_blocks(self, near, far):
        back = yield self.across(far, 2)
        mine = (near.astype(F32) + back).reshape(-1, near.shape[2])
        share = lax.psum_scatter(mine, "seq", scatter_dimension=0, tiled=True).astype(BF)
        return (yield from self.spread(share))

    spread = Direct.spread


def gate(array, *earlier):
    return lax.optimization_barrier((array,) + earlier)[0]


class Chain:
    def __init__(self, plan, steps):
        self.plan, self.steps = plan, steps
        self.value = None
        self.sent = next(steps)
        self.operands = tuple(plan.given())

    def hold(self, *earlier):
        if self.sent is not None:
            self.sent = gate(self.sent, *earlier)

    def step(self, count=1):
        for _ in range(count):
            if self.sent is not None:
                try:
                    self.sent = self.steps.send(self.sent)
                except StopIteration as end:
                    self.sent, self.value = None, end.value
                self.operands = tuple(self.plan.given())

    def end(self):
        while self.sent is not None:
            self.step()
        return self.value


def halves(front, pair, other):
    half = pair.shape[0] // 2
    one, two = pair[half:], other[:half]
    near = jnp.concatenate([pair[:half], jnp.where(front, two, one)], axis=0)
    far = jnp.concatenate([jnp.where(front, one, two), other[half:]], axis=0)
    return near, far


def lane_masks():
    lane = lax.broadcasted_iota(jnp.int32, (1, GROUP), 1)
    turned = [(lane % LANES) // (HEAD_DIM // 2) == i for i in range(4)]
    plain = [lane // HEAD_DIM == i for i in range(4)]
    return turned, plain


def only(mask, array):
    return jnp.where(mask, array, jnp.zeros_like(array))


def spin(raw, c, s, way):
    a, b = raw[:, :LANES], raw[:, LANES:]
    return a * c - way * (b * s), b * c + way * (a * s)


def prepare_kernel(places, *refs):
    *blocks, out = refs
    width = blocks[0].shape[1] - LANES
    rows = out.shape[0] // len(blocks)
    count = places.shape[0]
    size = width // count
    for i, block in enumerate(blocks):
        normal = centre(block[:, :width].astype(F32))[0].astype(BF)
        at = slice(i * rows, (i + 1) * rows)
        out[at, width:] = block[:, width:]
        for s in range(count):
            to = pl.multiple_of(places[s] * size, LANES)
            out[at, pl.ds(to, size)] = normal[:, s * size : (s + 1) * size]


def mix_kernel(ours, theirs, near, far, tables, near_out, far_out, cosine, sine):
    count = pl.num_programs(0) // 2
    step = pl.program_id(0)
    half = near.shape[0]
    rows = jnp.where(step < count, ours[...], theirs[...])
    marks = rows[:, half : half + LANES].astype(F32)
    lane = lax.broadcasted_iota(jnp.int32, (1, LANES), 1).astype(F32)
    exact = lambda flags, table: jnp.dot(
        flags.astype(F32), table, preferred_element_type=F32, precision=lax.Precision.HIGHEST
    )
    coarse = exact(marks[:, 0:1] == lane, tables[:LANES])
    fine = exact(marks[:, 1:2] == lane, tables[LANES:])
    c = coarse[:, :LANES] * fine[:, :LANES] - coarse[:, LANES:] * fine[:, LANES:]
    s = coarse[:, LANES:] * fine[:, :LANES] + coarse[:, :LANES] * fine[:, LANES:]
    for weight, out in ((near, near_out), (far, far_out)):
        raw = dot(rows[:, :half], weight[...])
        for kind, scale in ((0, SCALE), (1, 1.0)):
            at = kind * GROUP
            a, b = spin(raw[:, at : at + GROUP], c, s, 1.0)
            out[:, at : at + LANES] = (a * scale).astype(BF)
            out[:, at + LANES : at + GROUP] = (b * scale).astype(BF)
        out[:, 2 * GROUP :] = raw[:, 2 * GROUP :].astype(BF)

    @pl.when(step % count == 0)
    def _():
        cosine[...] = c
        sine[...] = s


def attend_kernel(q0, k0, v0, q1, k1, v1, doc_row, doc_column, attended, attended_low, logs):
    turned, plain = lane_masks()
    allowed = doc_column[...] == doc_row[0]
    lane = lax.broadcasted_iota(jnp.int32, (1, LANES), 1)
    totals = jnp.zeros((q0.shape[0], LANES), F32)
    for group, (q, k, v) in enumerate(((q0, k0, v0), (q1, k1, v1))):
        queries, keys, values = q[...], k[...], v[...]
        kept = jnp.zeros(queries.shape, F32)
        for i in range(4):
            raw = outer_rows(only(turned[i], queries), keys)
            raw = jnp.where(allowed, raw, -jnp.inf)
            top = jnp.max(raw, axis=-1, keepdims=True)
            weights = jnp.exp(raw - top)
            total = jnp.sum(weights, axis=-1, keepdims=True)
            found = dot(weights.astype(BF), values) / total
            kept = jnp.where(plain[i], found, kept)
            totals = jnp.where(lane == 4 * group + i, top + jnp.log(total), totals)
        attended[:, group * GROUP : (group + 1) * GROUP] = kept
        attended_low[:, group * GROUP : (group + 1) * GROUP] = kept.astype(BF)
    logs[...] = totals


def around_kernel(grads, attended, logs, around, numbers):
    heads = HEADS // 2
    width = grads.shape[1]
    row = lax.broadcasted_iota(jnp.int32, (width, LANES), 0)
    lane = lax.broadcasted_iota(jnp.int32, (width, LANES), 1)
    low = grads[...].astype(BF)
    delta = jnp.dot(
        low.astype(F32) * attended[...],
        (row // HEAD_DIM == lane - 2 * heads).astype(F32),
        preferred_element_type=F32,
        precision=lax.Precision.HIGHEST,
    )
    both = logs[...] + delta
    numbers[...] = both
    high = both.astype(BF).astype(F32)
    around[:, :width] = low
    around[:, width:] = (high + pltpu.roll(both - high, heads, 1)).astype(BF)


def query_kernel(q0, k0, v0, q1, k1, v1, around, numbers, doc_row, doc_column, cosine, sine, d_q):
    turned, plain = lane_masks()
    allowed = doc_column[...] == doc_row[0]
    c, s = cosine[...] * SCALE, sine[...] * SCALE
    for group, (q, k, v) in enumerate(((q0, k0, v0), (q1, k1, v1))):
        queries, keys, values = q[...], k[...], v[...]
        grads = around[:, group * GROUP : (group + 1) * GROUP]
        kept = jnp.zeros(queries.shape, F32)
        for i in range(4):
            at = 4 * group + i
            raw = outer_rows(only(turned[i], queries), keys)
            weights = jnp.where(allowed, jnp.exp(raw - numbers[:, at : at + 1]), 0.0)
            d_weights = outer_rows(only(plain[i], grads), values)
            d_raw = (weights * (d_weights - numbers[:, 16 + at : 17 + at])).astype(BF)
            kept = jnp.where(turned[i], dot(d_raw, keys), kept)
        a, b = spin(kept, c, s, -1.0)
        d_q[:, group * GROUP : group * GROUP + LANES] = a.astype(BF)
        d_q[:, group * GROUP + LANES : (group + 1) * GROUP] = b.astype(BF)


def key_kernel(q0, k0, v0, q1, k1, v1, d_q, doc_row, doc_column, cosine, sine, *refs):
    *around, near, far = refs
    turned, plain = lane_masks()
    rows = k0.shape[0]
    c, s = cosine[...], sine[...]
    column = doc_column[...]
    kept = [[jnp.zeros(k0.shape, F32), jnp.zeros(k0.shape, F32)] for _ in (0, 1)]
    for j, block in enumerate(around):
        part = slice(j * rows, (j + 1) * rows)
        allowed = column == doc_row[0, :, part]
        numbers = block[:, 2 * GROUP :].astype(F32)
        numbers = (numbers + pltpu.roll(numbers, LANES - HEADS // 2, 1)).T
        for group, (q, k, v) in enumerate(((q0, k0, v0), (q1, k1, v1))):
            queries, keys, values = q[part, :], k[...], v[...]
            grads = block[:, group * GROUP : (group + 1) * GROUP]
            add_k = jnp.zeros(k0.shape, F32)
            add_v = jnp.zeros(k0.shape, F32)
            for i in range(4):
                at = 4 * group + i
                raw = outer_rows(only(turned[i], keys), queries)
                weights = jnp.where(allowed, jnp.exp(raw - numbers[at : at + 1, :]), 0.0)
                add_v = jnp.where(plain[i], dot(weights.astype(BF), grads), add_v)
                d_weights = outer_rows(only(plain[i], values), grads)
                d_raw = (weights * (d_weights - numbers[16 + at : 17 + at, :])).astype(BF)
                add_k = jnp.where(turned[i], dot(d_raw, queries), add_k)
            kept[group][0] += add_k
            kept[group][1] += add_v
    for group, out in enumerate((near, far)):
        a, b = spin(kept[group][0], c, s, -1.0)
        out[:, :GROUP] = d_q[:, group * GROUP : (group + 1) * GROUP]
        out[:, GROUP : GROUP + LANES] = a.astype(BF)
        out[:, GROUP + LANES : 2 * GROUP] = b.astype(BF)
        out[:, 2 * GROUP :] = kept[group][1].astype(BF)


def pack_kernel(place, active, grads, attended, branch, near, far):
    count, depth = near.shape[0], attended.shape[1] // near.shape[0]
    rows = active.shape[1] // count
    wide = near.shape[2]
    for i in (0, 1):
        one = inner_rows(active[...], grads[:, i * wide : (i + 1) * wide]).astype(BF)
        two = inner_rows(attended[...], branch[i]).astype(BF)

        def store(out):
            for s in range(count):
                out[s, :rows] = one[s * rows : (s + 1) * rows]
                at = s * depth
                out[s, rows:, :GROUP] = two[at : at + depth // 2]
                out[s, rows:, GROUP:] = two[at + depth // 2 : at + depth]

        @pl.when(place[0] == i)
        def _():
            store(near)

        @pl.when(place[0] != i)
        def _():
            store(far)


def place_kernel(rest, one_low, one_high, two_low, two_high, weight, gain, grads, gains):
    length, half, rows, pad = rest
    full = weight.shape[1] // 2
    for i, pair in enumerate(((one_low, two_low), (one_high, two_high))):
        for s in range(length):
            for c, share in enumerate(pair):
                size = min(half, rows - c * half)
                at = i * full + s * rows + c * half
                grads[:, at : at + size] = share[:, s * pad : s * pad + size].astype(F32)
    raw = grads[...]
    total = jnp.sum(raw * weight[...].astype(F32), axis=1, keepdims=True)
    gains[...] = jnp.broadcast_to(total, gains.shape)
    grads[...] = raw * gain[...]


def call_kernel(kernel, ins, outs, grid=1, room=40, micros=5):
    spec = lambda block, at: (
        pl.BlockSpec(memory_space=pltpu.SMEM) if block is None else pl.BlockSpec(block, at)
    )
    return pl.pallas_call(
        kernel,
        grid=(grid,),
        in_specs=[spec(block, at) for _, block, at in ins],
        out_specs=tuple(pl.BlockSpec(block, at) for _, _, block, at in outs),
        out_shape=tuple(jax.ShapeDtypeStruct(shape, kind) for shape, kind, _, _ in outs),
        compiler_params=pltpu.CompilerParams(vmem_limit_bytes=room * 2**20),
        cost_estimate=pl.CostEstimate(flops=micros * 10**9, bytes_accessed=1, transcendentals=0),
    )(*[a for a, _, _ in ins])


def gelu_parts(inner):
    share = 0.5 * (1.0 + lax.erf(inner * 0.7071067811865476))
    return inner * share, share + inner * (0.3989422804014327 * jnp.exp(-0.5 * inner * inner))


def hidden_kernel(marks, rows, grads, pair, other, shrink_pair, shrink_other, *refs):
    active, lifted_grads, out, out_there, d_rows, d_there = refs[:6]
    expand_w, shrink_w, semaphore = refs[6:]
    units = shrink_w.shape[0]
    half = pair.shape[0] // 2
    wide = shrink_pair.shape[1]
    places = marks.shape[0] - 2
    block = units // places
    front = marks[0] == 1
    x = marks[1]
    step = pl.program_id(0)

    def weights(source, start, at, row):
        return source.at[pl.ds(start, half)], expand_w.at[at, pl.ds(row, half)]

    def shrinks(source, high, at, low):
        found = []
        for j in range(places // 2):
            start = high * (source.shape[0] // 2) + j * block
            row = pl.multiple_of(marks[2 + low * (places // 2) + j], 16)
            column = pl.multiple_of(at * wide, LANES)
            found.append(
                (
                    source.at[pl.ds(start, block)],
                    shrink_w.at[pl.ds(row, block), pl.ds(column, wide)],
                )
            )
        return found

    def begin(moves, first):
        copies = [
            pltpu.make_async_copy(a, b, semaphore.at[first + k]) for k, (a, b) in enumerate(moves)
        ]
        for copy in copies:
            copy.start()
        return copies

    @pl.when(step == 0)
    def _():
        moves = [weights(pair, 0, x, 0), weights(other, half, 1 - x, half)]
        moves += shrinks(shrink_pair, 0, x, 0) + shrinks(shrink_other, 1, 1 - x, 1)
        copies = begin(moves, 0)
        for flag, low, high in ((front, other, pair), (jnp.logical_not(front), pair, other)):

            @pl.when(flag)
            def _():
                start = 0 if low is other else half
                back = half - start
                shrink_low = shrink_other if low is other else shrink_pair
                shrink_high = shrink_pair if low is other else shrink_other
                crossed = [weights(low, start, x, half), weights(high, back, 1 - x, 0)]
                crossed += shrinks(shrink_low, start // half, x, 1)
                crossed += shrinks(shrink_high, back // half, 1 - x, 0)
                for copy in begin(crossed, len(moves)):
                    copy.wait()

        for copy in copies:
            copy.wait()

    values, dy = rows[...], grads[...]
    tile = 256
    for at in range(0, units, tile):
        cut = slice(at, min(at + tile, units))
        inner = dot(values, expand_w[0, :, cut])
        gate = dot(values, expand_w[1, :, cut])
        d_active = outer_rows(dy, shrink_w[cut, :])
        value, slope = gelu_parts(inner)
        active[:, cut] = (value * gate).astype(BF)
        lifted_grads[x, :, cut] = (d_active * gate * slope).astype(BF)
        lifted_grads[1 - x, :, cut] = (d_active * value).astype(BF)
    result = dot(active[...], shrink_w[...])
    back = outer_rows(lifted_grads[x], expand_w[0]) + outer_rows(lifted_grads[1 - x], expand_w[1])

    @pl.when(step == 0)
    def _():
        out[...] = result
        d_rows[...] = back

    @pl.when(step == 1)
    def _():
        out_there[...] = result.astype(BF)
        d_there[...] = back.astype(BF)


def hidden(marks, rows, grads, expand, shrink):
    count, width = rows.shape
    units = expand[0].shape[1]
    size = count // 2
    moving = lambda i: (i, 0)
    still = lambda i: (0, 0)
    held = pl.BlockSpec(memory_space=pl.ANY)
    outs = [
        ((count, units), BF, (size, units), moving),
        ((2, count, units), BF, (2, size, units), lambda i: (0, i, 0)),
        ((size, width), F32, (size, width), still),
        ((size, width), BF, (size, width), still),
        ((size, width), F32, (size, width), still),
        ((size, width), BF, (size, width), still),
    ]
    return pl.pallas_call(
        hidden_kernel,
        grid=(2,),
        in_specs=[pl.BlockSpec(memory_space=pltpu.SMEM)]
        + [pl.BlockSpec((size, width), moving)] * 2
        + [held] * 4,
        out_specs=tuple(pl.BlockSpec(block, at) for _, _, block, at in outs),
        out_shape=tuple(jax.ShapeDtypeStruct(shape, kind) for shape, kind, _, _ in outs),
        scratch_shapes=[
            pltpu.VMEM((2, width, units), BF),
            pltpu.VMEM((units, width), BF),
            pltpu.SemaphoreType.DMA((2 * marks.shape[0],)),
        ],
        compiler_params=pltpu.CompilerParams(vmem_limit_bytes=36 * 2**20),
        cost_estimate=pl.CostEstimate(flops=8 * 10**9, bytes_accessed=1, transcendentals=0),
    )(marks, rows, grads, *expand, *shrink)


def on_device(
    direct,
    tokens,
    norm_first,
    joint_weight,
    output_weight,
    norm_second,
    expand_weight,
    shrink_weight,
    document_start,
    cotangent,
):
    rows, width = tokens.shape
    plan = Direct() if direct else Plain(rows)
    length = lax.axis_size("seq")
    here = lax.axis_index("seq")
    x, core = plan.x, plan.core
    near_x = x == 0
    depth = joint_weight.shape[0]
    unit_rows = shrink_weight.shape[0]
    unit_half = (unit_rows + 1) // 2
    units = -(-unit_half * length // LANES) * LANES
    while units % length:
        units += LANES
    unit_pad = units // length
    half_width = width // 2

    def mine(array, start):
        parts = [array[:, start + i * GROUP : start + (i + 1) * GROUP] for i in range(4)]
        low, high = pick(near_x, parts[0::2], parts[1::2])
        return jnp.where(core == 0, low, high)

    source = jnp.arange(GROUP)
    turn = (
        source[:, None]
        == ((source % LANES) // 32 * HEAD_DIM + source // LANES * 32 + source % 32)[None, :]
    ).astype(BF)
    gain_one = norm_first.astype(F32)[:, None]
    gain_two = norm_second.astype(F32)[:, None]
    joint_piece = jnp.concatenate(
        [
            (dot(mine(joint_weight, 0), turn) * gain_one).astype(BF),
            (dot(mine(joint_weight, width), turn) * gain_one).astype(BF),
            (mine(joint_weight, 2 * width).astype(F32) * gain_one).astype(BF),
            mine(output_weight, 0),
        ],
        axis=1,
    )
    slot = jnp.arange(units)
    inner = core * unit_half + slot % unit_pad
    fits = (slot % unit_pad < unit_half) & (inner < unit_rows)
    unit_of = jnp.where(fits, slot // unit_pad * unit_rows + inner, -2 * FF)
    spread_units = (jnp.arange(2 * FF)[:, None] == (unit_of + x * FF)[None, :]).astype(BF)
    expand_piece = (dot(expand_weight, spread_units) * gain_two).astype(BF)
    slot_row = jnp.arange(unit_pad)

    def picked(c):
        row = c * unit_half + slot_row
        row = jnp.where((slot_row < unit_half) & (row < unit_rows), row, -1)
        return (row[:, None] == jnp.arange(unit_rows)[None, :]).astype(BF)

    shrink_piece = dot(
        picked(core),
        jnp.where(near_x, shrink_weight[:, :half_width], shrink_weight[:, half_width:]),
    ).astype(BF)

    anchor = (lax.axis_index("rep") * length + here) * rows
    position = anchor + jnp.arange(rows, dtype=jnp.int32) - document_start
    marks = jnp.pad(
        jnp.stack([(position + 1) // 16, (position + 1) % 16], axis=1), ((0, 0), (0, LANES - 2))
    ).astype(BF)
    packed = jnp.concatenate([tokens, marks], axis=1)
    joint = Chain(plan, plan.gather(joint_piece, True))
    near_tokens = Chain(plan, plan.around(packed))
    joint.step(3)
    expand = Chain(plan, plan.gather(gate(expand_piece, *joint.operands), False))
    joint.step(2)
    blocks, offsets = near_tokens.end()
    expand.step(2)
    shrink = Chain(plan, plan.gather(gate(shrink_piece, *expand.operands), False))
    block_count = len(blocks)
    span = block_count * rows
    still = lambda i: (0, 0)
    moving = lambda i: (i, 0)
    (sent,) = call_kernel(
        prepare_kernel,
        [(plan.columns(width // depth), None, None)]
        + [(block, (rows, width + LANES), still) for block in blocks],
        [((span, width + LANES), BF, (span, width + LANES), still)],
        micros=2,
    )
    first = (sent, swap_core(sent))
    offset_rows = jnp.stack([jnp.int32(offset) for offset in offsets]) * rows
    index = (here * rows + offset_rows[:, None] + jnp.arange(rows)[None, :]).reshape(1, span)
    document_rows = []
    for rows_in in first:
        code = rows_in[:, width : width + 2].astype(F32).T
        code = code[:1] * 16.0 + code[1:]
        document_rows.append(jnp.where(code > 0, index.astype(F32) - (code - 1.0), FAR))
    document_row = jnp.stack(document_rows)
    document_column = jnp.concatenate([row[:, :rows] for row in document_rows], axis=1).T
    halves_of_head = HEAD_DIM // 2
    frequency = THETA ** (-(jnp.arange(halves_of_head, dtype=F32) * 2.0) / HEAD_DIM)
    frequency = jnp.tile(frequency, LANES // halves_of_head)[None, :]
    steps = jnp.arange(LANES, dtype=F32)[:, None]
    angle = jnp.concatenate([16.0 * steps * frequency, (steps - 1.0) * frequency], axis=0)
    tables = jnp.concatenate([jnp.cos(angle), jnp.sin(angle)], axis=1)

    joint_near, joint_far = halves(plan.front, *joint.value)
    output_mine = jnp.concatenate([joint_near[:, 3 * GROUP :], joint_far[:, 3 * GROUP :]], axis=1)
    output_all = jnp.concatenate([output_mine, swap_core(output_mine)], axis=1)

    def turn_columns(array):
        parts = [array[:, i * GROUP : (i + 1) * GROUP] for i in range(4)]
        parts = pick(core == 0, parts, parts[2:] + parts[:2])
        left, right = pick(near_x, parts[:2], parts[1::-1]), pick(near_x, parts[2:], parts[:1:-1])
        return jnp.concatenate(left + right, axis=-1)

    wide = 3 * GROUP
    *mixed, cosine, sine = call_kernel(
        mix_kernel,
        [
            (first[0], (rows, width + LANES), lambda i: (jnp.minimum(i, block_count - 1), 0)),
            (first[1], (rows, width + LANES), lambda i: (jnp.maximum(i - block_count, 0), 0)),
            (joint_near, (width, wide), still),
            (joint_far, (width, wide), still),
            (tables, (2 * LANES, 2 * LANES), still),
        ],
        [((2 * span, wide), BF, (rows, wide), moving)] * 2
        + [((2 * rows, LANES), F32, (rows, LANES), lambda i: (i // block_count, 0))] * 2,
        2 * block_count,
        micros=7,
    )
    expand.step()
    shrink.step(2)
    document_row = gate(document_row, *expand.operands)
    column = lambda kind, every: (
        ((span, GROUP), lambda i: (i, kind))
        if every
        else ((rows, GROUP), lambda i: (i * block_count, kind))
    )
    wide_keys = [
        (array, *column(kind, kind > 0)) for array in mixed for kind in range(3)
    ]
    wide_queries = [
        (array, *column(kind, kind == 0)) for array in mixed for kind in range(3)
    ]
    documents = [
        (document_row, (1, 1, span), lambda i: (i, 0, 0)),
        (document_column, (rows, 1), moving),
    ]
    both = lambda w, kind: ((2 * rows, w), kind, (rows, w), moving)
    attended, attended_low, logs = call_kernel(
        attend_kernel,
        wide_keys + documents,
        [both(2 * GROUP, F32), both(2 * GROUP, BF), both(LANES, F32)],
        2,
        micros=5,
    )
    shrink.step()
    shrink.step()
    expand_both = expand.end()
    attended_there = gate(swap_core(attended_low), *expand_both)
    attended_there = jnp.concatenate([attended_there[rows:], attended_there[:rows]], axis=0)
    attended_rows = plan.order(
        turn_columns(jnp.concatenate([attended_low, attended_there], axis=1)), depth
    )
    middle = tokens.astype(F32) + turn_columns(dot(attended_rows[:rows], output_all))
    second, second_scale = centre(middle)
    second_low = plan.order(second.astype(BF), depth)
    second_both = jnp.concatenate([second_low, swap_core(second_low)], axis=0)
    shrink_both = shrink.end()

    cotangents = jnp.concatenate([cotangent, swap_core(gate(cotangent, attended_low))], axis=0)

    where = jnp.stack(
        [plan.front.astype(jnp.int32), x.astype(jnp.int32)]
        + [row.astype(jnp.int32) for row in plan.rows_of(unit_pad)]
    )
    active_low, lifted_grads, out, out_there, second_grad, second_there = hidden(
        where, second_both, cotangents, expand_both, shrink_both
    )
    expand = Chain(plan, plan.reduce(second_both, lifted_grads[0], lifted_grads[1], False))
    result = middle + out + swap_core(out_there).astype(F32)
    second_grad = second_grad + swap_core(second_there).astype(F32)
    middle_grad = cotangent.astype(F32) + centre_back(
        second, second_scale, plan.restore(second_grad, depth)
    )
    branch = middle_grad.astype(BF)
    branch_both = turn_columns(jnp.concatenate([branch, swap_core(branch)], axis=0))
    attended_grad = turn_columns(plan.restore(outer_rows(branch_both, output_all), depth))
    around, numbers = call_kernel(
        around_kernel,
        [
            (attended_grad[:, : 2 * GROUP], (rows, 2 * GROUP), moving),
            (attended, (rows, 2 * GROUP), moving),
            (logs, (rows, LANES), moving),
        ],
        [both(2 * GROUP + LANES, BF), both(LANES, F32)],
        2,
    )
    near_grads = Chain(plan, plan.around(around))
    branch_sides = jnp.stack(
        pick(near_x, *[[branch_both[:, i * GROUP : (i + 1) * GROUP] for i in o] for o in ((0, 1), (1, 0))])
    )
    kinds = [
        ((length, unit_pad + depth // 2, half_width), BF),
        (length, unit_pad + depth // 2, half_width),
        lambda i: (0, 0, 0),
    ]
    sums = call_kernel(
        pack_kernel,
        [
            (x.astype(jnp.int32)[None], None, 0),
            (active_low, (2 * rows, units), still),
            (cotangents, (2 * rows, width), still),
            (plan.restore(attended_rows, depth), (2 * rows, width), still),
            (branch_sides, (2, 2 * rows, GROUP), lambda i: (0, 0, 0)),
        ],
        [(*kinds[0], kinds[1], kinds[2])] * 2,
    )
    near_grads.step(2)
    shrink = Chain(plan, plan.reduce_blocks(*sums))
    turning = [(cosine, (rows, LANES), moving), (sine, (rows, LANES), moving)]
    (query_grad,) = call_kernel(
        query_kernel,
        wide_keys
        + [
            (around, (rows, 2 * GROUP), moving),
            (numbers, (rows, LANES), moving),
        ]
        + documents
        + turning,
        [both(2 * GROUP, BF)],
        2,
        micros=13,
    )
    expand.step()
    arounds, _ = near_grads.end()
    mixed_grads = call_kernel(
        key_kernel,
        wide_queries
        + [(query_grad, (rows, 2 * GROUP), moving)]
        + documents
        + turning
        + [(block, (rows, 2 * GROUP + LANES), moving) for block in arounds],
        [both(wide, BF), both(wide, BF)],
        2,
        micros=16,
    )
    own_first = jnp.concatenate([rows_in[:rows, :width] for rows_in in first], axis=0)
    joint = Chain(plan, plan.reduce(own_first, *mixed_grads, True))
    expand.step()
    shrink.step()
    joint.step()
    moved = joint.operands + expand.operands
    expand.hold(*moved)
    shrink.hold(*moved)
    first_part = outer_rows(mixed_grads[0], joint_near[:, :wide]) + outer_rows(
        mixed_grads[1], joint_far[:, :wide]
    )
    first_grad = first_part[:rows] + swap_core(first_part[rows:].astype(BF)).astype(F32)
    normal, normal_scale = centre(tokens.astype(F32))
    tokens_grad = middle_grad + centre_back(
        normal, normal_scale, plan.restore(first_grad, depth)
    )

    expand.step()
    shrink.hold(*expand.operands)
    shrink.step()
    joint.step()
    waits = joint.operands
    expand.step()
    shrink.hold(*waits, *expand.operands)
    expand.step()
    joint.step(3)
    shrink.step()
    expand_shares = expand.end()
    share_parts = [share for pair in expand_shares for share in pair]
    expand_grad, second_gains = call_kernel(
        functools.partial(place_kernel, (length, unit_half, unit_rows, unit_pad)),
        [(part, (depth, units), still) for part in share_parts]
        + [(expand_weight, (depth, 2 * FF), still), (gain_two, (depth, 1), still)],
        [
            ((depth, 2 * FF), F32, (depth, 2 * FF), still),
            ((depth, LANES), F32, (depth, LANES), still),
        ],
        micros=3,
    )
    second_gain_grad = second_gains[:, 0]
    shrink.step()
    joint.step()
    joint.hold(expand_grad)
    shrink_shares = shrink.end()
    joint_four = joint.end()

    shrink_grad = jnp.concatenate(
        [
            inner_rows(picked(0), shrink_shares[0][i][:unit_pad])
            + inner_rows(picked(1), shrink_shares[1][i][:unit_pad])
            for i in (0, 1)
        ],
        axis=1,
    )
    output_grad = []
    for pair in shrink_shares:
        for share in pair:
            share = share[unit_pad:]
            output_grad.append(jnp.concatenate([share[:, :GROUP], share[:, GROUP:]], axis=0))
    output_grad = jnp.concatenate(output_grad, axis=1).astype(F32)
    columns = []
    for kind in range(3):
        for c in (0, 1):
            for i in (0, 1):
                piece = joint_four[c][i][:, kind * GROUP : (kind + 1) * GROUP]
                columns.append(outer_rows(piece, turn) if kind < 2 else piece.astype(F32))
    joint_raw = jnp.concatenate(columns, axis=1)
    joint_grad = joint_raw * gain_one
    first_gain_grad = jnp.sum(joint_raw * joint_weight.astype(F32), axis=1)
    return (
        result.astype(BF),
        tokens_grad.astype(BF),
        first_gain_grad,
        joint_grad,
        output_grad,
        second_gain_grad,
        expand_grad,
        shrink_grad,
    )


def solution(mesh):
    placed = (
        P(("rep", "seq"), None),
        P("seq"),
        P("seq", None),
        P("seq", None),
        P("seq"),
        P("seq", None),
        P("seq", None),
        P(("rep", "seq")),
        P(("rep", "seq"), None),
    )
    return jax.shard_map(
        functools.partial(on_device, mesh.shape["seq"] == 8),
        mesh=mesh,
        in_specs=placed,
        out_specs=(
            P(("rep", "seq"), None),
            P(("rep", "seq"), None),
            P("seq"),
            P("seq", None),
            P("seq", None),
            P("seq"),
            P("seq", None),
            P("seq", None),
        ),
        check_vma=False,
    )
```

```python
import functools

import jax
import jax.numpy as jnp
from jax import lax
from jax.experimental import pallas as pl
from jax.experimental.pallas import tpu as pltpu
from jax.sharding import PartitionSpec as P

HEADS = 16
HEAD_DIM = 64
FF = 2624
HALO = 512
EPSILON = 1e-05
THETA = 160000.0
SCALE = 0.125
LANES = 128
GROUP = 256
FAR = -1e6
LONG = 10**11
BF = jnp.bfloat16
F32 = jnp.float32


def dot(left, right):
    return jnp.dot(left, right, preferred_element_type=F32)


def inner_rows(left, right):
    return lax.dot_general(left, right, (((0,), (0,)), ((), ())), preferred_element_type=F32)


def outer_rows(left, right):
    return lax.dot_general(left, right, (((1,), (1,)), ((), ())), preferred_element_type=F32)


def pick(flag, one, two):
    return [jnp.where(flag, a, b) for a, b in zip(one, two)]


def centre(rows):
    middle = jnp.mean(rows, axis=-1, keepdims=True)
    centered = rows - middle
    spread = jnp.mean(centered * centered, axis=-1, keepdims=True)
    scale = lax.rsqrt(spread + EPSILON)
    return centered * scale, scale


def centre_back(normal, scale, grads):
    return scale * (
        grads
        - jnp.mean(grads, axis=-1, keepdims=True)
        - normal * jnp.mean(grads * normal, axis=-1, keepdims=True)
    )


def two_parts(values):
    high = lax.reduce_precision(values, 8, 7)
    return high.astype(BF), (values - high).astype(BF)


def swap_core(array):
    return lax.ppermute(array, "rep", [(i, i ^ 1) for i in range(lax.axis_size("rep"))])


def swap_far(array):
    return lax.ppermute(array, "rep", [(i, i ^ 2) for i in range(lax.axis_size("rep"))])


class Moves:
    def __init__(self):
        self.recent = []

    def send(self, array, axes, route):
        self.recent.append(array)
        return lax.ppermute(array, axes, route)

    def across(self, array, flip):
        return self.send(array, "rep", [(i, i ^ flip) for i in range(lax.axis_size("rep"))])

    def given(self):
        found, self.recent = self.recent, []
        return found


class Direct(Moves):
    depth = 4

    def __init__(self):
        super().__init__()
        self.place = lax.axis_index("seq")
        self.z = self.place // 2
        self.y = self.place % 2
        self.x = lax.axis_index("rep") // 2
        self.core = lax.axis_index("rep") % 2
        self.front = self.core == 0

    def along(self, array, flip):
        route = [(s, s ^ (2 * flip)) for s in range(2 * self.depth)]
        return self.send(array, "seq", route)

    def cross(self, array, turn):
        n = 2 * self.depth
        route = []
        for r in range(4):
            for s in range(n):
                to = (r ^ 2, s) if r % 2 == turn else (r, s ^ 1)
                route.append((r * n + s, to[0] * n + to[1]))
        return self.send(array, ("rep", "seq"), route)

    def around(self, array):
        rows = array.shape[0]
        last = 2 * self.depth
        low = self.send(array, "seq", [(s, s + 2) for s in range(last - 2)])
        high = self.send(array, "seq", [(s, s - 2) for s in range(2, last)])
        low = yield low
        high = yield high
        sent = jnp.concatenate([array, jnp.where(self.y == 0, high, low)], axis=0)
        beside = yield self.send(sent, "seq", [(s, s ^ 1) for s in range(last)])
        step = 1 - 2 * self.y
        return [array, low, high, beside[:rows], beside[rows:]], [0, -2, 2, step, -step]

    def gather(self, piece, at_once):
        if at_once:
            sent = [self.along(piece, k) for k in (1, 2, 3)]
            found = [piece]
            for array in sent:
                array = yield array
                found.append(array)
            rows = jnp.concatenate(found, axis=0)
        else:
            there = yield self.along(piece, 1)
            pair = jnp.concatenate([piece, there], axis=0)
            there = yield self.along(pair, 2)
            rows = jnp.concatenate([pair, there], axis=0)
        once = yield self.cross(rows, 0)
        pair = jnp.concatenate([rows, once], axis=0)
        other = yield self.cross(pair, 1)
        return pair, other

    def to_near(self, grid):
        turned = [pick(self.y == 0, pair, pair[::-1]) for pair in grid]
        near = []
        for y in (0, 1):
            a, b, c, d = [pair[y] for pair in turned]
            a, b, c, d = pick(self.z % 2 == 0, [a, b, c, d], [b, a, d, c])
            near.append(pick(self.z // 2 == 0, [a, b, c, d], [c, d, a, b]))
        return near

    def to_mesh(self, near):
        lines = []
        for a, b, c, d in near:
            a, b, c, d = pick(self.z % 2 == 0, [a, b, c, d], [b, a, d, c])
            lines.append(pick(self.z // 2 == 0, [a, b, c, d], [c, d, a, b]))
        return [pick(self.y == 0, list(pair), list(pair)[::-1]) for pair in zip(*lines)]

    def rows_of(self, size):
        return [
            (2 * (self.z ^ k) + (self.y ^ y)) * size for y in (0, 1) for k in range(self.depth)
        ]

    def columns(self, count):
        z, y = jnp.arange(count) // 2, jnp.arange(count) % 2
        return (4 * (y ^ self.y) + (z ^ self.z)).astype(jnp.int32)

    def order(self, array, size):
        n = self.depth
        cut = lambda s: array[..., s * size : (s + 1) * size]
        near = self.to_near([[cut(2 * z), cut(2 * z + 1)] for z in range(n)])
        return jnp.concatenate(near[0] + near[1], axis=-1)

    def restore(self, array, size):
        n = self.depth
        cut = lambda j: array[..., j * size : (j + 1) * size]
        grid = self.to_mesh([[cut(n * y + k) for k in range(n)] for y in (0, 1)])
        return jnp.concatenate([part for pair in grid for part in pair], axis=-1)

    def down(self, mine, at_once):
        rows = mine.shape[0] // 4
        cut = lambda k, n: mine[k * rows : (k + n) * rows]
        if at_once:
            sent = [self.along(cut(k, 1), k) for k in (1, 2, 3)]
            total = cut(0, 1).astype(F32)
            for array in sent:
                array = yield array
                total = total + array.astype(F32)
            share = total.astype(BF)
        else:
            there = yield self.along(cut(2, 2), 2)
            pair = (cut(0, 2).astype(F32) + there.astype(F32)).astype(BF)
            there = yield self.along(pair[rows:], 1)
            share = (pair[:rows].astype(F32) + there.astype(F32)).astype(BF)
        return (yield from self.spread(share))

    def reduce(self, left, near, far, at_once):
        half = left.shape[1] // 2
        top, bottom = left[:, :half], left[:, half:]
        sent = lax.dot_general(
            jnp.stack([jnp.where(self.front, bottom, top), bottom]),
            jnp.stack([jnp.where(self.front, near, far), far]),
            (((1,), (1,)), ((0,), (0,))),
            preferred_element_type=F32,
        ).astype(BF)
        back = yield self.cross(sent, 1)
        once = inner_rows(jnp.where(self.front, top, bottom), jnp.where(self.front, far, near))
        once_in = yield self.cross((once + back[1]).astype(BF), 0)
        mine = (inner_rows(top, near) + back[0] + once_in).astype(BF)
        return (yield from self.down(mine, at_once))

    def reduce_blocks(self, near, far):
        back = yield self.across(far, 2)
        total = (near.astype(F32) + back.astype(F32)).astype(BF)
        lines = self.to_near([total[2 * z : 2 * z + 2] for z in range(self.depth)])
        mine, sent = [jnp.concatenate(line, axis=0) for line in lines]
        route = [(s, s ^ 1) for s in range(2 * self.depth)]
        back = yield self.send(sent, "seq", route)
        mine = (mine.astype(F32) + back.astype(F32)).astype(BF)
        return (yield from self.down(mine, False))

    def spread(self, share):
        there = yield self.across(share, 2)
        pair = [share, there]
        low, high = pick(self.x == 0, pair, pair[::-1])
        both = jnp.concatenate([low, high], axis=1)
        there = yield self.across(both, 1)
        size = share.shape[1]
        cores = pick(self.core == 0, [both, there], [there, both])
        return [[part[:, :size], part[:, size:]] for part in cores]


class Plain(Moves):
    def __init__(self, rows):
        super().__init__()
        self.rows = rows
        self.x = lax.axis_index("rep") // 2
        self.core = lax.axis_index("rep") % 2
        self.front = jnp.bool_(True)

    def around(self, array):
        length = lax.axis_size("seq")
        reach = min(HALO // self.rows, length - 1)
        blocks, offsets = [array], [0]
        for offset in list(range(-reach, 0)) + list(range(1, reach + 1)):
            route = [(i + offset, i) for i in range(length) if 0 <= i + offset < length]
            blocks.append((yield self.send(array, "seq", route)))
            offsets.append(offset)
        return blocks, offsets

    def gather(self, piece, at_once):
        near = yield lax.all_gather(piece, "seq", axis=0, tiled=True)
        far = yield self.across(near, 2)
        half = near.shape[0] // 2
        return (
            jnp.concatenate([near[:half], far[:half]], axis=0),
            jnp.concatenate([near[half:], far[half:]], axis=0),
        )

    def rows_of(self, size):
        return [jnp.int32(0), jnp.int32(lax.axis_size("seq") // 2 * size)]

    def columns(self, count):
        return jnp.zeros((1,), jnp.int32)

    def order(self, array, size):
        return array

    def restore(self, array, size):
        return array

    def reduce(self, left, near, far, at_once=False):
        back = yield self.across(inner_rows(left, far).astype(BF), 2)
        mine = inner_rows(left, near) + back
        share = lax.psum_scatter(mine, "seq", scatter_dimension=0, tiled=True).astype(BF)
        return (yield from self.spread(share))

    def reduce_blocks(self, near, far):
        back = yield self.across(far, 2)
        mine = (near.astype(F32) + back).reshape(-1, near.shape[2])
        share = lax.psum_scatter(mine, "seq", scatter_dimension=0, tiled=True).astype(BF)
        return (yield from self.spread(share))

    spread = Direct.spread


def gate(array, *earlier):
    return lax.optimization_barrier((array,) + earlier)[0]


class Chain:
    def __init__(self, plan, steps):
        self.plan, self.steps = plan, steps
        self.value = None
        self.sent = next(steps)
        self.operands = tuple(plan.given())

    def hold(self, *earlier):
        if self.sent is not None:
            self.sent = gate(self.sent, *earlier)

    def step(self, count=1):
        for _ in range(count):
            if self.sent is not None:
                try:
                    self.sent = self.steps.send(self.sent)
                except StopIteration as end:
                    self.sent, self.value = None, end.value
                self.operands = tuple(self.plan.given())

    def end(self):
        while self.sent is not None:
            self.step()
        return self.value


def halves(front, pair, other):
    half = pair.shape[0] // 2
    one, two = pair[half:], other[:half]
    near = jnp.concatenate([pair[:half], jnp.where(front, two, one)], axis=0)
    far = jnp.concatenate([jnp.where(front, one, two), other[half:]], axis=0)
    return near, far


def lane_masks():
    lane = lax.broadcasted_iota(jnp.int32, (1, GROUP), 1)
    turned = [(lane % LANES) // (HEAD_DIM // 2) == i for i in range(4)]
    plain = [lane // HEAD_DIM == i for i in range(4)]
    return turned, plain


def only(mask, array):
    return jnp.where(mask, array, jnp.zeros_like(array))


def spin(raw, c, s, way):
    a, b = raw[:, :LANES], raw[:, LANES:]
    return a * c - way * (b * s), b * c + way * (a * s)


def prepare_kernel(places, *refs):
    *blocks, out = refs
    width = blocks[0].shape[1] - LANES
    rows = out.shape[0] // len(blocks)
    count = places.shape[0]
    size = width // count
    for i, block in enumerate(blocks):
        normal = centre(block[:, :width].astype(F32))[0].astype(BF)
        at = slice(i * rows, (i + 1) * rows)
        out[at, width:] = block[:, width:]
        for s in range(count):
            to = pl.multiple_of(places[s] * size, LANES)
            out[at, pl.ds(to, size)] = normal[:, s * size : (s + 1) * size]


def mix_kernel(ours, theirs, near, far, tables, near_out, far_out, cosine, sine):
    count = pl.num_programs(0) // 2
    step = pl.program_id(0)
    half = near.shape[0]
    rows = jnp.where(step < count, ours[...], theirs[...])
    marks = rows[:, half : half + LANES].astype(F32)
    lane = lax.broadcasted_iota(jnp.int32, (1, LANES), 1).astype(F32)
    exact = lambda flags, table: jnp.dot(
        flags.astype(F32), table, preferred_element_type=F32, precision=lax.Precision.HIGHEST
    )
    coarse = exact(marks[:, 0:1] == lane, tables[:LANES])
    fine = exact(marks[:, 1:2] == lane, tables[LANES:])
    c = coarse[:, :LANES] * fine[:, :LANES] - coarse[:, LANES:] * fine[:, LANES:]
    s = coarse[:, LANES:] * fine[:, :LANES] + coarse[:, :LANES] * fine[:, LANES:]
    for weight, out in ((near, near_out), (far, far_out)):
        raw = dot(rows[:, :half], weight[...])
        for kind, scale in ((0, SCALE), (1, 1.0)):
            at = kind * GROUP
            a, b = spin(raw[:, at : at + GROUP], c, s, 1.0)
            out[:, at : at + LANES] = (a * scale).astype(BF)
            out[:, at + LANES : at + GROUP] = (b * scale).astype(BF)
        out[:, 2 * GROUP :] = raw[:, 2 * GROUP :].astype(BF)

    @pl.when(step % count == 0)
    def _():
        cosine[...] = c
        sine[...] = s


def attend_kernel(q0, k0, v0, q1, k1, v1, doc_row, doc_column, attended, attended_low, logs):
    turned, plain = lane_masks()
    allowed = doc_column[...] == doc_row[0]
    lane = lax.broadcasted_iota(jnp.int32, (1, LANES), 1)
    totals = jnp.zeros((q0.shape[0], LANES), F32)
    for group, (q, k, v) in enumerate(((q0, k0, v0), (q1, k1, v1))):
        queries, keys, values = q[...], k[...], v[...]
        kept = jnp.zeros(queries.shape, F32)
        for i in range(4):
            raw = outer_rows(only(turned[i], queries), keys)
            raw = jnp.where(allowed, raw, -jnp.inf)
            top = jnp.max(raw, axis=-1, keepdims=True)
            weights = jnp.exp(raw - top)
            total = jnp.sum(weights, axis=-1, keepdims=True)
            found = dot(weights.astype(BF), values) / total
            kept = jnp.where(plain[i], found, kept)
            totals = jnp.where(lane == 4 * group + i, top + jnp.log(total), totals)
        attended[:, group * GROUP : (group + 1) * GROUP] = kept
        attended_low[:, group * GROUP : (group + 1) * GROUP] = kept.astype(BF)
    logs[...] = totals


def around_kernel(grads, attended, logs, around, numbers):
    heads = HEADS // 2
    width = grads.shape[1]
    row = lax.broadcasted_iota(jnp.int32, (width, LANES), 0)
    lane = lax.broadcasted_iota(jnp.int32, (width, LANES), 1)
    low = grads[...].astype(BF)
    delta = jnp.dot(
        low.astype(F32) * attended[...],
        (row // HEAD_DIM == lane - 2 * heads).astype(F32),
        preferred_element_type=F32,
        precision=lax.Precision.HIGHEST,
    )
    both = logs[...] + delta
    numbers[...] = both
    high = both.astype(BF).astype(F32)
    around[:, :width] = low
    around[:, width:] = (high + pltpu.roll(both - high, heads, 1)).astype(BF)


def query_kernel(q0, k0, v0, q1, k1, v1, around, numbers, doc_row, doc_column, cosine, sine, d_q):
    turned, plain = lane_masks()
    allowed = doc_column[...] == doc_row[0]
    c, s = cosine[...] * SCALE, sine[...] * SCALE
    for group, (q, k, v) in enumerate(((q0, k0, v0), (q1, k1, v1))):
        queries, keys, values = q[...], k[...], v[...]
        grads = around[:, group * GROUP : (group + 1) * GROUP]
        kept = jnp.zeros(queries.shape, F32)
        for i in range(4):
            at = 4 * group + i
            raw = outer_rows(only(turned[i], queries), keys)
            weights = jnp.where(allowed, jnp.exp(raw - numbers[:, at : at + 1]), 0.0)
            d_weights = outer_rows(only(plain[i], grads), values)
            d_raw = (weights * (d_weights - numbers[:, 16 + at : 17 + at])).astype(BF)
            kept = jnp.where(turned[i], dot(d_raw, keys), kept)
        a, b = spin(kept, c, s, -1.0)
        d_q[:, group * GROUP : group * GROUP + LANES] = a.astype(BF)
        d_q[:, group * GROUP + LANES : (group + 1) * GROUP] = b.astype(BF)


def key_kernel(q0, k0, v0, q1, k1, v1, d_q, doc_row, doc_column, cosine, sine, *refs):
    *around, near, far = refs
    turned, plain = lane_masks()
    rows = k0.shape[0]
    c, s = cosine[...], sine[...]
    column = doc_column[...]
    kept = [[jnp.zeros(k0.shape, F32), jnp.zeros(k0.shape, F32)] for _ in (0, 1)]
    for j, block in enumerate(around):
        part = slice(j * rows, (j + 1) * rows)
        allowed = column == doc_row[0, :, part]
        numbers = block[:, 2 * GROUP :].astype(F32)
        numbers = (numbers + pltpu.roll(numbers, LANES - HEADS // 2, 1)).T
        for group, (q, k, v) in enumerate(((q0, k0, v0), (q1, k1, v1))):
            queries, keys, values = q[part, :], k[...], v[...]
            grads = block[:, group * GROUP : (group + 1) * GROUP]
            add_k = jnp.zeros(k0.shape, F32)
            add_v = jnp.zeros(k0.shape, F32)
            for i in range(4):
                at = 4 * group + i
                raw = outer_rows(only(turned[i], keys), queries)
                weights = jnp.where(allowed, jnp.exp(raw - numbers[at : at + 1, :]), 0.0)
                add_v = jnp.where(plain[i], dot(weights.astype(BF), grads), add_v)
                d_weights = outer_rows(only(plain[i], values), grads)
                d_raw = (weights * (d_weights - numbers[16 + at : 17 + at, :])).astype(BF)
                add_k = jnp.where(turned[i], dot(d_raw, queries), add_k)
            kept[group][0] += add_k
            kept[group][1] += add_v
    for group, out in enumerate((near, far)):
        a, b = spin(kept[group][0], c, s, -1.0)
        out[:, :GROUP] = d_q[:, group * GROUP : (group + 1) * GROUP]
        out[:, GROUP : GROUP + LANES] = a.astype(BF)
        out[:, GROUP + LANES : 2 * GROUP] = b.astype(BF)
        out[:, 2 * GROUP :] = kept[group][1].astype(BF)


def pack_kernel(place, active, grads, attended, branch, near, far):
    count, depth = near.shape[0], attended.shape[1] // near.shape[0]
    rows = active.shape[1] // count
    wide = near.shape[2]
    for i in (0, 1):
        one = inner_rows(active[...], grads[:, i * wide : (i + 1) * wide]).astype(BF)
        two = inner_rows(attended[...], branch[i]).astype(BF)

        def store(out):
            for s in range(count):
                out[s, :rows] = one[s * rows : (s + 1) * rows]
                at = s * depth
                out[s, rows:, :GROUP] = two[at : at + depth // 2]
                out[s, rows:, GROUP:] = two[at + depth // 2 : at + depth]

        @pl.when(place[0] == i)
        def _():
            store(near)

        @pl.when(place[0] != i)
        def _():
            store(far)


def place_kernel(rest, one_low, one_high, two_low, two_high, weight, gain, grads, gains):
    length, half, rows, pad = rest
    full = weight.shape[1] // 2
    for i, pair in enumerate(((one_low, two_low), (one_high, two_high))):
        for s in range(length):
            for c, share in enumerate(pair):
                size = min(half, rows - c * half)
                at = i * full + s * rows + c * half
                grads[:, at : at + size] = share[:, s * pad : s * pad + size].astype(F32)
    raw = grads[...]
    total = jnp.sum(raw * weight[...].astype(F32), axis=1, keepdims=True)
    gains[...] = jnp.broadcast_to(total, gains.shape)
    grads[...] = raw * gain[...]


def call_kernel(kernel, ins, outs, grid=1, room=32, micros=5):
    spec = lambda block, at: (
        pl.BlockSpec(memory_space=pltpu.SMEM) if block is None else pl.BlockSpec(block, at)
    )
    return pl.pallas_call(
        kernel,
        grid=(grid,),
        in_specs=[spec(block, at) for _, block, at in ins],
        out_specs=tuple(pl.BlockSpec(block, at) for _, _, block, at in outs),
        out_shape=tuple(jax.ShapeDtypeStruct(shape, kind) for shape, kind, _, _ in outs),
        compiler_params=pltpu.CompilerParams(vmem_limit_bytes=room * 2**20),
        cost_estimate=pl.CostEstimate(flops=micros * 10**9, bytes_accessed=1, transcendentals=0),
    )(*[a for a, _, _ in ins])


def gelu_parts(inner):
    share = 0.5 * (1.0 + lax.erf(inner * 0.7071067811865476))
    return inner * share, share + inner * (0.3989422804014327 * jnp.exp(-0.5 * inner * inner))


def hidden_kernel(marks, rows, grads, pair, other, shrink_pair, shrink_other, *refs):
    active, lifted_grads, out, out_there, d_rows, d_there = refs[:6]
    expand_w, shrink_w, semaphore = refs[6:]
    units = shrink_w.shape[0]
    half = pair.shape[0] // 2
    wide = shrink_pair.shape[1]
    places = marks.shape[0] - 2
    block = units // places
    front = marks[0] == 1
    x = marks[1]
    step = pl.program_id(0)

    def weights(source, start, at, row):
        return source.at[pl.ds(start, half)], expand_w.at[at, pl.ds(row, half)]

    def shrinks(source, high, at, low):
        found = []
        for j in range(places // 2):
            start = high * (source.shape[0] // 2) + j * block
            row = pl.multiple_of(marks[2 + low * (places // 2) + j], 16)
            column = pl.multiple_of(at * wide, LANES)
            found.append(
                (
                    source.at[pl.ds(start, block)],
                    shrink_w.at[pl.ds(row, block), pl.ds(column, wide)],
                )
            )
        return found

    def begin(moves, first):
        copies = [
            pltpu.make_async_copy(a, b, semaphore.at[first + k]) for k, (a, b) in enumerate(moves)
        ]
        for copy in copies:
            copy.start()
        return copies

    @pl.when(step == 0)
    def _():
        moves = [weights(pair, 0, x, 0), weights(other, half, 1 - x, half)]
        moves += shrinks(shrink_pair, 0, x, 0) + shrinks(shrink_other, 1, 1 - x, 1)
        copies = begin(moves, 0)
        for flag, low, high in ((front, other, pair), (jnp.logical_not(front), pair, other)):

            @pl.when(flag)
            def _():
                start = 0 if low is other else half
                back = half - start
                shrink_low = shrink_other if low is other else shrink_pair
                shrink_high = shrink_pair if low is other else shrink_other
                crossed = [weights(low, start, x, half), weights(high, back, 1 - x, 0)]
                crossed += shrinks(shrink_low, start // half, x, 1)
                crossed += shrinks(shrink_high, back // half, 1 - x, 0)
                for copy in begin(crossed, len(moves)):
                    copy.wait()

        for copy in copies:
            copy.wait()

    values, dy = rows[...], grads[...]
    tile = 256
    for at in range(0, units, tile):
        cut = slice(at, min(at + tile, units))
        inner = dot(values, expand_w[0, :, cut])
        gate = dot(values, expand_w[1, :, cut])
        d_active = outer_rows(dy, shrink_w[cut, :])
        value, slope = gelu_parts(inner)
        active[:, cut] = (value * gate).astype(BF)
        lifted_grads[x, :, cut] = (d_active * gate * slope).astype(BF)
        lifted_grads[1 - x, :, cut] = (d_active * value).astype(BF)
    result = dot(active[...], shrink_w[...])
    back = outer_rows(lifted_grads[x], expand_w[0]) + outer_rows(lifted_grads[1 - x], expand_w[1])

    @pl.when(step == 0)
    def _():
        out[...] = result
        d_rows[...] = back

    @pl.when(step == 1)
    def _():
        out_there[...] = result.astype(BF)
        d_there[...] = back.astype(BF)


def hidden(marks, rows, grads, expand, shrink):
    count, width = rows.shape
    units = expand[0].shape[1]
    size = count // 2
    moving = lambda i: (i, 0)
    still = lambda i: (0, 0)
    held = pl.BlockSpec(memory_space=pl.ANY)
    outs = [
        ((count, units), BF, (size, units), moving),
        ((2, count, units), BF, (2, size, units), lambda i: (0, i, 0)),
        ((size, width), F32, (size, width), still),
        ((size, width), BF, (size, width), still),
        ((size, width), F32, (size, width), still),
        ((size, width), BF, (size, width), still),
    ]
    return pl.pallas_call(
        hidden_kernel,
        grid=(2,),
        in_specs=[pl.BlockSpec(memory_space=pltpu.SMEM)]
        + [pl.BlockSpec((size, width), moving)] * 2
        + [held] * 4,
        out_specs=tuple(pl.BlockSpec(block, at) for _, _, block, at in outs),
        out_shape=tuple(jax.ShapeDtypeStruct(shape, kind) for shape, kind, _, _ in outs),
        scratch_shapes=[
            pltpu.VMEM((2, width, units), BF),
            pltpu.VMEM((units, width), BF),
            pltpu.SemaphoreType.DMA((2 * marks.shape[0],)),
        ],
        compiler_params=pltpu.CompilerParams(vmem_limit_bytes=36 * 2**20),
        cost_estimate=pl.CostEstimate(flops=8 * 10**9, bytes_accessed=1, transcendentals=0),
    )(marks, rows, grads, *expand, *shrink)


def on_device(
    direct,
    tokens,
    norm_first,
    joint_weight,
    output_weight,
    norm_second,
    expand_weight,
    shrink_weight,
    document_start,
    cotangent,
):
    rows, width = tokens.shape
    plan = Direct() if direct else Plain(rows)
    length = lax.axis_size("seq")
    here = lax.axis_index("seq")
    x, core = plan.x, plan.core
    near_x = x == 0
    depth = joint_weight.shape[0]
    unit_rows = shrink_weight.shape[0]
    unit_half = (unit_rows + 1) // 2
    units = -(-unit_half * length // LANES) * LANES
    while units % length:
        units += LANES
    unit_pad = units // length
    half_width = width // 2

    def mine(array, start):
        parts = [array[:, start + i * GROUP : start + (i + 1) * GROUP] for i in range(4)]
        low, high = pick(near_x, parts[0::2], parts[1::2])
        return jnp.where(core == 0, low, high)

    source = jnp.arange(GROUP)
    turn = (
        source[:, None]
        == ((source % LANES) // 32 * HEAD_DIM + source // LANES * 32 + source % 32)[None, :]
    ).astype(BF)
    gain_one = norm_first.astype(F32)[:, None]
    gain_two = norm_second.astype(F32)[:, None]
    joint_piece = jnp.concatenate(
        [
            (dot(mine(joint_weight, 0), turn) * gain_one).astype(BF),
            (dot(mine(joint_weight, width), turn) * gain_one).astype(BF),
            (mine(joint_weight, 2 * width).astype(F32) * gain_one).astype(BF),
            mine(output_weight, 0),
        ],
        axis=1,
    )
    slot = jnp.arange(units)
    inner = core * unit_half + slot % unit_pad
    fits = (slot % unit_pad < unit_half) & (inner < unit_rows)
    unit_of = jnp.where(fits, slot // unit_pad * unit_rows + inner, -2 * FF)
    spread_units = (jnp.arange(2 * FF)[:, None] == (unit_of + x * FF)[None, :]).astype(BF)
    expand_piece = (dot(expand_weight, spread_units) * gain_two).astype(BF)
    slot_row = jnp.arange(unit_pad)

    def picked(c):
        row = c * unit_half + slot_row
        row = jnp.where((slot_row < unit_half) & (row < unit_rows), row, -1)
        return (row[:, None] == jnp.arange(unit_rows)[None, :]).astype(BF)

    shrink_piece = dot(
        picked(core),
        jnp.where(near_x, shrink_weight[:, :half_width], shrink_weight[:, half_width:]),
    ).astype(BF)

    anchor = (lax.axis_index("rep") * length + here) * rows
    position = anchor + jnp.arange(rows, dtype=jnp.int32) - document_start
    marks = jnp.pad(
        jnp.stack([(position + 1) // 16, (position + 1) % 16], axis=1), ((0, 0), (0, LANES - 2))
    ).astype(BF)
    packed = jnp.concatenate([tokens, marks], axis=1)
    joint = Chain(plan, plan.gather(joint_piece, True))
    near_tokens = Chain(plan, plan.around(packed))
    joint.step(3)
    expand = Chain(plan, plan.gather(gate(expand_piece, *joint.operands), False))
    joint.step(2)
    blocks, offsets = near_tokens.end()
    expand.step(2)
    shrink = Chain(plan, plan.gather(gate(shrink_piece, *expand.operands), False))
    block_count = len(blocks)
    span = block_count * rows
    still = lambda i: (0, 0)
    moving = lambda i: (i, 0)
    (sent,) = call_kernel(
        prepare_kernel,
        [(plan.columns(width // depth), None, None)]
        + [(block, (rows, width + LANES), still) for block in blocks],
        [((span, width + LANES), BF, (span, width + LANES), still)],
        micros=2,
    )
    first = (sent, swap_core(sent))
    offset_rows = jnp.stack([jnp.int32(offset) for offset in offsets]) * rows
    index = (here * rows + offset_rows[:, None] + jnp.arange(rows)[None, :]).reshape(1, span)
    document_rows = []
    for rows_in in first:
        code = rows_in[:, width : width + 2].astype(F32).T
        code = code[:1] * 16.0 + code[1:]
        document_rows.append(jnp.where(code > 0, index.astype(F32) - (code - 1.0), FAR))
    document_row = jnp.stack(document_rows)
    document_column = jnp.concatenate([row[:, :rows] for row in document_rows], axis=1).T
    halves_of_head = HEAD_DIM // 2
    frequency = THETA ** (-(jnp.arange(halves_of_head, dtype=F32) * 2.0) / HEAD_DIM)
    frequency = jnp.tile(frequency, LANES // halves_of_head)[None, :]
    steps = jnp.arange(LANES, dtype=F32)[:, None]
    angle = jnp.concatenate([16.0 * steps * frequency, (steps - 1.0) * frequency], axis=0)
    tables = jnp.concatenate([jnp.cos(angle), jnp.sin(angle)], axis=1)

    joint_near, joint_far = halves(plan.front, *joint.value)
    output_mine = jnp.concatenate([joint_near[:, 3 * GROUP :], joint_far[:, 3 * GROUP :]], axis=1)
    output_all = jnp.concatenate([output_mine, swap_core(output_mine)], axis=1)

    def turn_columns(array):
        parts = [array[:, i * GROUP : (i + 1) * GROUP] for i in range(4)]
        parts = pick(core == 0, parts, parts[2:] + parts[:2])
        left, right = pick(near_x, parts[:2], parts[1::-1]), pick(near_x, parts[2:], parts[:1:-1])
        return jnp.concatenate(left + right, axis=-1)

    wide = 3 * GROUP
    *mixed, cosine, sine = call_kernel(
        mix_kernel,
        [
            (first[0], (rows, width + LANES), lambda i: (jnp.minimum(i, block_count - 1), 0)),
            (first[1], (rows, width + LANES), lambda i: (jnp.maximum(i - block_count, 0), 0)),
            (joint_near, (width, wide), still),
            (joint_far, (width, wide), still),
            (tables, (2 * LANES, 2 * LANES), still),
        ],
        [((2 * span, wide), BF, (rows, wide), moving)] * 2
        + [((2 * rows, LANES), F32, (rows, LANES), lambda i: (i // block_count, 0))] * 2,
        2 * block_count,
        micros=7,
    )
    expand.step()
    shrink.step(2)
    document_row = gate(document_row, *expand.operands)
    column = lambda kind, every: (
        ((span, GROUP), lambda i: (i, kind))
        if every
        else ((rows, GROUP), lambda i: (i * block_count, kind))
    )
    wide_keys = [
        (array, *column(kind, kind > 0)) for array in mixed for kind in range(3)
    ]
    wide_queries = [
        (array, *column(kind, kind == 0)) for array in mixed for kind in range(3)
    ]
    documents = [
        (document_row, (1, 1, span), lambda i: (i, 0, 0)),
        (document_column, (rows, 1), moving),
    ]
    both = lambda w, kind: ((2 * rows, w), kind, (rows, w), moving)
    attended, attended_low, logs = call_kernel(
        attend_kernel,
        wide_keys + documents,
        [both(2 * GROUP, F32), both(2 * GROUP, BF), both(LANES, F32)],
        2,
        micros=5,
    )
    shrink.step()
    shrink.step()
    expand_both = expand.end()
    attended_there = gate(swap_core(attended_low), *expand_both)
    attended_there = jnp.concatenate([attended_there[rows:], attended_there[:rows]], axis=0)
    attended_rows = plan.order(
        turn_columns(jnp.concatenate([attended_low, attended_there], axis=1)), depth
    )
    middle = tokens.astype(F32) + turn_columns(dot(attended_rows[:rows], output_all))
    second, second_scale = centre(middle)
    second_low = plan.order(second.astype(BF), depth)
    second_both = jnp.concatenate([second_low, swap_core(second_low)], axis=0)
    shrink_both = shrink.end()

    cotangents = jnp.concatenate([cotangent, swap_core(gate(cotangent, attended_low))], axis=0)

    where = jnp.stack(
        [plan.front.astype(jnp.int32), x.astype(jnp.int32)]
        + [row.astype(jnp.int32) for row in plan.rows_of(unit_pad)]
    )
    active_low, lifted_grads, out, out_there, second_grad, second_there = hidden(
        where, second_both, cotangents, expand_both, shrink_both
    )
    expand = Chain(plan, plan.reduce(second_both, lifted_grads[0], lifted_grads[1], False))
    result = middle + out + swap_core(out_there).astype(F32)
    second_grad = second_grad + swap_core(second_there).astype(F32)
    middle_grad = cotangent.astype(F32) + centre_back(
        second, second_scale, plan.restore(second_grad, depth)
    )
    branch = middle_grad.astype(BF)
    branch_both = turn_columns(jnp.concatenate([branch, swap_core(branch)], axis=0))
    attended_grad = turn_columns(plan.restore(outer_rows(branch_both, output_all), depth))
    around, numbers = call_kernel(
        around_kernel,
        [
            (attended_grad[:, : 2 * GROUP], (rows, 2 * GROUP), moving),
            (attended, (rows, 2 * GROUP), moving),
            (logs, (rows, LANES), moving),
        ],
        [both(2 * GROUP + LANES, BF), both(LANES, F32)],
        2,
    )
    near_grads = Chain(plan, plan.around(around))
    branch_sides = jnp.stack(
        pick(near_x, *[[branch_both[:, i * GROUP : (i + 1) * GROUP] for i in o] for o in ((0, 1), (1, 0))])
    )
    kinds = [
        ((length, unit_pad + depth // 2, half_width), BF),
        (length, unit_pad + depth // 2, half_width),
        lambda i: (0, 0, 0),
    ]
    sums = call_kernel(
        pack_kernel,
        [
            (x.astype(jnp.int32)[None], None, 0),
            (active_low, (2 * rows, units), still),
            (cotangents, (2 * rows, width), still),
            (plan.restore(attended_rows, depth), (2 * rows, width), still),
            (branch_sides, (2, 2 * rows, GROUP), lambda i: (0, 0, 0)),
        ],
        [(*kinds[0], kinds[1], kinds[2])] * 2,
    )
    near_grads.step(2)
    shrink = Chain(plan, plan.reduce_blocks(*sums))
    turning = [(cosine, (rows, LANES), moving), (sine, (rows, LANES), moving)]
    (query_grad,) = call_kernel(
        query_kernel,
        wide_keys
        + [
            (around, (rows, 2 * GROUP), moving),
            (numbers, (rows, LANES), moving),
        ]
        + documents
        + turning,
        [both(2 * GROUP, BF)],
        2,
        micros=13,
    )
    expand.step()
    arounds, _ = near_grads.end()
    mixed_grads = call_kernel(
        key_kernel,
        wide_queries
        + [(query_grad, (rows, 2 * GROUP), moving)]
        + documents
        + turning
        + [(block, (rows, 2 * GROUP + LANES), moving) for block in arounds],
        [both(wide, BF), both(wide, BF)],
        2,
        micros=16,
    )
    own_first = jnp.concatenate([rows_in[:rows, :width] for rows_in in first], axis=0)
    joint = Chain(plan, plan.reduce(own_first, *mixed_grads, True))
    expand.step()
    shrink.step()
    joint.step()
    moved = joint.operands + expand.operands
    expand.hold(*moved)
    shrink.hold(*moved)
    first_part = outer_rows(mixed_grads[0], joint_near[:, :wide]) + outer_rows(
        mixed_grads[1], joint_far[:, :wide]
    )
    first_grad = first_part[:rows] + swap_core(first_part[rows:].astype(BF)).astype(F32)
    normal, normal_scale = centre(tokens.astype(F32))
    tokens_grad = middle_grad + centre_back(
        normal, normal_scale, plan.restore(first_grad, depth)
    )

    expand.step()
    shrink.hold(*expand.operands)
    shrink.step()
    joint.step()
    waits = joint.operands
    expand.step()
    shrink.hold(*waits, *expand.operands)
    expand.step()
    joint.step(3)
    shrink.step()
    expand_shares = expand.end()
    share_parts = [share for pair in expand_shares for share in pair]
    expand_grad, second_gains = call_kernel(
        functools.partial(place_kernel, (length, unit_half, unit_rows, unit_pad)),
        [(part, (depth, units), still) for part in share_parts]
        + [(expand_weight, (depth, 2 * FF), still), (gain_two, (depth, 1), still)],
        [
            ((depth, 2 * FF), F32, (depth, 2 * FF), still),
            ((depth, LANES), F32, (depth, LANES), still),
        ],
        micros=3,
    )
    second_gain_grad = second_gains[:, 0]
    shrink.step()
    joint.step()
    joint.hold(expand_grad)
    shrink_shares = shrink.end()
    joint_four = joint.end()

    shrink_grad = jnp.concatenate(
        [
            inner_rows(picked(0), shrink_shares[0][i][:unit_pad])
            + inner_rows(picked(1), shrink_shares[1][i][:unit_pad])
            for i in (0, 1)
        ],
        axis=1,
    )
    output_grad = []
    for pair in shrink_shares:
        for share in pair:
            share = share[unit_pad:]
            output_grad.append(jnp.concatenate([share[:, :GROUP], share[:, GROUP:]], axis=0))
    output_grad = jnp.concatenate(output_grad, axis=1).astype(F32)
    columns = []
    for kind in range(3):
        for c in (0, 1):
            for i in (0, 1):
                piece = joint_four[c][i][:, kind * GROUP : (kind + 1) * GROUP]
                columns.append(outer_rows(piece, turn) if kind < 2 else piece.astype(F32))
    joint_raw = jnp.concatenate(columns, axis=1)
    joint_grad = joint_raw * gain_one
    first_gain_grad = jnp.sum(joint_raw * joint_weight.astype(F32), axis=1)
    return (
        result.astype(BF),
        tokens_grad.astype(BF),
        first_gain_grad,
        joint_grad,
        output_grad,
        second_gain_grad,
        expand_grad,
        shrink_grad,
    )


def solution(mesh):
    placed = (
        P(("rep", "seq"), None),
        P("seq"),
        P("seq", None),
        P("seq", None),
        P("seq"),
        P("seq", None),
        P("seq", None),
        P(("rep", "seq")),
        P(("rep", "seq"), None),
    )
    return jax.shard_map(
        functools.partial(on_device, mesh.shape["seq"] == 8),
        mesh=mesh,
        in_specs=placed,
        out_specs=(
            P(("rep", "seq"), None),
            P(("rep", "seq"), None),
            P("seq"),
            P("seq", None),
            P("seq", None),
            P("seq"),
            P("seq", None),
            P("seq", None),
        ),
        check_vma=False,
    )
```
